32 devices in a mesh: wide: 16 (over z, y, core), narrow: 2 (over x).
Axes of the slice: x: 2, y: 2, z: 4, core: 2. Of those that a mesh axis runs over, the one named last changes fastest.
Arguments:
- tokens: bfloat16 [32, 1024, 768], P(('wide', 'narrow')), may hold values from -6 to 6
- doc_ids: int32 [32, 1024], P(('wide', 'narrow')), may hold values from 0 to 5, never falling along the last dimension, each value on 1 to 512 neighbouring positions
- cotangent: bfloat16 [32, 1024, 768], P(('wide', 'narrow')), may hold values from -6 to 6
- owner: int32 [1], replicated, may hold values from 0 to 15
- ln1_gain: bfloat16 [16, 768], P('wide', 'narrow'), may hold values from 0.25 to 1.75
- ln1_bias: bfloat16 [16, 768], P('wide', 'narrow'), may hold values from -2 to 2
- qkv_weight: bfloat16 [16, 768, 2304], P('wide', 'narrow'), may hold values from -0.21875 to 0.21875
- qv_bias: bfloat16 [16, 1536], P('wide', 'narrow'), may hold values from -2 to 2
- out_weight: bfloat16 [16, 768, 768], P('wide', 'narrow'), may hold values from -1.75 to 1.75
- out_bias: bfloat16 [16, 768], P('wide', 'narrow'), may hold values from -2 to 2
- ln2_gain: bfloat16 [16, 768], P('wide', 'narrow'), may hold values from 0.25 to 1.75
- ln2_bias: bfloat16 [16, 768], P('wide', 'narrow'), may hold values from -2 to 2
- fc_weight: bfloat16 [16, 768, 3072], P('wide', 'narrow'), may hold values from -0.21875 to 0.21875
- fc_bias: bfloat16 [16, 3072], P('wide', 'narrow'), may hold values from -3 to 3
- proj_weight: bfloat16 [16, 3072, 768], P('wide', 'narrow'), may hold values from -0.109375 to 0.109375
- proj_bias: bfloat16 [16, 768], P('wide', 'narrow'), may hold values from -2 to 2
Outputs:
- block_out: bfloat16 [32, 1024, 768], P(('wide', 'narrow'))
- tokens_grad: bfloat16 [32, 1024, 768], P(('wide', 'narrow'))
- ln1_gain_grad: float32 [16, 768], P('wide', 'narrow')
- ln1_bias_grad: float32 [16, 768], P('wide', 'narrow')
- qkv_weight_grad: float32 [16, 768, 2304], P('wide', 'narrow')
- qv_bias_grad: float32 [16, 1536], P('wide', 'narrow')
- out_weight_grad: float32 [16, 768, 768], P('wide', 'narrow')
- out_bias_grad: float32 [16, 768], P('wide', 'narrow')
- ln2_gain_grad: float32 [16, 768], P('wide', 'narrow')
- ln2_bias_grad: float32 [16, 768], P('wide', 'narrow')
- fc_weight_grad: float32 [16, 768, 3072], P('wide', 'narrow')
- fc_bias_grad: float32 [16, 3072], P('wide', 'narrow')
- proj_weight_grad: float32 [16, 3072, 768], P('wide', 'narrow')
- proj_bias_grad: float32 [16, 768], P('wide', 'narrow')
The draws below stay inside these ranges and needn't reach their ends.
Inputs may be any that keep to these rules, and one draw needn't show every extreme that they name: `owner`: the slot that holds the source layer. `doc_ids`: along each row the numbers never fall; equal numbers mark one document.
All inputs are finite; a program needn't handle non-finite values.
Results may differ from the reference program's by a relative error of at most 0.019.
Values may be sent and summed in bfloat16 or wider, within the bound.
No kernel may reach another device: no remote copies, remote signals or barrier semaphores. Data moves between devices by JAX's collectives and lax.ppermute only.
A program may use at most 192 MiB of HBM per device.

```python
import functools
import math
import jax
import jax.numpy as jnp
import numpy as np
from jax import lax

D = 768
H = 12
HD = 64
FF = 3072
SEQ = 1024
ROWS = 32
SLOTS = 16
N_WIDE = 16


def block_levels(stream_key, dims, cuts, low, top_value):
    factor_of, own = 1.0, jax.random.fold_in(stream_key, 6)
    for axis_at, blocks in cuts:
        heights = jnp.exp(jax.random.uniform(jax.random.fold_in(own, axis_at), (blocks,), jnp.float32, low / len(cuts), top_value / len(cuts)))
        factor_of = factor_of * jnp.repeat(heights, dims[axis_at] // blocks).reshape([-1 if axis == axis_at else 1 for axis in range(len(dims))])
    return factor_of


def length_profile(count, total, reach, skew):
    portions = [(1 << 20) // math.isqrt(grade ** skew) + 1 for grade in range(2, count + 1)]
    spare, holding = total - reach - (count - 1), [1] * (count - 1)
    while spare > 0:
        movable = [i for i in range(count - 1) if holding[i] < reach]
        whole, budget = sum([portions[i] for i in movable]), spare
        for i in movable:
            more = min(reach - holding[i], max(1, budget * portions[i] // whole), spare)
            holding[i] = holding[i] + more
            spare = spare - more
    return np.array([reach] + holding)


def uneven(key, count, total, limit, lean):
    if count == 2:
        one = jax.random.randint(key, (), max(1, total - limit), min(limit, total - 1) + 1)
        return jnp.stack([one, total - one])
    sizes = jnp.asarray(length_profile(count, total, limit, lean), jnp.int32)
    twos = (count - 1) // 2
    giver, receiver = sizes[1:1 + 2 * twos:2], sizes[2:2 + 2 * twos:2]
    slack = jnp.minimum(giver - 1, limit - receiver)
    passed = jax.random.randint(jax.random.fold_in(key, 1), (twos,), 0, 1 << 20) % (slack + 1)
    sizes = sizes.at[1:1 + 2 * twos:2].set(giver - passed).at[2:2 + 2 * twos:2].set(receiver + passed)
    return sizes[jax.random.permutation(jax.random.fold_in(key, 2), count)]


def normal_values(key, shape, width, most, shards=(), held_as=jnp.bfloat16):
    values = jax.random.normal(key, shape, jnp.float32) * width
    if len(shards) > 0:
        values = block_levels(key, shape, shards, -0.22, 0.18) * values
    return jnp.clip(values, min=-most, max=most).astype(held_as)


def setup_inputs(seed: int = 0) -> dict:
    streams_of = jax.random.split(jax.random.key(seed), 17)
    tokens = normal_values(streams_of[0], (ROWS, SEQ, D), 1.0, 6.0, ((0, 32),))
    doc_ids = jax.vmap(lambda own: jnp.searchsorted(jnp.cumsum(uneven(own, 6, SEQ, SEQ // 2, 0)), jnp.arange(SEQ), side="right"))(jax.random.split(streams_of[1], ROWS)).reshape((ROWS, SEQ)).astype(jnp.int32)
    cotangent = normal_values(streams_of[2], (ROWS, SEQ, D), 1.0, 6.0, ((0, 32),))
    owner = jax.random.randint(streams_of[3], (1,), 0, N_WIDE).astype(jnp.int32)
    ln1_gain = jnp.clip(1.0 + 0.15 * jax.random.normal(streams_of[4], (SLOTS, D), jnp.float32), 0.25, 1.75).astype(jnp.bfloat16)
    ln1_bias = normal_values(streams_of[5], (SLOTS, D), 0.3, 2.0, ((0, 16), (1, 2)))
    qkv_weight = normal_values(streams_of[6], (SLOTS, D, 3 * D), D ** -0.5, 0.21875, ((0, 16), (1, 2)))
    qv_bias = normal_values(streams_of[7], (SLOTS, 2 * D), 0.3, 2.0, ((0, 16), (1, 2)))
    out_weight = normal_values(streams_of[8], (SLOTS, D, D), (max(D // 64, 4)) ** -0.5, 1.75, ((0, 16), (1, 2)))
    out_bias = normal_values(streams_of[9], (SLOTS, D), 0.3, 2.0, ((0, 16), (1, 2)))
    ln2_gain = jnp.clip(1.0 + 0.15 * jax.random.normal(streams_of[10], (SLOTS, D), jnp.float32), 0.25, 1.75).astype(jnp.bfloat16)
    ln2_bias = normal_values(streams_of[11], (SLOTS, D), 0.3, 2.0, ((0, 16), (1, 2)))
    fc_weight = normal_values(streams_of[12], (SLOTS, D, FF), D ** -0.5, 0.21875, ((0, 16), (1, 2)))
    fc_bias = normal_values(streams_of[13], (SLOTS, FF), 0.5, 3.0, ((0, 16), (1, 2)))
    proj_weight = normal_values(streams_of[14], (SLOTS, FF, D), FF ** -0.5, 0.109375, ((0, 16), (1, 2)))
    proj_bias = normal_values(streams_of[15], (SLOTS, D), 0.3, 2.0, ((0, 16), (1, 2)))
    return {"tokens": tokens, "doc_ids": doc_ids, "cotangent": cotangent, "owner": owner, "ln1_gain": ln1_gain, "ln1_bias": ln1_bias, "qkv_weight": qkv_weight, "qv_bias": qv_bias, "out_weight": out_weight, "out_bias": out_bias, "ln2_gain": ln2_gain, "ln2_bias": ln2_bias, "fc_weight": fc_weight, "fc_bias": fc_bias, "proj_weight": proj_weight, "proj_bias": proj_bias}


@jax.custom_vjp
def low(v):
    return lax.optimization_barrier(v.astype(jnp.bfloat16)).astype(jnp.float32)

@jax.custom_vjp
def low_back(v):
    return v

def low_keep(v):
    return (low(v), None)

def low_pass(kept, grad):
    return (grad,)

def back_keep(v):
    return (v, None)

def back_low(kept, grad):
    return (low(grad),)
low.defvjp(low_keep, low_pass)
low_back.defvjp(back_keep, back_low)
epsilon = 1e-05
highest = lax.Precision.HIGHEST

def norm_rows(values, gain, shift):
    center = values - lax.optimization_barrier(jnp.mean(values, axis=-1, keepdims=True))
    spread = lax.optimization_barrier(jnp.mean(center * center, axis=-1, keepdims=True))
    return center * lax.rsqrt(spread + epsilon) * gain + shift

def gelu_tanh(values):
    inner = math.sqrt(2.0 / math.pi) * (values + 0.044715 * values * values * values)
    return 0.5 * values * (1.0 + jnp.tanh(inner))

def project(left, right):
    return jnp.einsum('rsd,de->rse', left, right, precision=highest)

def attend_head(pieces, allowed):
    queries, keys, values = pieces
    scores = low_back(jnp.dot(queries, keys.T, precision=highest) * HD ** (-0.5))
    scores = jnp.where(allowed, scores, -1000000000.0)
    row_max = lax.optimization_barrier(jnp.max(scores, axis=-1, keepdims=True))
    expon = jnp.exp(scores - row_max)
    soft = expon / lax.optimization_barrier(jnp.sum(expon, axis=-1, keepdims=True))
    return jnp.dot(low(soft), values, precision=highest)

def attend_row(pieces):
    packed, doc_row = pieces
    places = jnp.arange(SEQ)
    allowed = (places[:, None] >= places[None, :]) & (doc_row[:, None] == doc_row[None, :])
    heads = packed.reshape(SEQ, 3, H, HD).transpose(1, 2, 0, 3)
    mixed = lax.map(jax.checkpoint(functools.partial(attend_head, allowed=allowed)), (heads[0], heads[1], heads[2]))
    return mixed.transpose(1, 0, 2).reshape(SEQ, D)

def layer(inputs, doc_rows, ln1_gain, ln1_bias, qkv_weight, qv_bias, out_weight, out_bias, ln2_gain, ln2_bias, fc_weight, fc_bias, proj_weight, proj_bias):
    normed = low(norm_rows(inputs, ln1_gain, ln1_bias))
    full_bias = jnp.concatenate([qv_bias[:D], jnp.zeros((D,), jnp.float32), qv_bias[D:]])
    packed = low(low_back(project(normed, qkv_weight) + full_bias))
    mixed = lax.map(attend_row, (packed, doc_rows))
    mixed = low(low_back(mixed))
    middle = inputs + low_back(project(mixed, out_weight) + out_bias)
    second = low(norm_rows(middle, ln2_gain, ln2_bias))
    hidden = low_back(project(second, fc_weight) + fc_bias)
    active = low(gelu_tanh(hidden))
    return middle + low_back(project(active, proj_weight) + proj_bias)

def reference(tokens, doc_ids, cotangent, owner, ln1_gain, ln1_bias, qkv_weight, qv_bias, out_weight, out_bias, ln2_gain, ln2_bias, fc_weight, fc_bias, proj_weight, proj_bias):
    source = owner[0]
    stacked = (ln1_gain, ln1_bias, qkv_weight, qv_bias, out_weight, out_bias, ln2_gain, ln2_bias, fc_weight, fc_bias, proj_weight, proj_bias)
    params = tuple((member[source].astype(jnp.float32) for member in stacked))
    group = math.gcd(ROWS, 4)
    inputs = tokens.reshape(ROWS // group, group, SEQ, D)
    doc_groups = doc_ids.reshape(ROWS // group, group, SEQ)
    cot_groups = cotangent.reshape(ROWS // group, group, SEQ, D)

    def step(totals, item):
        block_in, doc_rows, cot_rows = item

        def forward(values, *weights):
            return layer(values, doc_rows, *weights)
        result, pull = jax.vjp(forward, block_in.astype(jnp.float32), *params)
        grads = pull(cot_rows.astype(jnp.float32))
        totals = tuple((total + grad for total, grad in zip(totals, grads[1:])))
        return (totals, (result.astype(jnp.bfloat16), grads[0].astype(jnp.bfloat16)))
    start = tuple((jnp.zeros(member.shape, jnp.float32) for member in params))
    totals, (outputs, input_grads) = lax.scan(step, start, (inputs, doc_groups, cot_groups))
    placed = tuple((jnp.zeros((N_WIDE,) + total.shape, jnp.float32).at[source].set(total) for total in totals))
    return (outputs.reshape(ROWS, SEQ, D), input_grads.reshape(ROWS, SEQ, D), placed[0], placed[1], placed[2], placed[3], placed[4], placed[5], placed[6], placed[7], placed[8], placed[9], placed[10], placed[11])
```

```python
import functools
import math

import jax
import jax.numpy as jnp
from jax import lax
from jax.experimental import pallas as pl
from jax.experimental.pallas import tpu as pltpu
from jax.sharding import PartitionSpec as P

H = 12
HD = 64
QB = 256
REACH = 512

epsilon = 1e-05
AXES = ("wide", "narrow")
VMEM = 56 * 1024 * 1024
f32 = jnp.float32
bf16 = jnp.bfloat16


def spans(length):
    out = []
    for b in range(length // QB):
        low = max(0, (b * QB - (REACH - 1)) // QB * QB)
        out.append((low, (b + 1) * QB))
    return out


def attend_kernel(doc_ref, q_ref, k_ref, v_ref, o_ref, p_ref, *, length):
    lane = lax.broadcasted_iota(jnp.int32, (length, 128), 1)
    low = lane < HD
    hot = (lane & (HD - 1)) == doc_ref[...]
    q_side = jnp.where(hot, 1.0, 0.0)
    k_side = jnp.where(hot, 0.0, -1e9)
    q = q_ref[...].astype(f32) * HD ** (-0.5)
    k = k_ref[...].astype(f32)
    v_t = v_ref[...].T
    sides = []
    for h in range(2):
        mine = low if h == 0 else jnp.logical_not(low)
        sides.append(
            (jnp.where(mine, q, q_side).astype(bf16), jnp.where(mine, k, k_side).astype(bf16))
        )
    rows = lax.broadcasted_iota(jnp.int32, (QB, QB), 0)
    tri = rows <= lax.broadcasted_iota(jnp.int32, (QB, QB), 1)
    at = 0
    for b, (lo, hi) in enumerate(spans(length)):
        n = hi - lo
        outs = []
        for h in range(2):
            qa, ka = sides[h]
            s = lax.dot_general(
                ka[lo:hi],
                qa[b * QB : (b + 1) * QB],
                (((1,), (1,)), ((), ())),
                preferred_element_type=f32,
            )
            last = jnp.where(tri, s[n - QB :], -1e9)
            s = last if n == QB else jnp.concatenate([s[: n - QB], last], axis=0)
            e = jnp.exp(s - jnp.max(s, axis=0, keepdims=True))
            p = (e * (1.0 / jnp.sum(e, axis=0, keepdims=True))).astype(bf16)
            p_ref[h, at : at + n, :] = p
            outs.append(
                jnp.dot(v_t[h * HD : (h + 1) * HD, lo:hi], p, preferred_element_type=f32)
            )
        o_ref[b * QB : (b + 1) * QB, :] = jnp.concatenate(outs, axis=0).T.astype(bf16)
        at += n


def attend(qkv, doc):
    length = qkv.shape[0]
    pairs = H // 2
    rows = sum(hi - lo for lo, hi in spans(length))
    col = lambda off: pl.BlockSpec((length, 128), lambda i: (0, off + i))
    return pl.pallas_call(
        functools.partial(attend_kernel, length=length),
        grid=(pairs,),
        in_specs=[
            pl.BlockSpec((length, 1), lambda i: (0, 0)),
            col(0),
            col(pairs),
            col(2 * pairs),
        ],
        out_specs=[col(0), pl.BlockSpec((2, rows, QB), lambda i: (i, 0, 0))],
        out_shape=[
            jax.ShapeDtypeStruct((length, pairs * 128), bf16),
            jax.ShapeDtypeStruct((2 * pairs, rows, QB), bf16),
        ],
        compiler_params=pltpu.CompilerParams(vmem_limit_bytes=VMEM),
        name="attend",
    )(doc, qkv, qkv, qkv)


def attend_back_kernel(
    q_ref, k_ref, v_ref, o_ref, do_ref, p_ref, dq_ref, dk_ref, dv_ref, dk_acc, dv_acc, *, length
):
    lane = lax.broadcasted_iota(jnp.int32, (length, 128), 1)
    low = lane < HD
    spot = lane & (HD - 1)
    q = q_ref[...].astype(f32) * HD ** (-0.5)
    do = do_ref[...].astype(f32)
    v = v_ref[...].astype(f32)
    product = do * o_ref[...].astype(f32)
    k_t = k_ref[...].T
    sides = []
    for h in range(2):
        mine = low if h == 0 else jnp.logical_not(low)
        center = jnp.sum(jnp.where(mine, product, 0.0), axis=1, keepdims=True)
        first = center.astype(bf16).astype(f32)
        second = (center - first).astype(bf16).astype(f32)
        third = center - first - second
        extra = jnp.where(
            spot == 0, -first, jnp.where(spot == 1, -second, jnp.where(spot == 2, -third, 0.0))
        )
        sides.append(
            (
                jnp.where(mine, do, extra).astype(bf16),
                jnp.where(mine, v, jnp.where(spot < 3, 1.0, 0.0)).astype(bf16),
                jnp.where(mine, do, 0.0).astype(bf16),
                jnp.where(mine, q, 0.0).astype(bf16),
            )
        )
    dk_acc[...] = jnp.zeros_like(dk_acc)
    dv_acc[...] = jnp.zeros_like(dv_acc)
    at = 0
    for b, (lo, hi) in enumerate(spans(length)):
        n = hi - lo
        here = slice(b * QB, (b + 1) * QB)
        dqs = []
        dk = dv = None
        for h in range(2):
            do_more, v_more, do_own, q_own = sides[h]
            p = p_ref[h, at : at + n, :]
            dp = lax.dot_general(
                v_more[lo:hi],
                do_more[here],
                (((1,), (1,)), ((), ())),
                preferred_element_type=f32,
            )
            ds = (p.astype(f32) * dp).astype(bf16)
            dv_part = jnp.dot(p, do_own[here], preferred_element_type=f32)
            dk_part = jnp.dot(ds, q_own[here], preferred_element_type=f32)
            dv = dv_part if dv is None else dv + dv_part
            dk = dk_part if dk is None else dk + dk_part
            dqs.append(
                jnp.dot(k_t[h * HD : (h + 1) * HD, lo:hi], ds, preferred_element_type=f32)
            )
        dv_acc[lo:hi, :] += dv
        dk_acc[lo:hi, :] += dk
        dq_ref[here, :] = (jnp.concatenate(dqs, axis=0) * HD ** (-0.5)).T.astype(bf16)
        at += n
    dk_ref[...] = dk_acc[...].astype(bf16)
    dv_ref[...] = dv_acc[...].astype(bf16)


def attend_back(qkv, mixed, grad_mixed, soft):
    length = qkv.shape[0]
    pairs = H // 2
    rows = soft.shape[1]
    col = lambda off: pl.BlockSpec((length, 128), lambda i: (0, off + i))
    out = jax.ShapeDtypeStruct((length, pairs * 128), bf16)
    return pl.pallas_call(
        functools.partial(attend_back_kernel, length=length),
        grid=(pairs,),
        in_specs=[
            col(0),
            col(pairs),
            col(2 * pairs),
            col(0),
            col(0),
            pl.BlockSpec((2, rows, QB), lambda i: (i, 0, 0)),
        ],
        out_specs=[col(0)] * 3,
        out_shape=[out] * 3,
        scratch_shapes=[pltpu.VMEM((length, 128), f32)] * 2,
        compiler_params=pltpu.CompilerParams(vmem_limit_bytes=VMEM),
        name="attend_back",
    )(qkv, qkv, qkv, mixed, grad_mixed, soft)


class Place:
    def __init__(self, owner, wide, narrow):
        self.wide, self.narrow = wide, narrow
        self.deep = wide // 4
        mine = lax.axis_index("wide")
        self.core, self.y, self.z = mine & 1, (mine >> 1) & 1, mine >> 2
        self.o_core, self.o_y, self.o_z = owner & 1, (owner >> 1) & 1, owner >> 2
        self.x = lax.axis_index("narrow")
        self.holder = mine == owner

    def swap(self, value, flip):
        return lax.ppermute(value, "wide", [(i, i ^ flip) for i in range(self.wide)])

    def z_flips(self):
        step = self.deep // 2
        while step:
            yield step
            step //= 2


def pick(parts, index):
    return lax.dynamic_index_in_dim(parts, index, axis=0, keepdims=False)


def ordered(mine, other, index):
    first = index == 0
    return jnp.stack([jnp.where(first, mine, other), jnp.where(first, other, mine)])


def spread(place, shard):
    rows, width = shard.shape
    cut = rows % 64 == 0
    now = shard
    if cut:
        halves = shard.reshape(2, rows // 2, width)
        other = place.swap(pick(halves, 1 - place.core), 1)
        now = jnp.where(place.core == place.o_core, pick(halves, place.core), other)
        halves = now.reshape(2, rows // 4, width)
        other = place.swap(pick(halves, 1 - place.y), 2)
        now = jnp.where(place.y == place.o_y, pick(halves, place.y), other)
    else:
        now = jnp.where(place.core == place.o_core, now, place.swap(now, 1))
        now = jnp.where(place.y == place.o_y, now, place.swap(now, 2))
    for step in place.z_flips():
        other = place.swap(now, 4 * step)
        now = jnp.where((place.z & step) == (place.o_z & step), now, other)
    if cut:
        now = ordered(now, place.swap(now, 2), place.y)
        if place.narrow == 2:
            other = lax.ppermute(now, "narrow", [(0, 1), (1, 0)])
            now = ordered(now, other, place.x)
        else:
            now = lax.all_gather(now, "narrow", axis=0)
        other = place.swap(now, 1)
        first = place.core == 0
        now = jnp.stack([jnp.where(first, now, other), jnp.where(first, other, now)], axis=1)
        return now.reshape(place.narrow * rows, width)
    return lax.all_gather(now, "narrow", axis=0, tiled=True)


def collect(place, terms):
    total, width = terms.shape
    rows = total // place.narrow
    cut = rows % 64 == 0
    now = terms.astype(bf16)
    add = lambda a, b: (a.astype(f32) + b.astype(f32)).astype(bf16)
    if cut:
        now = now.reshape(place.narrow, 2, rows // 2, width)
        take = lambda i: lax.dynamic_index_in_dim(now, i, axis=1, keepdims=False)
        other = place.swap(take(1 - place.core), 1)
        now = add(take(place.core), other)
        if place.narrow == 2:
            other = lax.ppermute(pick(now, 1 - place.x), "narrow", [(0, 1), (1, 0)])
            now = add(pick(now, place.x), other)
        else:
            now = lax.psum_scatter(now, "narrow", scatter_dimension=0, tiled=False)
        now = now.reshape(2, rows // 4, width)
        other = place.swap(pick(now, 1 - place.y), 2)
        now = add(pick(now, place.y), other)
        for step in place.z_flips():
            now = add(now, place.swap(now, 4 * step))
        now = ordered(now, place.swap(now, 2), place.y)
        now = ordered(now, place.swap(now, 1), place.core)
        return now.reshape(rows, width)
    now = lax.psum_scatter(now, "narrow", scatter_dimension=0, tiled=True)
    return lax.psum(now, "wide")


VECTORS = (
    "ln1_gain",
    "ln1_bias",
    "qv_bias",
    "out_bias",
    "ln2_gain",
    "ln2_bias",
    "fc_bias",
    "proj_bias",
)


def spread_vectors(place, vectors):
    sizes = [v.shape[-1] for v in vectors]
    now = jnp.concatenate([v.reshape(-1) for v in vectors]).reshape(-1, 128)
    now = jnp.where(place.core == place.o_core, now, place.swap(now, 1))
    now = jnp.where(place.y == place.o_y, now, place.swap(now, 2))
    for step in place.z_flips():
        now = jnp.where((place.z & step) == (place.o_z & step), now, place.swap(now, 4 * step))
    if place.narrow == 2:
        now = ordered(now, lax.ppermute(now, "narrow", [(0, 1), (1, 0)]), place.x)
    else:
        now = lax.all_gather(now, "narrow", axis=0)
    now = now.reshape(place.narrow, -1).astype(f32)
    out, at = [], 0
    for size in sizes:
        out.append(now[:, at : at + size].reshape(-1))
        at += size
    return out


def collect_vectors(place, vectors):
    sizes = [v.shape[0] // place.narrow for v in vectors]
    now = jnp.concatenate([v.reshape(place.narrow, -1) for v in vectors], axis=1)
    now = now.reshape(place.narrow, -1, 128)
    now = now + place.swap(now, 1)
    if place.narrow == 2:
        now = pick(now, place.x) + lax.ppermute(
            pick(now, 1 - place.x), "narrow", [(0, 1), (1, 0)]
        )
    else:
        now = lax.psum_scatter(now, "narrow", scatter_dimension=0, tiled=False)
    now = now + place.swap(now, 2)
    for step in place.z_flips():
        now = now + place.swap(now, 4 * step)
    now = now.reshape(-1)
    out, at = [], 0
    for size in sizes:
        out.append(now[at : at + size])
        at += size
    return out


def norm_rows(values, gain, shift):
    center = values - jnp.mean(values, axis=-1, keepdims=True)
    spread_of = jnp.mean(center * center, axis=-1, keepdims=True)
    return center * lax.rsqrt(spread_of + epsilon) * gain + shift


def norm_back(values, gain, grad):
    center = values - jnp.mean(values, axis=-1, keepdims=True)
    inverse = lax.rsqrt(jnp.mean(center * center, axis=-1, keepdims=True) + epsilon)
    hat = center * inverse
    scaled = grad * gain
    inner = jnp.mean(scaled * hat, axis=-1, keepdims=True)
    back = inverse * (scaled - jnp.mean(scaled, axis=-1, keepdims=True) - hat * inner)
    return back, jnp.sum(grad * hat, axis=0), jnp.sum(grad, axis=0)


def gelu_both(u):
    c = math.sqrt(2.0 / math.pi)
    t = jnp.tanh(c * (u + 0.044715 * u * u * u))
    slope = 0.5 * (1.0 + t) + 0.5 * u * (1.0 - t * t) * c * (1.0 + 3 * 0.044715 * u * u)
    return 0.5 * u * (1.0 + t), slope


def dot(a, b, dims=((1,), (0,))):
    return lax.dot_general(a, b, (dims, ((), ())), preferred_element_type=f32)


def on_device(
    wide,
    narrow,
    tokens,
    doc_ids,
    cotangent,
    owner,
    ln1_gain,
    ln1_bias,
    qkv_weight,
    qv_bias,
    out_weight,
    out_bias,
    ln2_gain,
    ln2_bias,
    fc_weight,
    fc_bias,
    proj_weight,
    proj_bias,
):
    _, length, width = tokens.shape
    place = Place(owner[0], wide, narrow)
    x = tokens[0].astype(f32)
    dout = cotangent[0]

    gain1, shift1, qv, outb, gain2, shift2, fcb, projb = spread_vectors(
        place, (ln1_gain, ln1_bias, qv_bias, out_bias, ln2_gain, ln2_bias, fc_bias, proj_bias)
    )
    w_qkv = spread(place, qkv_weight[0])
    w_out = spread(place, out_weight[0])
    w_fc = spread(place, fc_weight[0])
    w_proj = spread(place, proj_weight[0])

    h1 = norm_rows(x, gain1, shift1).astype(bf16)
    bias = jnp.concatenate([qv[:width], jnp.zeros((width,), f32), qv[width:]])
    qkv = (dot(h1, w_qkv) + bias).astype(bf16)
    mixed, soft = attend(qkv, doc_ids[0][:, None])
    y1 = x + dot(mixed, w_out) + outb
    h2 = norm_rows(y1, gain2, shift2).astype(bf16)
    g, slope = gelu_both(dot(h2, w_fc) + fcb)
    g, slope = g.astype(bf16), slope.astype(bf16)
    block_out = (y1 + dot(g, w_proj) + projb).astype(bf16)

    d_proj = dot(g, dout, ((0,), (0,)))
    d_projb = jnp.sum(dout.astype(f32), axis=0)
    du = (dot(dout, w_proj, ((1,), (1,))) * slope.astype(f32)).astype(bf16)
    d_fc = dot(h2, du, ((0,), (0,)))
    d_fcb = jnp.sum(du.astype(f32), axis=0)
    dh2 = dot(du, w_fc, ((1,), (1,)))
    back, d_gain2, d_shift2 = norm_back(y1, gain2, dh2)
    dy1 = dout.astype(f32) + back
    db1 = dy1.astype(bf16)
    d_out = dot(mixed, db1, ((0,), (0,)))
    d_outb = jnp.sum(db1.astype(f32), axis=0)
    dmixed = dot(db1, w_out, ((1,), (1,))).astype(bf16)
    dqkv = jnp.concatenate(attend_back(qkv, mixed, dmixed, soft), axis=1)
    d_qkv = dot(h1, dqkv, ((0,), (0,)))
    sums = jnp.sum(dqkv.astype(f32), axis=0)
    d_qv = jnp.concatenate([sums[:width], sums[2 * width :]])
    dh1 = dot(dqkv, w_qkv, ((1,), (1,)))
    back, d_gain1, d_shift1 = norm_back(x, gain1, dh1)
    tokens_grad = (dy1 + back).astype(bf16)

    grads = [collect(place, g) for g in (d_proj, d_fc, d_out, d_qkv)]
    small = collect_vectors(
        place, (d_gain1, d_shift1, d_qv, d_outb, d_gain2, d_shift2, d_fcb, d_projb)
    )
    put = lambda v: jnp.where(place.holder, v.astype(f32), 0.0)[None]
    s_proj, s_fc, s_out, s_qkv = [put(v) for v in grads]
    s_gain1, s_shift1, s_qv, s_outb, s_gain2, s_shift2, s_fcb, s_projb = [put(v) for v in small]
    return (
        block_out[None],
        tokens_grad[None],
        s_gain1,
        s_shift1,
        s_qkv,
        s_qv,
        s_out,
        s_outb,
        s_gain2,
        s_shift2,
        s_fc,
        s_fcb,
        s_proj,
        s_projb,
    )


def solution(mesh):
    rows = P(AXES, None, None)
    flat, deep = P("wide", "narrow"), P("wide", "narrow", None)
    in_specs = (
        rows,
        P(AXES, None),
        rows,
        P(),
        flat,
        flat,
        deep,
        flat,
        deep,
        flat,
        flat,
        flat,
        deep,
        flat,
        deep,
        flat,
    )
    out_specs = (
        rows,
        rows,
        flat,
        flat,
        deep,
        flat,
        deep,
        flat,
        flat,
        flat,
        deep,
        flat,
        deep,
        flat,
    )
    body = functools.partial(on_device, mesh.shape["wide"], mesh.shape["narrow"])
    return jax.shard_map(
        body, mesh=mesh, in_specs=in_specs, out_specs=out_specs, check_vma=False
    )
```

```python
import functools
import math

import jax
import jax.numpy as jnp
from jax import lax
from jax.experimental import pallas as pl
from jax.experimental.pallas import tpu as pltpu
from jax.sharding import PartitionSpec as P

H = 12
HD = 64
QB = 256
REACH = 512

epsilon = 1e-05
AXES = ("wide", "narrow")
VMEM = 56 * 1024 * 1024
TINY = pl.CostEstimate(flops=1000, bytes_accessed=1000, transcendentals=0)
f32 = jnp.float32
bf16 = jnp.bfloat16


def spans(length):
    out = []
    for b in range(length // QB):
        low = max(0, (b * QB - (REACH - 1)) // QB * QB)
        out.append((low, (b + 1) * QB))
    return out


def soft_rows(length):
    return sum(hi - lo for lo, hi in spans(length))


def attend_pair(doc, q, k, v, o_ref, p_ref):
    length = q.shape[0]
    lane = lax.broadcasted_iota(jnp.int32, (length, 128), 1)
    low = lane < HD
    hot = (lane & (HD - 1)) == doc
    q_side = jnp.where(hot, 1.0, 0.0)
    k_side = jnp.where(hot, 0.0, -1e9)
    q = q.astype(f32) * HD ** (-0.5)
    k = k.astype(f32)
    v_t = v.T
    sides = []
    for h in range(2):
        mine = low if h == 0 else jnp.logical_not(low)
        sides.append(
            (jnp.where(mine, q, q_side).astype(bf16), jnp.where(mine, k, k_side).astype(bf16))
        )
    rows = lax.broadcasted_iota(jnp.int32, (QB, QB), 0)
    tri = rows <= lax.broadcasted_iota(jnp.int32, (QB, QB), 1)
    at = 0
    for b, (lo, hi) in enumerate(spans(length)):
        n = hi - lo
        outs = []
        for h in range(2):
            qa, ka = sides[h]
            s = dot(ka[lo:hi], qa[b * QB : (b + 1) * QB], ((1,), (1,)))
            last = jnp.where(tri, s[n - QB :], -1e9)
            s = last if n == QB else jnp.concatenate([s[: n - QB], last], axis=0)
            e = jnp.exp(s - jnp.max(s, axis=0, keepdims=True))
            p = (e * (1.0 / jnp.sum(e, axis=0, keepdims=True))).astype(bf16)
            p_ref[h, at : at + n, :] = p
            outs.append(dot(v_t[h * HD : (h + 1) * HD, lo:hi], p))
        o_ref[b * QB : (b + 1) * QB, :] = jnp.concatenate(outs, axis=0).T.astype(bf16)
        at += n


def attend(place, doc, x, vec, weights, column, first, count, before):
    length, width = x.shape
    start = before is None
    packed = vec is None
    rows = soft_rows(length)
    n_p, n_v = len(weights.arrays), 0 if packed else 1
    n_a = 0 if start else 3

    def kernel(*refs):
        refs = list(refs)
        take = lambda n: [refs.pop(0) for _ in range(n)]
        place_ref, doc_ref, x_ref = take(3)
        vec_refs, pieces = take(n_v), take(n_p)
        take(n_a)
        mixed_ref, soft_ref, qkv_ref = take(3)
        if start:
            h1_ref, h1_t_ref, vec_out = take(3)
        w, sem = take(2)
        step = pl.program_id(0)

        @pl.when(step == 0)
        def _():
            weights.load(place_ref, pieces, w, sem)
            if start:
                if packed:
                    vec_out[...] = unpack_rows(w)
                else:
                    vec_out[...] = vec_refs[0][...]
                for at in range(0, length, 256):
                    here = slice(at, at + 256)
                    h1 = norm_rows(
                        x_ref[here, :].astype(f32), row_of(vec_out, GAIN1), row_of(vec_out, SHIFT1)
                    ).astype(bf16)
                    h1_ref[here, :] = h1
                    h1_t_ref[:, here] = h1.T

        h1 = (h1_ref if start else x_ref)[...]
        known = vec_out if start else vec_refs[0]
        cols = w[:, pl.ds(pl.multiple_of(column + step * 384, 128), 384)]
        bias = jnp.concatenate(
            [
                known[pl.ds(QV[0] + first + step, 1), :],
                jnp.zeros((1, 128), f32),
                known[pl.ds(QV[0] + 6 + first + step, 1), :],
            ],
            axis=1,
        )
        qkv = (dot(h1, cols) + bias).astype(bf16)
        qkv_ref[...] = qkv
        attend_pair(
            doc_ref[...], qkv[:, :128], qkv[:, 128:256], qkv[:, 256:], mixed_ref, soft_ref
        )

    full = lambda shape: pl.BlockSpec(shape, lambda i: (0,) * len(shape))
    anyplace = pl.BlockSpec(memory_space=pl.ANY)
    outs = [
        ((length, width), (length, 128), lambda i: (0, first + i), bf16),
        ((H, rows, QB), (2, rows, QB), lambda i: (first + i, 0, 0), bf16),
        ((length, 3 * width), (length, 384), lambda i: (0, first + i), bf16),
    ]
    if start:
        outs += [
            ((length, width), (length, width), lambda i: (0, 0), bf16),
            ((width, length), (width, length), lambda i: (0, 0), bf16),
            ((72, 128), (72, 128), lambda i: (0, 0), f32),
        ]
    given = [place.spot, doc, x] + ([] if packed else [vec]) + weights.arrays
    aliases = {}
    if not start:
        aliases = {len(given) + i: i for i in range(3)}
        given += before
    return pl.pallas_call(
        kernel,
        grid=(count,),
        in_specs=[pl.BlockSpec(memory_space=pltpu.SMEM), full((length, 1)), full(x.shape)]
        + [full((72, 128))] * n_v
        + [anyplace] * (n_p + n_a),
        out_specs=[pl.BlockSpec(block, index) for _, block, index, _ in outs],
        out_shape=[jax.ShapeDtypeStruct(shape, kind) for shape, _, _, kind in outs],
        scratch_shapes=[
            pltpu.VMEM((weights.rows, weights.width), bf16),
            pltpu.SemaphoreType.DMA((n_p,)),
        ],
        input_output_aliases=aliases,
        compiler_params=pltpu.CompilerParams(vmem_limit_bytes=VMEM),
        cost_estimate=TINY,
        name="attend",
    )(*given)


def lay_blocks(ref, place_ref, other, rows):
    out = []
    core = 1 - place_ref[0] if other else place_ref[0]
    for x in range(2):
        for y in range(2):
            at = pl.multiple_of((4 * x + 2 * core + y) * rows, 16)
            out.append(ref[pl.ds(at, rows), :])
    return jnp.concatenate(out, axis=0)


def attend_back_kernel(
    place_ref,
    q_ref,
    k_ref,
    v_ref,
    o_ref,
    do_ref,
    p_ref,
    h1_t_ref,
    *refs,
    length,
):
    out_ref, send_ref, keep_ref, dk_acc, dv_acc = refs[-5:]
    lane = lax.broadcasted_iota(jnp.int32, (length, 128), 1)
    low = lane < HD
    spot = lane & (HD - 1)
    q = q_ref[...].astype(f32) * HD ** (-0.5)
    do = do_ref[...].astype(f32)
    v = v_ref[...].astype(f32)
    product = do * o_ref[...].astype(f32)
    k_t = k_ref[...].T
    sides = []
    for h in range(2):
        mine = low if h == 0 else jnp.logical_not(low)
        center = jnp.sum(jnp.where(mine, product, 0.0), axis=1, keepdims=True)
        first = center.astype(bf16).astype(f32)
        second = (center - first).astype(bf16).astype(f32)
        third = center - first - second
        extra = jnp.where(
            spot == 0, -first, jnp.where(spot == 1, -second, jnp.where(spot == 2, -third, 0.0))
        )
        sides.append(
            (
                jnp.where(mine, do, extra).astype(bf16),
                jnp.where(mine, v, jnp.where(spot < 3, 1.0, 0.0)).astype(bf16),
                jnp.where(mine, do, 0.0).astype(bf16),
                jnp.where(mine, q, 0.0).astype(bf16),
            )
        )
    dk_acc[...] = jnp.zeros_like(dk_acc)
    dv_acc[...] = jnp.zeros_like(dv_acc)
    at = 0
    for b, (lo, hi) in enumerate(spans(length)):
        n = hi - lo
        here = slice(b * QB, (b + 1) * QB)
        dqs = []
        dk = dv = None
        for h in range(2):
            do_more, v_more, do_own, q_own = sides[h]
            p = p_ref[h, at : at + n, :]
            dp = dot(v_more[lo:hi], do_more[here], ((1,), (1,)))
            ds = (p.astype(f32) * dp).astype(bf16)
            dv_part = dot(p, do_own[here])
            dk_part = dot(ds, q_own[here])
            dv = dv_part if dv is None else dv + dv_part
            dk = dk_part if dk is None else dk + dk_part
            dqs.append(dot(k_t[h * HD : (h + 1) * HD, lo:hi], ds))
        dv_acc[lo:hi, :] += dv
        dk_acc[lo:hi, :] += dk
        out_ref[here, :128] = (jnp.concatenate(dqs, axis=0) * HD ** (-0.5)).T.astype(bf16)
        at += n
    out_ref[:, 128:256] = dk_acc[...].astype(bf16)
    out_ref[:, 256:] = dv_acc[...].astype(bf16)
    parts = out_ref[...]
    for other, ref in ((True, send_ref), (False, keep_ref)):
        rows = h1_t_ref.shape[0] // 8
        ref[...] = dot(lay_blocks(h1_t_ref, place_ref, other, rows), parts).astype(bf16)


def attend_back(place, qkv, mixed, grad_mixed, soft, h1_t, first, count, before):
    length, width = mixed.shape
    rows = soft_rows(length)
    col = lambda off: pl.BlockSpec((length, 128), lambda i: (0, 3 * (first + i) + off))
    pair = pl.BlockSpec((length, 128), lambda i: (0, first + i))
    terms = pl.BlockSpec((width // 2, 384), lambda i: (0, i))
    term = jax.ShapeDtypeStruct((width // 2, 384 * count), bf16)
    given = [place.spot, qkv, qkv, qkv, mixed, grad_mixed, soft, h1_t]
    aliases = {}
    if before is not None:
        aliases = {len(given): 0}
        given.append(before)
    return pl.pallas_call(
        functools.partial(attend_back_kernel, length=length),
        grid=(count,),
        in_specs=[
            pl.BlockSpec(memory_space=pltpu.SMEM),
            col(0),
            col(1),
            col(2),
            pair,
            pair,
            pl.BlockSpec((2, rows, QB), lambda i: (first + i, 0, 0)),
            pl.BlockSpec(h1_t.shape, lambda i: (0, 0)),
        ]
        + [pl.BlockSpec(memory_space=pl.ANY)] * len(aliases),
        out_specs=[pl.BlockSpec((length, 384), lambda i: (0, first + i)), terms, terms],
        out_shape=[jax.ShapeDtypeStruct(qkv.shape, bf16), term, term],
        scratch_shapes=[pltpu.VMEM((length, 128), f32)] * 2,
        input_output_aliases=aliases,
        compiler_params=pltpu.CompilerParams(vmem_limit_bytes=VMEM),
        cost_estimate=TINY,
        name="attend_back",
    )(*given)


def proj_terms(place, g_t, dout):
    hidden, length = g_t.shape
    width = dout.shape[1]
    rows = hidden // 8

    def kernel(place_ref, g_ref, dout_ref, send_ref, keep_ref):
        value = dot(g_ref[...], dout_ref[...]).astype(bf16)

        @pl.when(pl.program_id(0) < 4)
        def _():
            send_ref[...] = value

        @pl.when(pl.program_id(0) >= 4)
        def _():
            keep_ref[...] = value

    def block(i, place_ref):
        core = jnp.where(i < 4, 1 - place_ref[0], place_ref[0])
        j = i % 4
        return 4 * (j // 2) + 2 * core + j % 2, 0

    out = jax.ShapeDtypeStruct((hidden // 2, width), bf16)
    return pl.pallas_call(
        kernel,
        grid_spec=pltpu.PrefetchScalarGridSpec(
            num_scalar_prefetch=1,
            grid=(8,),
            in_specs=[
                pl.BlockSpec((rows, length), block),
                pl.BlockSpec((length, width), lambda i, p: (0, 0)),
            ],
            out_specs=[
                pl.BlockSpec((rows, width), lambda i, p: (jnp.minimum(i, 3), 0)),
                pl.BlockSpec((rows, width), lambda i, p: (jnp.maximum(i - 4, 0), 0)),
            ],
        ),
        out_shape=[out, out],
        compiler_params=pltpu.CompilerParams(vmem_limit_bytes=VMEM),
        cost_estimate=TINY,
        name="proj_terms",
    )(place.spot, g_t, dout)


def back_middle(place, dout, slope, y1, mixed, h2_t, vec, w_out, w_fc, w_proj):
    length, width = dout.shape
    hidden = w_fc.width
    step_rows, part = 256, 512
    steps = length // step_rows
    f_steps, rows = hidden // width, width // 8
    weights = (w_out, w_fc, w_proj)
    counts = [len(w.arrays) for w in weights]

    def kernel(*refs):
        refs = list(refs)
        take = lambda n: [refs.pop(0) for _ in range(n)]
        place_ref, dout_ref, slope_ref, y1_ref, mixed_ref, h2_t, vec_ref = take(7)
        pieces = [take(n) for n in counts]
        dmixed_ref, dy1_ref, send_ref, keep_ref = take(4)
        gain_ref, shift_ref, outb_ref, fcb_ref, projb_ref = sums = take(5)
        wo, wf, wp = buffers = take(3)
        sems = take(3)
        du_all, mixed_t, db1_all = take(3)
        i = pl.program_id(0)

        @pl.when(i == 0)
        def _():
            for w, own, buffer, sem in zip(weights, pieces, buffers, sems):
                w.load(place_ref, own, buffer, sem)
            for ref in sums:
                ref[...] = jnp.zeros_like(ref)

        @pl.when(i < steps)
        def _():
            here = pl.ds(pl.multiple_of(i * step_rows, step_rows), step_rows)
            dout = dout_ref[...]
            mixed_t[:, here] = mixed_ref[...].T
            dh2 = jnp.zeros((step_rows, width), f32)
            for c in range(0, hidden, part):
                cols = slice(c, c + part)
                du = dot(dout, wp[cols, :], ((1,), (1,))) * slope_ref[:, cols].astype(f32)
                du = du.astype(bf16)
                du_all[here, cols] = du
                fcb_ref[:, cols] += jnp.sum(du.astype(f32), axis=0, keepdims=True)
                dh2 = dh2 + dot(du, wf[:, cols], ((1,), (1,)))
            back, gain, shift = norm_back(y1_ref[...], row_of(vec_ref, GAIN2), dh2)
            wide_dout = dout.astype(f32)
            dy1 = wide_dout + back
            db1 = dy1.astype(bf16)
            dy1_ref[...] = dy1
            db1_all[here, :] = db1
            dmixed_ref[...] = dot(db1, wo[...], ((1,), (1,))).astype(bf16)
            gain_ref[...] += gain
            shift_ref[...] += shift
            outb_ref[...] += jnp.sum(db1.astype(f32), axis=0, keepdims=True)
            projb_ref[...] += jnp.sum(wide_dout, axis=0, keepdims=True)

        j = i - steps

        @pl.when((j >= 0) & (j < f_steps))
        def _():
            cols = pl.ds(pl.multiple_of(j * width, 128), width)
            for other, ref in ((True, send_ref), (False, keep_ref)):
                value = dot(lay_blocks(h2_t, place_ref, other, rows), du_all[:, cols])
                ref[...] = value.astype(bf16).reshape(ref.shape)

        @pl.when(j == f_steps)
        def _():
            for other, ref in ((True, send_ref), (False, keep_ref)):
                value = dot(lay_blocks(mixed_t, place_ref, other, rows), db1_all[...])
                ref[...] = value.astype(bf16).reshape(ref.shape)

    full = lambda shape: pl.BlockSpec(shape, lambda i: (0,) * len(shape))
    slab = lambda n: pl.BlockSpec((step_rows, n), lambda i: (jnp.minimum(i, steps - 1), 0))
    terms = pl.BlockSpec(
        (4, rows, width), lambda i: (0, jnp.clip(i - steps, 0, f_steps), 0)
    )
    like = jax.ShapeDtypeStruct
    one = (1, width)
    sum_shapes = [one, one, one, (1, hidden), one]
    return pl.pallas_call(
        kernel,
        grid=(steps + f_steps + 1,),
        in_specs=[
            pl.BlockSpec(memory_space=pltpu.SMEM),
            slab(width),
            slab(hidden),
            slab(width),
            slab(width),
            full(h2_t.shape),
            full((72, 128)),
        ]
        + [pl.BlockSpec(memory_space=pl.ANY)] * sum(counts),
        out_specs=[slab(width), slab(width), terms, terms] + [full(v) for v in sum_shapes],
        out_shape=[
            like((length, width), bf16),
            like((length, width), f32),
            like((4, rows * (f_steps + 1), width), bf16),
            like((4, rows * (f_steps + 1), width), bf16),
        ]
        + [like(v, f32) for v in sum_shapes],
        scratch_shapes=[pltpu.VMEM((w.rows, w.width), bf16) for w in weights]
        + [pltpu.SemaphoreType.DMA((n,)) for n in counts]
        + [
            pltpu.VMEM((length, hidden), bf16),
            pltpu.VMEM((width, length), bf16),
            pltpu.VMEM((length, width), bf16),
        ],
        compiler_params=pltpu.CompilerParams(vmem_limit_bytes=VMEM),
        cost_estimate=TINY,
        name="back_middle",
    )(place.spot, dout, slope, y1, mixed, h2_t, vec, *[v for w in weights for v in w.arrays])


class Place:
    def __init__(self, owner, wide, narrow, plain):
        self.wide, self.narrow = wide, narrow
        self.deep = wide // 4
        mine = lax.axis_index("wide")
        self.core, self.y, self.z = mine & 1, (mine >> 1) & 1, mine >> 2
        self.o_core, self.o_y, self.o_z = owner & 1, (owner >> 1) & 1, owner >> 2
        self.x = lax.axis_index("narrow")
        self.holder = mine == owner
        spot = jnp.stack([self.core, self.x, self.y]).astype(jnp.int32)
        self.spot = jnp.zeros_like(spot) if plain else spot

    def swap(self, value, flip):
        return lax.ppermute(value, "wide", [(i, i ^ flip) for i in range(self.wide)])

    def cross(self, value, flip):
        pairs = [(2 * i + j, 2 * (i ^ flip) + 1 - j) for i in range(self.wide) for j in range(2)]
        return lax.ppermute(value, AXES, pairs)

    def z_flips(self):
        step = self.deep // 2
        while step:
            yield step
            step //= 2


def pick(parts, index):
    return lax.dynamic_index_in_dim(parts, index, axis=0, keepdims=False)


def ordered(mine, other, index):
    first = index == 0
    return jnp.stack([jnp.where(first, mine, other), jnp.where(first, other, mine)])


def spread_plain(place, shard):
    now = jnp.where(place.core == place.o_core, shard, place.swap(shard, 1))
    now = jnp.where(place.y == place.o_y, now, place.swap(now, 2))
    for step in place.z_flips():
        other = place.swap(now, 4 * step)
        now = jnp.where((place.z & step) == (place.o_z & step), now, other)
    return lax.all_gather(now, "narrow", axis=0, tiled=True)


def spread_steps(place, shard):
    if isinstance(shard, tuple):
        keep, send = shard
    else:
        halves = shard.reshape(2, shard.shape[0] // 2, shard.shape[1])
        keep, send = pick(halves, place.core), pick(halves, 1 - place.core)
    rows, width = 2 * keep.shape[0], keep.shape[1]
    (other,) = yield [(send, 1)]
    now = jnp.where(place.core == place.o_core, keep, other)
    halves = now.reshape(2, rows // 4, width)
    (other,) = yield [(pick(halves, 1 - place.y), 2)]
    now = jnp.where(place.y == place.o_y, pick(halves, place.y), other)
    for step in place.z_flips():
        (other,) = yield [(now, 4 * step)]
        now = jnp.where((place.z & step) == (place.o_z & step), now, other)
    by_y, by_x = yield [(now, 2), (now, 0)]
    cut = rows // 8
    far_a, far_b = yield [(by_y[:cut], 0), (by_x[cut:], 2)]
    mine = [
        (now, (0, 0, 0), 0),
        (by_y, (0, 0, 1), 0),
        (by_x, (0, 1, 0), 0),
        (far_a, (0, 1, 1), 0),
        (far_b, (0, 1, 1), cut),
    ]
    theirs = yield [(piece, 1) for piece, _, _ in mine]
    return Pieces(
        mine + [(got, (1, x, y), row) for got, (_, (_, x, y), row) in zip(theirs, mine)]
    )


class Pieces:
    def __init__(self, found):
        self.arrays = [piece for piece, _, _ in found]
        self.spots = [(flips, row) for _, flips, row in found]
        self.block, self.width = self.arrays[0].shape
        self.rows = self.block if len(found) == 1 else 8 * self.block

    def over(self, arrays):
        return Pieces([(v, flips, row) for v, (flips, row) in zip(arrays, self.spots)])

    def load(self, place_ref, refs, buffer, sem):
        copies = []
        for ref, ((core, x, y), row) in zip(refs, self.spots):
            start = 0
            if len(refs) > 1:
                at = 4 * (place_ref[1] ^ x) + 2 * (place_ref[0] ^ core) + (place_ref[2] ^ y)
                start = pl.multiple_of(at * self.block + row, 16)
            target = buffer.at[pl.ds(start, ref.shape[0]), :]
            copies.append(pltpu.make_async_copy(ref, target, sem.at[len(copies)]))
        for copy in copies:
            copy.start()
        for copy in copies:
            copy.wait()


ROWS = 256


def by_rows(name, body, place, blocks, wholes, weights, out_blocks, out_sums):
    length = blocks[0].shape[0]
    n_b, n_w, n_o, n_s = len(blocks), len(wholes), len(out_blocks), len(out_sums)
    counts = [len(w.arrays) for w in weights]

    def kernel(*refs):
        refs = list(refs)
        take = lambda n: [refs.pop(0) for _ in range(n)]
        (place_ref,) = take(1)
        block_refs, whole_refs = take(n_b), take(n_w)
        piece_refs = [take(n) for n in counts]
        out_refs, sum_refs = take(n_o), take(n_s)
        buffers, sems = take(len(weights)), take(len(weights))

        @pl.when(pl.program_id(0) == 0)
        def _():
            for w, pieces, buffer, sem in zip(weights, piece_refs, buffers, sems):
                w.load(place_ref, pieces, buffer, sem)
            for ref in sum_refs:
                ref[...] = jnp.zeros_like(ref)

        body(block_refs, whole_refs, buffers, out_refs, sum_refs)

    full = lambda shape: pl.BlockSpec(shape, lambda i: (0,) * len(shape))
    slab = lambda shape: (
        pl.BlockSpec((ROWS, shape[1]), lambda i: (i, 0))
        if shape[0] == length
        else pl.BlockSpec((shape[0], ROWS), lambda i: (0, i))
    )
    return pl.pallas_call(
        kernel,
        grid=(length // ROWS,),
        in_specs=[pl.BlockSpec(memory_space=pltpu.SMEM)]
        + [slab(v.shape) for v in blocks]
        + [full(v.shape) for v in wholes]
        + [pl.BlockSpec(memory_space=pl.ANY)] * sum(counts),
        out_specs=[slab(shape) for shape, _ in out_blocks] + [full(s) for s in out_sums],
        out_shape=[jax.ShapeDtypeStruct(shape, kind) for shape, kind in out_blocks]
        + [jax.ShapeDtypeStruct(shape, f32) for shape in out_sums],
        scratch_shapes=[pltpu.VMEM((w.rows, w.width), bf16) for w in weights]
        + [pltpu.SemaphoreType.DMA((n,)) for n in counts],
        compiler_params=pltpu.CompilerParams(vmem_limit_bytes=VMEM),
        cost_estimate=TINY,
        name=name,
    )(place.spot, *blocks, *wholes, *[v for w in weights for v in w.arrays])


def tie(groups):
    flat, tree = jax.tree.flatten(groups)
    return jax.tree.unflatten(tree, lax.optimization_barrier(flat))


class Steps:
    def __init__(self, place):
        self.place = place
        self.asked, self.flips, self.chains, self.done, self.going = {}, {}, {}, {}, {}

    def ask(self, name, pairs):
        self.asked[name] = [value for value, _ in pairs]
        self.flips[name] = [flip for _, flip in pairs]

    def add(self, name, chain):
        self.chains[name] = chain
        self.ask(name, next(chain))

    def exchange(self, value, flip):
        if flip <= 0:
            return self.place.cross(value, -flip)
        return self.place.swap(value, flip)

    def slot(self, names="", hold="", work=None, given=()):
        names, hold = names.split(), hold.split()
        assert not set(names) & set(self.going)
        asked = {name: self.asked[name] for name in names if name in self.asked}
        held = tie({"asked": asked, "given": given})
        for name, values in held["asked"].items():
            self.going[name] = [
                self.exchange(value, flip) for value, flip in zip(values, self.flips[name])
            ]
        result = work(*held["given"]) if work else ()
        ready = {name: got for name, got in self.going.items() if name not in hold}
        ready, result, self.asked = tie((ready, result, self.asked))
        for name, got in ready.items():
            del self.going[name], self.asked[name]
            try:
                self.ask(name, self.chains[name].send(got))
            except StopIteration as stop:
                self.done[name] = stop.value
        return result


def collect_plain(place, keep, send):
    width = keep.shape[-1]
    parts = [v.reshape(2, 1, 2, -1, width) for v in (keep, send)]
    terms = jnp.concatenate(parts, axis=1).reshape(-1, width)
    now = lax.psum_scatter(terms, "narrow", scatter_dimension=0, tiled=True)
    return lax.psum(now, "wide")


def add(*values):
    return functools.reduce(lambda a, b: a + b, [v.astype(f32) for v in values]).astype(bf16)


def collect_steps(place, keep, send):
    width, deep = keep.shape[-1], place.deep
    (other,) = yield [(send, 1)]
    now = add(keep, other).reshape(4, -1, width)
    spot = 2 * place.x + place.y
    got = yield [(pick(now, spot ^ 2), 0), (pick(now, spot ^ 1), 2), (pick(now, spot ^ 3), -2)]
    now = add(pick(now, spot), *got).reshape(deep, -1, width)
    got = yield [(pick(now, place.z ^ i), 4 * i) for i in range(1, deep)]
    now = add(pick(now, place.z), *got)
    got = yield [(now, 4 * i) for i in range(1, deep)]
    now = jnp.stack(
        [lax.select_n(place.z ^ i, now, *got) for i in range(deep)]
    ).reshape(-1, width)
    (other,) = yield [(now, 2)]
    now = ordered(now, other, place.y)
    (other,) = yield [(now, 1)]
    return ordered(now, other, place.core).reshape(-1, width)


def unpack_vectors(now, sizes):
    now = now.reshape(1, -1)
    out, at = [], 0
    for size in sizes:
        out.append(now[:, at : at + size])
        at += size
    return out


def shares(vectors, narrow):
    out = []
    for i in range(narrow):
        for v in vectors:
            size = v.shape[1] // narrow
            out.append(v[:, i * size : (i + 1) * size])
    return jnp.concatenate(out, axis=1)


def collect_vectors_steps(place, vectors):
    now = shares(vectors, 2).reshape(2, -1, 128)
    (other,) = yield [(now, 1)]
    now = now + other
    (other,) = yield [(pick(now, 1 - place.x), 0)]
    now = pick(now, place.x) + other
    (other,) = yield [(now, 2)]
    now = now + other
    for step in place.z_flips():
        (other,) = yield [(now, 4 * step)]
        now = now + other
    return now


def collect_vectors_plain(place, vectors):
    now = shares(vectors, place.narrow).reshape(place.narrow, -1)
    now = lax.psum_scatter(now, "narrow", scatter_dimension=0, tiled=False)
    return lax.psum(now, "wide")


def norm_rows(values, gain, shift):
    center = values - jnp.mean(values, axis=-1, keepdims=True)
    spread_of = jnp.mean(center * center, axis=-1, keepdims=True)
    return center * lax.rsqrt(spread_of + epsilon) * gain + shift


def norm_back(values, gain, grad):
    center = values - jnp.mean(values, axis=-1, keepdims=True)
    inverse = lax.rsqrt(jnp.mean(center * center, axis=-1, keepdims=True) + epsilon)
    hat = center * inverse
    scaled = grad * gain
    inner = jnp.mean(scaled * hat, axis=-1, keepdims=True)
    back = inverse * (scaled - jnp.mean(scaled, axis=-1, keepdims=True) - hat * inner)
    return (
        back,
        jnp.sum(grad * hat, axis=0, keepdims=True),
        jnp.sum(grad, axis=0, keepdims=True),
    )


def gelu_both(u):
    c = math.sqrt(2.0 / math.pi)
    square = u * u
    half = 0.5 + 0.5 * jnp.tanh(u * (c + c * 0.044715 * square))
    g = u * half
    return g, half + g * (1.0 - half) * (2 * c + 6 * c * 0.044715 * square)


def dot(a, b, dims=((1,), (0,))):
    return lax.dot_general(a, b, (dims, ((), ())), preferred_element_type=f32)


GAIN1, SHIFT1, QV, OUTB = (0, 6), (6, 6), (12, 12), (24, 6)
GAIN2, SHIFT2, FCB, PROJB = (30, 6), (36, 6), (42, 24), (66, 6)


def row_of(vec, spot, first=0, count=None):
    start = spot[0] + first
    count = spot[1] if count is None else count
    return jnp.concatenate([vec[start + i : start + i + 1, :] for i in range(count)], axis=1)


def unpack_rows(w):
    shard = w.shape[0] // 2
    near = w[:64, w.shape[1] - 128 :].astype(f32)
    far = w[shard : shard + 64, w.shape[1] - 128 :].astype(f32)
    parts = []
    for start, count in (GAIN1, SHIFT1, QV, OUTB, GAIN2, SHIFT2, FCB, PROJB):
        rows = slice(start // 2, (start + count) // 2)
        parts += [near[rows], far[rows]]
    return jnp.concatenate(parts, axis=0)


def pack_kernel(core_ref, w_ref, *refs):
    vectors, outs, rows_ref = refs[:-5], refs[-5:-1], refs[-1]
    half, width = w_ref.shape[0] // 2, w_ref.shape[1] // 3
    rows_ref[...] = jnp.zeros_like(rows_ref)
    at = 0
    for ref in vectors:
        value = ref[...].astype(f32)
        for i in range(value.shape[1] // 128):
            rows_ref[at : at + 1, :] = value[:, i * 128 : (i + 1) * 128]
            at += 1
    pairs = width // 128
    for other in range(2):
        core = 1 - core_ref[0] if other else core_ref[0]
        w = w_ref[pl.ds(pl.multiple_of(core * half, 16), half), :]
        for part in range(2):
            ref = outs[2 * part + other]
            for p in range(pairs // 2):
                for j in range(3):
                    source = j * width + (part * (pairs // 2) + p) * 128
                    to = (3 * p + j) * 128
                    ref[:, to : to + 128] = w[:, source : source + 128]
            if part == 0:
                block = rows_ref[...].astype(bf16)
                ref[:, 3 * width // 2 :] = jnp.concatenate([block, block], axis=0)


def pack(place, w, vectors):
    rows, width = w.shape
    side = width // 2
    shape = lambda more: jax.ShapeDtypeStruct((rows // 2, side + more), bf16)
    vmem = pl.BlockSpec(memory_space=pltpu.VMEM)
    near, near_send, far, far_send = pl.pallas_call(
        pack_kernel,
        in_specs=[pl.BlockSpec(memory_space=pltpu.SMEM)] + [vmem] * (1 + len(vectors)),
        out_specs=[vmem] * 4,
        out_shape=[shape(128), shape(128), shape(0), shape(0)],
        scratch_shapes=[pltpu.VMEM((rows // 4, 128), f32)],
        compiler_params=pltpu.CompilerParams(vmem_limit_bytes=VMEM),
        cost_estimate=TINY,
        name="pack",
    )(place.spot, w, *vectors)
    return (near, near_send), (far, far_send)


def widen_body(blocks, wholes, weights, outs, sums):
    (x_ref, mixed_ref), (vec,), (w_out, w_fc) = blocks, wholes, weights
    y1_ref, slope_ref, h2_t_ref, g_t_ref = outs
    y1 = x_ref[...].astype(f32) + dot(mixed_ref[...], w_out[...]) + row_of(vec, OUTB)
    y1_ref[...] = y1
    h2 = norm_rows(y1, row_of(vec, GAIN2), row_of(vec, SHIFT2)).astype(bf16)
    h2_t_ref[...] = h2.T
    for at in range(0, w_fc.shape[1], 512):
        here = slice(at, at + 512)
        g, slope = gelu_both(dot(h2, w_fc[:, here]) + row_of(vec, FCB, at // 128, 4))
        g_t_ref[here, :] = g.astype(bf16).T
        slope_ref[:, here] = slope.astype(bf16)


def finish_body(blocks, wholes, weights, outs, sums):
    (y1_ref, g_t_ref), (vec,), (w,) = blocks, wholes, weights
    result = y1_ref[...] + dot(g_t_ref[...], w[...], ((0,), (0,))) + row_of(vec, PROJB)
    outs[0][...] = result.astype(bf16)


def back_first_body(blocks, wholes, weights, outs, sums):
    (dqkv_ref, x_ref, dy1_ref), (vec,), (w_a, w_b) = blocks, wholes, weights
    side = w_b.shape[1]
    dqkv = dqkv_ref[...]
    dh1 = dot(dqkv[:, :side], w_a[:, :side], ((1,), (1,)))
    dh1 = dh1 + dot(dqkv[:, side:], w_b[...], ((1,), (1,)))
    back, gain, shift = norm_back(x_ref[...].astype(f32), row_of(vec, GAIN1), dh1)
    outs[0][...] = (dy1_ref[...] + back).astype(bf16)
    total = jnp.sum(dqkv.astype(f32), axis=0, keepdims=True)
    parts = [total[:, p * 384 + j : p * 384 + j + 128] for j in (0, 256) for p in range(H // 2)]
    for ref, value in zip(sums, (gain, shift, jnp.concatenate(parts, axis=1))):
        ref[...] += value


def on_device(
    wide,
    narrow,
    tokens,
    doc_ids,
    cotangent,
    owner,
    ln1_gain,
    ln1_bias,
    qkv_weight,
    qv_bias,
    out_weight,
    out_bias,
    ln2_gain,
    ln2_bias,
    fc_weight,
    fc_bias,
    proj_weight,
    proj_bias,
):
    _, length, width = tokens.shape
    plain = narrow != 2 or ln1_gain.shape[1] % 128 != 0
    place = Place(owner[0], wide, narrow, plain)
    x = tokens[0]
    dout = cotangent[0]
    doc = doc_ids[0][:, None]
    pairs = H // 2
    half = pairs // 2

    def begin(name, shard):
        if plain:
            steps.done[name] = Pieces([(spread_plain(place, shard), (0, 0, 0), 0)])
        else:
            steps.add(name, spread_steps(place, shard))

    def end(name, keep, send):
        if plain:
            steps.done[name] = collect_plain(place, keep, send)
        else:
            steps.add(name, collect_steps(place, keep, send))

    steps = Steps(place)
    vectors = (ln1_gain, ln1_bias, qv_bias, out_bias, ln2_gain, ln2_bias, fc_bias, proj_bias)
    sizes = [v.shape[1] for v in vectors]
    vec = None
    if plain:
        rows = spread_plain(place, jnp.concatenate(vectors, axis=1))
        parts, at = [], 0
        for size in sizes:
            parts.append(rows[:, at : at + size].reshape(-1))
            at += size
        vec = jnp.concatenate(parts).reshape(-1, 128).astype(f32)
        order = [
            qkv_weight[0][:, j * width + p * 128 : j * width + (p + 1) * 128]
            for p in range(pairs)
            for j in range(3)
        ]
        near = jnp.concatenate(order[: 3 * half], axis=1)
        far = jnp.concatenate(order[3 * half :], axis=1)
    else:
        near, far = pack(place, qkv_weight[0], vectors)
    begin("qa", near)
    begin("qb", far)
    begin("o", out_weight[0])
    begin("f", fc_weight[0])
    begin("p", proj_weight[0])

    def attention(x, vec, name, column, first, count, before):
        weights = steps.done[name]

        def run(x, vec, arrays, before):
            return attend(place, doc, x, vec, weights.over(arrays), column, first, count, before)

        return dict(work=run, given=(x, vec, weights.arrays, before))

    def rows_work(name, body, blocks, wholes, weights, out_blocks, out_sums):
        def run(blocks, wholes, arrays):
            held = [w.over(own) for w, own in zip(weights, arrays)]
            return by_rows(name, body, place, blocks, wholes, held, out_blocks, out_sums)

        return dict(work=run, given=(blocks, wholes, [w.arrays for w in weights]))

    steps.slot("qa qb")
    steps.slot("qa o f p")
    steps.slot("qa qb o")
    steps.slot("qa qb f", hold="qb f")
    steps.slot("qa", hold="f")
    steps.slot("qa qb o")
    steps.slot("qa qb f p", hold="f p")
    state = steps.slot("qb o", **attention(x, vec, "qa", 0, 0, 2, None))
    state, (h1, h1_t, vec) = list(state[:3]), state[3:]
    state = steps.slot(
        "qb o f p", hold="p", **attention(h1, vec, "qa", 768, 2, 1, state)
    )
    state = steps.slot("o f", hold="", **attention(h1, vec, "qb", 0, 3, 2, list(state)))
    state = steps.slot("f o p", **attention(h1, vec, "qb", 768, 5, 1, list(state)))
    mixed, soft, qkv = state
    steps.slot("f p", hold="p")
    w_a, w_b, w_out, w_fc = [steps.done[name] for name in ("qa", "qb", "o", "f")]
    hidden = w_fc.width
    y1, slope, h2_t, g_t = steps.slot(
        "",
        **rows_work(
            "widen",
            widen_body,
            [x, mixed],
            [vec],
            [w_out, w_fc],
            [
                ((length, width), f32),
                ((length, hidden), bf16),
                ((width, length), bf16),
                ((hidden, length), bf16),
            ],
            [],
        ),
    )
    p_send, p_keep = steps.slot(
        "p", work=lambda g_t, dout: proj_terms(place, g_t, dout), given=(g_t, dout)
    )
    end("dp", p_keep, p_send)
    steps.slot("p dp")
    w_proj = steps.done["p"]

    def run(dout, slope, y1, mixed, h2_t, vec, arrays):
        held = [w.over(own) for w, own in zip((w_out, w_fc, w_proj), arrays)]
        return back_middle(place, dout, slope, y1, mixed, h2_t, vec, *held)

    found = steps.slot(
        "dp",
        work=run,
        given=(dout, slope, y1, mixed, h2_t, vec, [w.arrays for w in (w_out, w_fc, w_proj)]),
    )
    dmixed, dy1, f_send, f_keep, d_gain2, d_shift2, d_outb, d_fcb, d_projb = found
    end("df", f_keep, f_send)

    def heads_back(first, count, before):
        def run(qkv, mixed, dmixed, soft, h1_t, before):
            return attend_back(place, qkv, mixed, dmixed, soft, h1_t, first, count, before)

        return dict(work=run, given=(qkv, mixed, dmixed, soft, h1_t, before))

    steps.slot("df dp", hold="dp")
    dqkv, a_send, a_keep = steps.slot("df", hold="df", **heads_back(0, half, None))
    end("da", a_keep, a_send)
    steps.slot("da dp", hold="dp df")
    dqkv, b_send, b_keep = steps.slot("da", **heads_back(half, half, dqkv))
    end("db", b_keep, b_send)
    sums = [(1, width), (1, width), (1, 2 * width)]
    tokens_grad, d_gain1, d_shift1, d_qv = steps.slot(
        "db df dp da",
        **rows_work(
            "back_first",
            back_first_body,
            [dqkv, x, dy1],
            [vec],
            [w_a, w_b],
            [((length, width), bf16)],
            sums,
        ),
    )
    small = (d_gain1, d_shift1, d_qv, d_outb, d_gain2, d_shift2, d_fcb, d_projb)
    if plain:
        steps.done["dv"] = collect_vectors_plain(place, small)
    else:
        steps.add("dv", collect_vectors_steps(place, small))
    (block_out,) = steps.slot(
        "db df dp da dv",
        **rows_work(
            "finish", finish_body, [y1, g_t], [vec], [w_proj], [((length, width), bf16)], []
        ),
    )
    while steps.asked:
        steps.slot("db da df dp dv")

    put = lambda v: jnp.where(place.holder, v.astype(f32), 0.0)
    s_proj = put(steps.done["dp"])[None]
    block = width // 8
    found = steps.done["df"].reshape(-1, hidden // width + 1, block, width)
    fc = [found[:, i].reshape(-1, width) for i in range(hidden // width)]
    s_fc = put(jnp.concatenate(fc, axis=1))[None]
    s_out = put(found[:, -1].reshape(-1, width))[None]
    both = [
        v[:, (3 * p + j) * 128 : (3 * p + j + 1) * 128]
        for j in range(3)
        for v in (steps.done["da"], steps.done["db"])
        for p in range(half)
    ]
    s_qkv = put(jnp.concatenate(both, axis=1))[None]
    small = unpack_vectors(steps.done["dv"], [v.shape[1] // narrow for v in small])
    s_gain1, s_shift1, s_qv, s_outb, s_gain2, s_shift2, s_fcb, s_projb = [put(v) for v in small]
    return (
        block_out[None],
        tokens_grad[None],
        s_gain1,
        s_shift1,
        s_qkv,
        s_qv,
        s_out,
        s_outb,
        s_gain2,
        s_shift2,
        s_fc,
        s_fcb,
        s_proj,
        s_projb,
    )


def solution(mesh):
    rows = P(AXES, None, None)
    flat, deep = P("wide", "narrow"), P("wide", "narrow", None)
    in_specs = (
        rows,
        P(AXES, None),
        rows,
        P(),
        flat,
        flat,
        deep,
        flat,
        deep,
        flat,
        flat,
        flat,
        deep,
        flat,
        deep,
        flat,
    )
    out_specs = (
        rows,
        rows,
        flat,
        flat,
        deep,
        flat,
        deep,
        flat,
        flat,
        flat,
        deep,
        flat,
        deep,
        flat,
    )
    body = functools.partial(on_device, mesh.shape["wide"], mesh.shape["narrow"])
    return jax.shard_map(
        body, mesh=mesh, in_specs=in_specs, out_specs=out_specs, check_vma=False
    )
```

```python
import functools
import math

import jax
import jax.numpy as jnp
from jax import lax
from jax.experimental import pallas as pl
from jax.experimental.pallas import tpu as pltpu
from jax.sharding import PartitionSpec as P

H = 12
HD = 64
QB = 256
REACH = 512

epsilon = 1e-05
AXES = ("wide", "narrow")
VMEM = 56 * 1024 * 1024
TINY = pl.CostEstimate(flops=1000, bytes_accessed=1000, transcendentals=0)
f32 = jnp.float32
bf16 = jnp.bfloat16


def spans(length):
    out = []
    for b in range(length // QB):
        low = max(0, (b * QB - (REACH - 1)) // QB * QB)
        out.append((low, (b + 1) * QB))
    return out


def soft_rows(length):
    return sum(hi - lo for lo, hi in spans(length))


def attend_pair(doc, q, k, v, o_ref, p_ref):
    length = q.shape[0]
    lane = lax.broadcasted_iota(jnp.int32, (length, 128), 1)
    low = lane < HD
    hot = (lane & (HD - 1)) == doc
    q_side = jnp.where(hot, 1.0, 0.0)
    k_side = jnp.where(hot, 0.0, -1e9)
    q = q.astype(f32) * HD ** (-0.5)
    k = k.astype(f32)
    v_t = v.T
    sides = []
    for h in range(2):
        mine = low if h == 0 else jnp.logical_not(low)
        sides.append(
            (jnp.where(mine, q, q_side).astype(bf16), jnp.where(mine, k, k_side).astype(bf16))
        )
    rows = lax.broadcasted_iota(jnp.int32, (QB, QB), 0)
    tri = rows <= lax.broadcasted_iota(jnp.int32, (QB, QB), 1)
    at = 0
    for b, (lo, hi) in enumerate(spans(length)):
        n = hi - lo
        outs = []
        for h in range(2):
            qa, ka = sides[h]
            s = dot(ka[lo:hi], qa[b * QB : (b + 1) * QB], ((1,), (1,)))
            last = jnp.where(tri, s[n - QB :], -1e9)
            s = last if n == QB else jnp.concatenate([s[: n - QB], last], axis=0)
            e = jnp.exp(s - jnp.max(s, axis=0, keepdims=True))
            p = (e * (1.0 / jnp.sum(e, axis=0, keepdims=True))).astype(bf16)
            p_ref[h, at : at + n, :] = p
            outs.append(dot(v_t[h * HD : (h + 1) * HD, lo:hi], p))
        o_ref[b * QB : (b + 1) * QB, :] = jnp.concatenate(outs, axis=0).T.astype(bf16)
        at += n


def attend(place, doc, x, vec, weights, column, first, count, before):
    length, width = x.shape
    start = before is None
    packed = vec is None
    rows = soft_rows(length)
    n_p, n_v = len(weights.arrays), 0 if packed else 1
    n_a = 0 if start else 3

    def kernel(*refs):
        refs = list(refs)
        take = lambda n: [refs.pop(0) for _ in range(n)]
        place_ref, doc_ref, x_ref = take(3)
        vec_refs, pieces = take(n_v), take(n_p)
        take(n_a)
        mixed_ref, soft_ref, qkv_ref = take(3)
        if start:
            h1_ref, h1_t_ref, vec_out = take(3)
        w, sem = take(2)
        step = pl.program_id(0)

        @pl.when(step == 0)
        def _():
            weights.load(place_ref, pieces, w, sem)
            if start:
                if packed:
                    vec_out[...] = unpack_rows(w)
                else:
                    vec_out[...] = vec_refs[0][...]
                for at in range(0, length, 256):
                    here = slice(at, at + 256)
                    h1 = norm_rows(
                        x_ref[here, :].astype(f32), row_of(vec_out, GAIN1), row_of(vec_out, SHIFT1)
                    ).astype(bf16)
                    h1_ref[here, :] = h1
                    h1_t_ref[:, here] = h1.T

        h1 = (h1_ref if start else x_ref)[...]
        known = vec_out if start else vec_refs[0]
        cols = w[:, pl.ds(pl.multiple_of(column + step * 384, 128), 384)]
        bias = jnp.concatenate(
            [
                known[pl.ds(QV[0] + first + step, 1), :],
                jnp.zeros((1, 128), f32),
                known[pl.ds(QV[0] + 6 + first + step, 1), :],
            ],
            axis=1,
        )
        qkv = (dot(h1, cols) + bias).astype(bf16)
        qkv_ref[...] = qkv
        attend_pair(
            doc_ref[...], qkv[:, :128], qkv[:, 128:256], qkv[:, 256:], mixed_ref, soft_ref
        )

    full = lambda shape: pl.BlockSpec(shape, lambda i: (0,) * len(shape))
    anyplace = pl.BlockSpec(memory_space=pl.ANY)
    outs = [
        ((length, width), (length, 128), lambda i: (0, first + i), bf16),
        ((H, rows, QB), (2, rows, QB), lambda i: (first + i, 0, 0), bf16),
        ((length, 3 * width), (length, 384), lambda i: (0, first + i), bf16),
    ]
    if start:
        outs += [
            ((length, width), (length, width), lambda i: (0, 0), bf16),
            ((width, length), (width, length), lambda i: (0, 0), bf16),
            ((72, 128), (72, 128), lambda i: (0, 0), f32),
        ]
    given = [place.spot, doc, x] + ([] if packed else [vec]) + weights.arrays
    aliases = {}
    if not start:
        aliases = {len(given) + i: i for i in range(3)}
        given += before
    return pl.pallas_call(
        kernel,
        grid=(count,),
        in_specs=[pl.BlockSpec(memory_space=pltpu.SMEM), full((length, 1)), full(x.shape)]
        + [full((72, 128))] * n_v
        + [anyplace] * (n_p + n_a),
        out_specs=[pl.BlockSpec(block, index) for _, block, index, _ in outs],
        out_shape=[jax.ShapeDtypeStruct(shape, kind) for shape, _, _, kind in outs],
        scratch_shapes=[
            pltpu.VMEM((weights.rows, weights.width), bf16),
            pltpu.SemaphoreType.DMA((n_p,)),
        ],
        input_output_aliases=aliases,
        compiler_params=pltpu.CompilerParams(vmem_limit_bytes=VMEM),
        cost_estimate=TINY,
        name="attend",
    )(*given)


def lay_blocks(ref, place_ref, other, rows):
    out = []
    core = 1 - place_ref[0] if other else place_ref[0]
    for x in range(2):
        for y in range(2):
            at = pl.multiple_of((4 * x + 2 * core + y) * rows, 16)
            out.append(ref[pl.ds(at, rows), :])
    return jnp.concatenate(out, axis=0)


def attend_back_kernel(
    place_ref,
    q_ref,
    k_ref,
    v_ref,
    o_ref,
    do_ref,
    p_ref,
    h1_t_ref,
    *refs,
    length,
):
    out_ref, send_ref, keep_ref, dk_acc, dv_acc = refs[-5:]
    lane = lax.broadcasted_iota(jnp.int32, (length, 128), 1)
    low = lane < HD
    spot = lane & (HD - 1)
    q = q_ref[...].astype(f32) * HD ** (-0.5)
    do = do_ref[...].astype(f32)
    v = v_ref[...].astype(f32)
    product = do * o_ref[...].astype(f32)
    k_t = k_ref[...].T
    sides = []
    for h in range(2):
        mine = low if h == 0 else jnp.logical_not(low)
        center = jnp.sum(jnp.where(mine, product, 0.0), axis=1, keepdims=True)
        first = center.astype(bf16).astype(f32)
        second = (center - first).astype(bf16).astype(f32)
        third = center - first - second
        extra = jnp.where(
            spot == 0, -first, jnp.where(spot == 1, -second, jnp.where(spot == 2, -third, 0.0))
        )
        sides.append(
            (
                jnp.where(mine, do, extra).astype(bf16),
                jnp.where(mine, v, jnp.where(spot < 3, 1.0, 0.0)).astype(bf16),
                jnp.where(mine, do, 0.0).astype(bf16),
                jnp.where(mine, q, 0.0).astype(bf16),
            )
        )
    dk_acc[...] = jnp.zeros_like(dk_acc)
    dv_acc[...] = jnp.zeros_like(dv_acc)
    at = 0
    for b, (lo, hi) in enumerate(spans(length)):
        n = hi - lo
        here = slice(b * QB, (b + 1) * QB)
        dqs = []
        dk = dv = None
        for h in range(2):
            do_more, v_more, do_own, q_own = sides[h]
            p = p_ref[h, at : at + n, :]
            dp = dot(v_more[lo:hi], do_more[here], ((1,), (1,)))
            ds = (p.astype(f32) * dp).astype(bf16)
            dv_part = dot(p, do_own[here])
            dk_part = dot(ds, q_own[here])
            dv = dv_part if dv is None else dv + dv_part
            dk = dk_part if dk is None else dk + dk_part
            dqs.append(dot(k_t[h * HD : (h + 1) * HD, lo:hi], ds))
        dv_acc[lo:hi, :] += dv
        dk_acc[lo:hi, :] += dk
        out_ref[here, :128] = (jnp.concatenate(dqs, axis=0) * HD ** (-0.5)).T.astype(bf16)
        at += n
    out_ref[:, 128:256] = dk_acc[...].astype(bf16)
    out_ref[:, 256:] = dv_acc[...].astype(bf16)
    parts = out_ref[...]
    for other, ref in ((True, send_ref), (False, keep_ref)):
        rows = h1_t_ref.shape[0] // 8
        ref[...] = dot(lay_blocks(h1_t_ref, place_ref, other, rows), parts).astype(bf16)


def attend_back(place, qkv, mixed, grad_mixed, soft, h1_t, first, count, before):
    length, width = mixed.shape
    rows = soft_rows(length)
    col = lambda off: pl.BlockSpec((length, 128), lambda i: (0, 3 * (first + i) + off))
    pair = pl.BlockSpec((length, 128), lambda i: (0, first + i))
    terms = pl.BlockSpec((width // 2, 384), lambda i: (0, i))
    term = jax.ShapeDtypeStruct((width // 2, 384 * count), bf16)
    given = [place.spot, qkv, qkv, qkv, mixed, grad_mixed, soft, h1_t]
    aliases = {}
    if before is not None:
        aliases = {len(given): 0}
        given.append(before)
    return pl.pallas_call(
        functools.partial(attend_back_kernel, length=length),
        grid=(count,),
        in_specs=[
            pl.BlockSpec(memory_space=pltpu.SMEM),
            col(0),
            col(1),
            col(2),
            pair,
            pair,
            pl.BlockSpec((2, rows, QB), lambda i: (first + i, 0, 0)),
            pl.BlockSpec(h1_t.shape, lambda i: (0, 0)),
        ]
        + [pl.BlockSpec(memory_space=pl.ANY)] * len(aliases),
        out_specs=[pl.BlockSpec((length, 384), lambda i: (0, first + i)), terms, terms],
        out_shape=[jax.ShapeDtypeStruct(qkv.shape, bf16), term, term],
        scratch_shapes=[pltpu.VMEM((length, 128), f32)] * 2,
        input_output_aliases=aliases,
        compiler_params=pltpu.CompilerParams(vmem_limit_bytes=VMEM),
        cost_estimate=TINY,
        name="attend_back",
    )(*given)


def proj_terms(place, g_t, dout):
    hidden, length = g_t.shape
    width = dout.shape[1]
    rows = hidden // 4

    def kernel(place_ref, g_ref, dout_ref, send_ref, keep_ref):
        value = dot(g_ref[...], dout_ref[...]).astype(bf16)

        @pl.when(pl.program_id(0) < 2)
        def _():
            send_ref[...] = value

        @pl.when(pl.program_id(0) >= 2)
        def _():
            keep_ref[...] = value

    def block(i, place_ref):
        core = jnp.where(i < 2, 1 - place_ref[0], place_ref[0])
        return 2 * (i % 2) + core, 0

    out = jax.ShapeDtypeStruct((hidden // 2, width), bf16)
    return pl.pallas_call(
        kernel,
        grid_spec=pltpu.PrefetchScalarGridSpec(
            num_scalar_prefetch=1,
            grid=(4,),
            in_specs=[
                pl.BlockSpec((rows, length), block),
                pl.BlockSpec((length, width), lambda i, p: (0, 0)),
            ],
            out_specs=[
                pl.BlockSpec((rows, width), lambda i, p: (jnp.minimum(i, 1), 0)),
                pl.BlockSpec((rows, width), lambda i, p: (jnp.maximum(i - 2, 0), 0)),
            ],
        ),
        out_shape=[out, out],
        compiler_params=pltpu.CompilerParams(vmem_limit_bytes=VMEM),
        cost_estimate=TINY,
        name="proj_terms",
    )(place.spot, g_t, dout)


def back_middle(place, dout, slope, y1, mixed, h2_t, vec, w_out, w_fc, w_proj):
    length, width = dout.shape
    hidden = w_fc.width
    step_rows, part = 256, PART
    steps = length // step_rows
    f_steps, rows = hidden // width, width // 8
    weights = (w_out, w_fc, w_proj)
    counts = [len(w.arrays) for w in weights]

    def kernel(*refs):
        refs = list(refs)
        take = lambda n: [refs.pop(0) for _ in range(n)]
        place_ref, dout_ref, slope_ref, y1_ref, mixed_ref, h2_t, vec_ref = take(7)
        pieces = [take(n) for n in counts]
        dmixed_ref, dy1_ref, send_ref, keep_ref = take(4)
        gain_ref, shift_ref, outb_ref, fcb_ref, projb_ref = sums = take(5)
        wo, wf, wp = buffers = take(3)
        sems = take(3)
        du_all, mixed_t, db1_all = take(3)
        i = pl.program_id(0)

        @pl.when(i == 0)
        def _():
            for w, own, buffer, sem in zip(weights, pieces, buffers, sems):
                w.load(place_ref, own, buffer, sem)
            for ref in sums:
                ref[...] = jnp.zeros_like(ref)

        @pl.when(i < steps)
        def _():
            here = pl.ds(pl.multiple_of(i * step_rows, step_rows), step_rows)
            dout = dout_ref[...]
            mixed_t[:, here] = mixed_ref[...].T
            dh2 = jnp.zeros((step_rows, width), f32)
            for c in range(0, hidden, part):
                cols = slice(c, c + part)
                du = dot(dout, wp[cols, :], ((1,), (1,))) * slope_ref[:, cols].astype(f32)
                du = du.astype(bf16)
                du_all[here, cols] = du
                fcb_ref[:, cols] += jnp.sum(du.astype(f32), axis=0, keepdims=True)
                dh2 = dh2 + dot(du, wf[:, cols], ((1,), (1,)))
            back, gain, shift = norm_back(y1_ref[...], row_of(vec_ref, GAIN2), dh2)
            wide_dout = dout.astype(f32)
            dy1 = wide_dout + back
            db1 = dy1.astype(bf16)
            dy1_ref[...] = dy1
            db1_all[here, :] = db1
            dmixed_ref[...] = dot(db1, wo[...], ((1,), (1,))).astype(bf16)
            gain_ref[...] += gain
            shift_ref[...] += shift
            outb_ref[...] += jnp.sum(db1.astype(f32), axis=0, keepdims=True)
            projb_ref[...] += jnp.sum(wide_dout, axis=0, keepdims=True)

        j = i - steps

        @pl.when((j >= 0) & (j < f_steps))
        def _():
            cols = pl.ds(pl.multiple_of(j * width, 128), width)
            for other, ref in ((True, send_ref), (False, keep_ref)):
                value = dot(lay_blocks(h2_t, place_ref, other, rows), du_all[:, cols])
                ref[...] = value.astype(bf16).reshape(ref.shape)

        @pl.when(j == f_steps)
        def _():
            for other, ref in ((True, send_ref), (False, keep_ref)):
                value = dot(lay_blocks(mixed_t, place_ref, other, rows), db1_all[...])
                ref[...] = value.astype(bf16).reshape(ref.shape)

    full = lambda shape: pl.BlockSpec(shape, lambda i: (0,) * len(shape))
    slab = lambda n: pl.BlockSpec((step_rows, n), lambda i: (jnp.minimum(i, steps - 1), 0))
    terms = pl.BlockSpec(
        (4, rows, width), lambda i: (0, jnp.clip(i - steps, 0, f_steps), 0)
    )
    like = jax.ShapeDtypeStruct
    one = (1, width)
    sum_shapes = [one, one, one, (1, hidden), one]
    return pl.pallas_call(
        kernel,
        grid=(steps + f_steps + 1,),
        in_specs=[
            pl.BlockSpec(memory_space=pltpu.SMEM),
            slab(width),
            slab(hidden),
            slab(width),
            slab(width),
            full(h2_t.shape),
            full((72, 128)),
        ]
        + [pl.BlockSpec(memory_space=pl.ANY)] * sum(counts),
        out_specs=[slab(width), slab(width), terms, terms] + [full(v) for v in sum_shapes],
        out_shape=[
            like((length, width), bf16),
            like((length, width), f32),
            like((4, rows * (f_steps + 1), width), bf16),
            like((4, rows * (f_steps + 1), width), bf16),
        ]
        + [like(v, f32) for v in sum_shapes],
        scratch_shapes=[pltpu.VMEM((w.rows, w.width), bf16) for w in weights]
        + [pltpu.SemaphoreType.DMA((n,)) for n in counts]
        + [
            pltpu.VMEM((length, hidden), bf16),
            pltpu.VMEM((width, length), bf16),
            pltpu.VMEM((length, width), bf16),
        ],
        compiler_params=pltpu.CompilerParams(vmem_limit_bytes=VMEM),
        cost_estimate=TINY,
        name="back_middle",
    )(place.spot, dout, slope, y1, mixed, h2_t, vec, *[v for w in weights for v in w.arrays])


class Place:
    def __init__(self, owner, wide, narrow, plain):
        self.wide, self.narrow = wide, narrow
        self.deep = wide // 4
        mine = lax.axis_index("wide")
        self.core, self.y, self.z = mine & 1, (mine >> 1) & 1, mine >> 2
        self.o_core, self.o_y, self.o_z = owner & 1, (owner >> 1) & 1, owner >> 2
        self.x = lax.axis_index("narrow")
        self.holder = mine == owner
        spot = jnp.stack([self.core, self.x, self.y, self.holder]).astype(jnp.int32)
        self.spot = jnp.zeros_like(spot) if plain else spot

    def swap(self, value, flip):
        return lax.ppermute(value, "wide", [(i, i ^ flip) for i in range(self.wide)])

    def cross(self, value, flip):
        pairs = [(2 * i + j, 2 * (i ^ flip) + 1 - j) for i in range(self.wide) for j in range(2)]
        return lax.ppermute(value, AXES, pairs)

    def shift(self, value, pairs):
        places = [(4 * a + low, 4 * b + low) for a, b in pairs for low in range(4)]
        return lax.ppermute(value, "wide", places)

    def z_pairs(self):
        last = self.deep - 1
        return [((i, i + 1), (last - i, last - i - 1)) for i in range(self.deep // 2 - 1)]

    def deal(self, value, kind):
        if kind == "plane":
            groups = [
                [2 * (4 * z + 2 * y + core) + x for x in range(2) for y in range(2)]
                for z in range(self.deep)
                for core in range(2)
            ]
            return lax.all_to_all(
                value, AXES, 0, 0, axis_index_groups=groups, tiled=True
            )
        groups = [
            [4 * z + 2 * y + core for y in range(2) for z in range(self.deep)]
            for core in range(2)
        ]
        return lax.all_to_all(value, "wide", 0, 0, axis_index_groups=groups, tiled=True)

    def z_flips(self):
        step = self.deep // 2
        while step:
            yield step
            step //= 2


def pick(parts, index):
    return lax.dynamic_index_in_dim(parts, index, axis=0, keepdims=False)


def ordered(mine, other, index):
    first = index == 0
    return jnp.stack([jnp.where(first, mine, other), jnp.where(first, other, mine)])


def spread_plain(place, shard):
    now = jnp.where(place.core == place.o_core, shard, place.swap(shard, 1))
    now = jnp.where(place.y == place.o_y, now, place.swap(now, 2))
    for step in place.z_flips():
        other = place.swap(now, 4 * step)
        now = jnp.where((place.z & step) == (place.o_z & step), now, other)
    return lax.all_gather(now, "narrow", axis=0, tiled=True)


def spread_steps(place, shard):
    if isinstance(shard, tuple):
        keep, send = shard
    else:
        halves = shard.reshape(2, shard.shape[0] // 2, shard.shape[1])
        keep, send = pick(halves, place.core), pick(halves, 1 - place.core)
    rows, width = 2 * keep.shape[0], keep.shape[1]
    (other,) = yield [(send, 1)]
    now = jnp.where(place.core == place.o_core, keep, other)
    halves = now.reshape(2, rows // 4, width)
    (other,) = yield [(pick(halves, 1 - place.y), 2)]
    now = jnp.where(place.y == place.o_y, pick(halves, place.y), other)
    for step in place.z_flips():
        (other,) = yield [(now, 4 * step)]
        now = jnp.where((place.z & step) == (place.o_z & step), now, other)
    by_y, by_x = yield [(now, 2), (now, 0)]
    cut = rows // 8
    far_a, far_b = yield [(by_y[:cut], 0), (by_x[cut:], 2)]
    mine = [
        (now, (0, 0, 0), 0),
        (by_y, (0, 0, 1), 0),
        (by_x, (0, 1, 0), 0),
        (far_a, (0, 1, 1), 0),
        (far_b, (0, 1, 1), cut),
    ]
    theirs = yield [(piece, 1) for piece, _, _ in mine]
    return Pieces(
        mine + [(got, (1, x, y), row) for got, (_, (_, x, y), row) in zip(theirs, mine)]
    )


class Pieces:
    def __init__(self, found):
        self.arrays = [piece for piece, _, _ in found]
        self.spots = [(flips, row) for _, flips, row in found]
        self.block, self.width = self.arrays[0].shape
        self.rows = self.block if len(found) == 1 else 8 * self.block

    def over(self, arrays):
        return Pieces([(v, flips, row) for v, (flips, row) in zip(arrays, self.spots)])

    def load(self, place_ref, refs, buffer, sem):
        copies = []
        for ref, ((core, x, y), row) in zip(refs, self.spots):
            start = 0
            if len(refs) > 1:
                at = 4 * (place_ref[1] ^ x) + 2 * (place_ref[0] ^ core) + (place_ref[2] ^ y)
                start = pl.multiple_of(at * self.block + row, 16)
            target = buffer.at[pl.ds(start, ref.shape[0]), :]
            copies.append(pltpu.make_async_copy(ref, target, sem.at[len(copies)]))
        for copy in copies:
            copy.start()
        for copy in copies:
            copy.wait()


ROWS = 256
PART = 1024


def by_rows(name, body, place, blocks, wholes, weights, out_blocks, out_sums):
    length = blocks[0].shape[0]
    n_b, n_w, n_o, n_s = len(blocks), len(wholes), len(out_blocks), len(out_sums)
    counts = [len(w.arrays) for w in weights]

    def kernel(*refs):
        refs = list(refs)
        take = lambda n: [refs.pop(0) for _ in range(n)]
        (place_ref,) = take(1)
        block_refs, whole_refs = take(n_b), take(n_w)
        piece_refs = [take(n) for n in counts]
        out_refs, sum_refs = take(n_o), take(n_s)
        buffers, sems = take(len(weights)), take(len(weights))

        @pl.when(pl.program_id(0) == 0)
        def _():
            for w, pieces, buffer, sem in zip(weights, piece_refs, buffers, sems):
                w.load(place_ref, pieces, buffer, sem)
            for ref in sum_refs:
                ref[...] = jnp.zeros_like(ref)

        body(block_refs, whole_refs, buffers, out_refs, sum_refs)

    full = lambda shape: pl.BlockSpec(shape, lambda i: (0,) * len(shape))
    slab = lambda shape: (
        pl.BlockSpec((ROWS, shape[1]), lambda i: (i, 0))
        if shape[0] == length
        else pl.BlockSpec((shape[0], ROWS), lambda i: (0, i))
    )
    return pl.pallas_call(
        kernel,
        grid=(length // ROWS,),
        in_specs=[pl.BlockSpec(memory_space=pltpu.SMEM)]
        + [slab(v.shape) for v in blocks]
        + [full(v.shape) for v in wholes]
        + [pl.BlockSpec(memory_space=pl.ANY)] * sum(counts),
        out_specs=[slab(shape) for shape, _ in out_blocks] + [full(s) for s in out_sums],
        out_shape=[jax.ShapeDtypeStruct(shape, kind) for shape, kind in out_blocks]
        + [jax.ShapeDtypeStruct(shape, f32) for shape in out_sums],
        scratch_shapes=[pltpu.VMEM((w.rows, w.width), bf16) for w in weights]
        + [pltpu.SemaphoreType.DMA((n,)) for n in counts],
        compiler_params=pltpu.CompilerParams(vmem_limit_bytes=VMEM),
        cost_estimate=TINY,
        name=name,
    )(place.spot, *blocks, *wholes, *[v for w in weights for v in w.arrays])


def tie(groups):
    flat, tree = jax.tree.flatten(groups)
    return jax.tree.unflatten(tree, lax.optimization_barrier(flat))


class Steps:
    def __init__(self, place):
        self.place = place
        self.asked, self.flips, self.chains, self.done, self.going = {}, {}, {}, {}, {}

    def ask(self, name, pairs):
        self.asked[name] = [value for value, _ in pairs]
        self.flips[name] = [flip for _, flip in pairs]

    def add(self, name, chain):
        self.chains[name] = chain
        self.ask(name, next(chain))

    def exchange(self, value, flip):
        if isinstance(flip, tuple):
            return self.place.shift(value, flip)
        if isinstance(flip, str):
            return self.place.deal(value, flip)
        if flip <= 0:
            return self.place.cross(value, -flip)
        return self.place.swap(value, flip)

    def slot(self, names="", hold="", work=None, given=(), strict=False):
        names = list(self.asked) if names == "all" else names.replace(",", " ").split()
        hold = hold.split()
        assert not set(names) & set(self.going)
        asked = {name: self.asked[name] for name in names if name in self.asked}
        if strict:
            asked = tie(asked)
        for name, values in asked.items():
            self.going[name] = [
                self.exchange(value, flip) for value, flip in zip(values, self.flips[name])
            ]
        held = tie({"asked": asked, "given": given})
        result = work(*held["given"]) if work else ()
        ready = {name: got for name, got in self.going.items() if name not in hold}
        ready, result, self.asked = tie((ready, result, self.asked))
        for name, got in ready.items():
            del self.going[name], self.asked[name]
            try:
                self.ask(name, self.chains[name].send(got))
            except StopIteration as stop:
                self.done[name] = stop.value
        return result


def collect_plain(place, keep, send):
    width = keep.shape[-1]
    parts = [v.reshape(2, 1, 2, -1, width) for v in (keep, send)]
    terms = jnp.concatenate(parts, axis=1).reshape(-1, width)
    now = lax.psum_scatter(terms, "narrow", scatter_dimension=0, tiled=True)
    return lax.psum(now, "wide")


def add(*values):
    return functools.reduce(lambda a, b: a + b, [v.astype(f32) for v in values]).astype(bf16)


def collect_steps(place, keep, send, plane, line):
    width = keep.shape[-1]
    (other,) = yield [(send, 1)]
    if plane == "deal":
        (got,) = yield [(add(keep, other).reshape(-1, width), "plane")]
        now = add(*got.reshape(4, -1, width))
    else:
        terms = [v.reshape(2, 2, -1, width) for v in (keep, other)]
        at_x = lambda v, i: pick(v, place.x ^ i)
        at_y = lambda v, i: lax.dynamic_index_in_dim(v, place.y ^ i, axis=1, keepdims=False)
        if plane == "turn":
            (other,) = yield [(add(*[at_x(v, 1) for v in terms]), 0)]
            terms = [at_x(v, 0) for v in terms] + [other]
            part = lambda i: add(*[pick(v, place.y ^ i) for v in terms])
            (other,) = yield [(part(1), 2)]
            now = add(part(0), other)
        else:
            cut = terms[0].shape[2] // 2
            upper = [v[:, :, :cut] for v in terms]
            lower = [v[:, :, cut:] for v in terms]
            by_x, by_y = yield [
                (add(*[at_x(v, 1) for v in upper]), 0),
                (add(*[at_y(v, 1) for v in lower]), 2),
            ]
            upper = [at_x(v, 0) for v in upper] + [by_x]
            lower = [at_y(v, 0) for v in lower] + [by_y]
            top = lambda i: add(*[pick(v, place.y ^ i) for v in upper])
            low = lambda i: add(*[pick(v, place.x ^ i) for v in lower])
            by_y, by_x = yield [(top(1), 2), (low(1), 0)]
            now = jnp.concatenate([add(top(0), by_y), add(low(0), by_x)], axis=0)
    if line:
        inward = place.z_pairs()
        for pairs in inward:
            (other,) = yield [(now, pairs)]
            now = add(now, other)
        half = place.deep // 2
        (other,) = yield [(now, ((half - 1, half), (half, half - 1)))]
        now = add(now, other)
        for pairs in reversed(inward):
            (other,) = yield [(now, tuple((b, a) for a, b in pairs))]
            got = (place.z == pairs[0][0]) | (place.z == pairs[1][0])
            now = jnp.where(got, other, now)
    else:
        for step in reversed(list(place.z_flips())):
            (other,) = yield [(now, 4 * step)]
            now = add(now, other)
    (other,) = yield [(now, 2)]
    far, far_other = yield [(now, 1), (other, 1)]
    return [now, other, far, far_other]


def put_kernel(place_ref, *refs, counts, bodies):
    refs = list(refs)
    take = lambda n: [refs.pop(0) for _ in range(n)]
    pieces = [take(4) for _ in range(counts[0])]
    outs = take(counts[1])
    buffers, sem = take(counts[0]), refs[0]
    copies = []
    for group, buffer in zip(pieces, buffers):
        for i, ref in enumerate(group):
            rows = ref.shape[0]
            at = 2 * (place_ref[0] ^ (i // 2)) + (place_ref[2] ^ (i % 2))
            target = buffer.at[pl.ds(pl.multiple_of(at * rows, 16), rows), :]
            copies.append(pltpu.make_async_copy(ref, target, sem.at[len(copies)]))
    for copy in copies:
        copy.start()
    for copy in copies:
        copy.wait()
    holder = place_ref[3] == 1
    bodies(buffers, outs, lambda v: jnp.where(holder, v.astype(f32), 0.0))


def put(place, groups, bodies, shapes, name):
    flat = [v for group in groups for v in group]
    return pl.pallas_call(
        functools.partial(put_kernel, counts=(len(groups), len(shapes)), bodies=bodies),
        in_specs=[pl.BlockSpec(memory_space=pltpu.SMEM)]
        + [pl.BlockSpec(memory_space=pl.ANY)] * len(flat),
        out_specs=[pl.BlockSpec(memory_space=pltpu.VMEM)] * len(shapes),
        out_shape=[jax.ShapeDtypeStruct(v, f32) for v in shapes],
        scratch_shapes=[
            pltpu.VMEM((4 * group[0].shape[0], group[0].shape[1]), bf16) for group in groups
        ]
        + [pltpu.SemaphoreType.DMA((len(flat),))],
        compiler_params=pltpu.CompilerParams(vmem_limit_bytes=VMEM),
        cost_estimate=TINY,
        name=name,
    )(place.spot, *flat)


def put_rows(buffers, outs, mask):
    outs[0][...] = mask(buffers[0][...])


def put_wide(buffers, outs, mask):
    wide, narrow = outs
    rows = narrow.shape[0] // 4
    width = narrow.shape[1]
    blocks = wide.shape[1] // width
    for quarter in range(4):
        here = slice(quarter * rows, (quarter + 1) * rows)
        for i in range(blocks + 1):
            start = (quarter * (blocks + 1) + i) * rows
            value = mask(buffers[0][start : start + rows, :])
            if i < blocks:
                wide[here, i * width : (i + 1) * width] = value
            else:
                narrow[here, :] = value


def put_pairs(buffers, outs, mask):
    width = outs[0].shape[1] // 3
    for part, buffer in enumerate(buffers):
        pairs = buffer.shape[1] // 384
        for p in range(pairs):
            for j in range(3):
                at = j * width + (part * pairs + p) * 128
                source = (3 * p + j) * 128
                outs[0][:, at : at + 128] = mask(buffer[:, source : source + 128])


def unpack_vectors(now, sizes):
    now = now.reshape(1, -1)
    out, at = [], 0
    for size in sizes:
        out.append(now[:, at : at + size])
        at += size
    return out


def shares(vectors, narrow):
    out = []
    for i in range(narrow):
        for v in vectors:
            size = v.shape[1] // narrow
            out.append(v[:, i * size : (i + 1) * size])
    return jnp.concatenate(out, axis=1)


def collect_vectors_steps(place, now):
    (other,) = yield [(now, 1)]
    now = now + other
    (other,) = yield [(pick(now, 1 - place.x), 0)]
    now = pick(now, place.x) + other
    (other,) = yield [(now, 2)]
    now = now + other
    for step in place.z_flips():
        (other,) = yield [(now, 4 * step)]
        now = now + other
    return now


def collect_vectors_plain(place, vectors):
    now = shares(vectors, place.narrow).reshape(place.narrow, -1)
    now = lax.psum_scatter(now, "narrow", scatter_dimension=0, tiled=False)
    return lax.psum(now, "wide")


def norm_rows(values, gain, shift):
    center = values - jnp.mean(values, axis=-1, keepdims=True)
    spread_of = jnp.mean(center * center, axis=-1, keepdims=True)
    return center * lax.rsqrt(spread_of + epsilon) * gain + shift


def norm_back(values, gain, grad):
    center = values - jnp.mean(values, axis=-1, keepdims=True)
    inverse = lax.rsqrt(jnp.mean(center * center, axis=-1, keepdims=True) + epsilon)
    hat = center * inverse
    scaled = grad * gain
    inner = jnp.mean(scaled * hat, axis=-1, keepdims=True)
    back = inverse * (scaled - jnp.mean(scaled, axis=-1, keepdims=True) - hat * inner)
    return (
        back,
        jnp.sum(grad * hat, axis=0, keepdims=True),
        jnp.sum(grad, axis=0, keepdims=True),
    )


def gelu_both(u):
    c = math.sqrt(2.0 / math.pi)
    square = u * u
    half = 0.5 + 0.5 * jnp.tanh(u * (c + c * 0.044715 * square))
    g = u * half
    return g, half + g * (1.0 - half) * (2 * c + 6 * c * 0.044715 * square)


def dot(a, b, dims=((1,), (0,))):
    return lax.dot_general(a, b, (dims, ((), ())), preferred_element_type=f32)


GAIN1, SHIFT1, QV, OUTB = (0, 6), (6, 6), (12, 12), (24, 6)
GAIN2, SHIFT2, FCB, PROJB = (30, 6), (36, 6), (42, 24), (66, 6)


def row_of(vec, spot, first=0, count=None):
    start = spot[0] + first
    count = spot[1] if count is None else count
    return jnp.concatenate([vec[start + i : start + i + 1, :] for i in range(count)], axis=1)


def unpack_rows(w):
    shard = w.shape[0] // 2
    near = w[:64, w.shape[1] - 128 :].astype(f32)
    far = w[shard : shard + 64, w.shape[1] - 128 :].astype(f32)
    parts = []
    for start, count in (GAIN1, SHIFT1, QV, OUTB, GAIN2, SHIFT2, FCB, PROJB):
        rows = slice(start // 2, (start + count) // 2)
        parts += [near[rows], far[rows]]
    return jnp.concatenate(parts, axis=0)


def pack_kernel(core_ref, w_ref, *refs):
    vectors, outs, rows_ref = refs[:-5], refs[-5:-1], refs[-1]
    half, width = w_ref.shape[0] // 2, w_ref.shape[1] // 3
    rows_ref[...] = jnp.zeros_like(rows_ref)
    at = 0
    for ref in vectors:
        value = ref[...].astype(f32)
        for i in range(value.shape[1] // 128):
            rows_ref[at : at + 1, :] = value[:, i * 128 : (i + 1) * 128]
            at += 1
    pairs = width // 128
    for other in range(2):
        core = 1 - core_ref[0] if other else core_ref[0]
        w = w_ref[pl.ds(pl.multiple_of(core * half, 16), half), :]
        for part in range(2):
            ref = outs[2 * part + other]
            for p in range(pairs // 2):
                for j in range(3):
                    source = j * width + (part * (pairs // 2) + p) * 128
                    to = (3 * p + j) * 128
                    ref[:, to : to + 128] = w[:, source : source + 128]
            if part == 0:
                block = rows_ref[...].astype(bf16)
                ref[:, 3 * width // 2 :] = jnp.concatenate([block, block], axis=0)


def pack(place, w, vectors):
    rows, width = w.shape
    side = width // 2
    shape = lambda more: jax.ShapeDtypeStruct((rows // 2, side + more), bf16)
    vmem = pl.BlockSpec(memory_space=pltpu.VMEM)
    near, near_send, far, far_send = pl.pallas_call(
        pack_kernel,
        in_specs=[pl.BlockSpec(memory_space=pltpu.SMEM)] + [vmem] * (1 + len(vectors)),
        out_specs=[vmem] * 4,
        out_shape=[shape(128), shape(128), shape(0), shape(0)],
        scratch_shapes=[pltpu.VMEM((rows // 4, 128), f32)],
        compiler_params=pltpu.CompilerParams(vmem_limit_bytes=VMEM),
        cost_estimate=TINY,
        name="pack",
    )(place.spot, w, *vectors)
    return (near, near_send), (far, far_send)


def widen_body(blocks, wholes, weights, outs, sums):
    (x_ref, mixed_ref), (vec,), (w_out, w_fc) = blocks, wholes, weights
    y1_ref, slope_ref, h2_t_ref, g_t_ref = outs
    y1 = x_ref[...].astype(f32) + dot(mixed_ref[...], w_out[...]) + row_of(vec, OUTB)
    y1_ref[...] = y1
    h2 = norm_rows(y1, row_of(vec, GAIN2), row_of(vec, SHIFT2)).astype(bf16)
    h2_t_ref[...] = h2.T
    for at in range(0, w_fc.shape[1], PART):
        here = slice(at, at + PART)
        g, slope = gelu_both(dot(h2, w_fc[:, here]) + row_of(vec, FCB, at // 128, PART // 128))
        g_t_ref[here, :] = g.astype(bf16).T
        slope_ref[:, here] = slope.astype(bf16)


def finish_body(blocks, wholes, weights, outs, sums):
    (y1_ref, g_t_ref), (vec,), (w,) = blocks, wholes, weights
    result = y1_ref[...] + dot(g_t_ref[...], w[...], ((0,), (0,))) + row_of(vec, PROJB)
    outs[0][...] = result.astype(bf16)


def back_first_body(blocks, wholes, weights, outs, sums):
    (dqkv_ref, x_ref, dy1_ref), (vec, *more), (w_a, w_b) = blocks, wholes, weights
    side = w_b.shape[1]
    dqkv = dqkv_ref[...]
    dh1 = dot(dqkv[:, :side], w_a[:, :side], ((1,), (1,)))
    dh1 = dh1 + dot(dqkv[:, side:], w_b[...], ((1,), (1,)))
    back, gain, shift = norm_back(x_ref[...].astype(f32), row_of(vec, GAIN1), dh1)
    outs[0][...] = (dy1_ref[...] + back).astype(bf16)
    total = jnp.sum(dqkv.astype(f32), axis=0, keepdims=True)
    parts = [total[:, p * 384 + j : p * 384 + j + 128] for j in (0, 256) for p in range(H // 2)]
    for ref, value in zip(sums, (gain, shift, jnp.concatenate(parts, axis=1))):
        ref[...] += value

    @pl.when(pl.program_id(0) == pl.num_programs(0) - 1)
    def _():
        found = sums[:3] + more
        at = 0
        for half in range(2):
            for ref in found:
                count = ref.shape[1] // 256
                for i in range(count):
                    start = (half * count + i) * 128
                    sums[3][at : at + 1, :] = ref[:, start : start + 128]
                    at += 1


def on_device(
    wide,
    narrow,
    tokens,
    doc_ids,
    cotangent,
    owner,
    ln1_gain,
    ln1_bias,
    qkv_weight,
    qv_bias,
    out_weight,
    out_bias,
    ln2_gain,
    ln2_bias,
    fc_weight,
    fc_bias,
    proj_weight,
    proj_bias,
):
    _, length, width = tokens.shape
    plain = narrow != 2 or ln1_gain.shape[1] % 128 != 0
    place = Place(owner[0], wide, narrow, plain)
    x = tokens[0]
    dout = cotangent[0]
    doc = doc_ids[0][:, None]
    pairs = H // 2
    half = pairs // 2

    def begin(name, shard):
        if plain:
            steps.done[name] = Pieces([(spread_plain(place, shard), (0, 0, 0), 0)])
        else:
            steps.add(name, spread_steps(place, shard))

    def end(name, keep, send, plane, line):
        if plain:
            steps.done[name] = collect_plain(place, keep, send)
        else:
            steps.add(name, collect_steps(place, keep, send, plane, line))

    steps = Steps(place)
    vectors = (ln1_gain, ln1_bias, qv_bias, out_bias, ln2_gain, ln2_bias, fc_bias, proj_bias)
    sizes = [v.shape[1] for v in vectors]
    vec = None
    if plain:
        rows = spread_plain(place, jnp.concatenate(vectors, axis=1))
        parts, at = [], 0
        for size in sizes:
            parts.append(rows[:, at : at + size].reshape(-1))
            at += size
        vec = jnp.concatenate(parts).reshape(-1, 128).astype(f32)
        order = [
            qkv_weight[0][:, j * width + p * 128 : j * width + (p + 1) * 128]
            for p in range(pairs)
            for j in range(3)
        ]
        near = jnp.concatenate(order[: 3 * half], axis=1)
        far = jnp.concatenate(order[3 * half :], axis=1)
    else:
        near, far = pack(place, qkv_weight[0], vectors)
    begin("qa", near)
    begin("qb", far)
    begin("o", out_weight[0])
    begin("f", fc_weight[0])
    begin("p", proj_weight[0])

    def attention(x, vec, name, column, first, count, before):
        weights = steps.done[name]

        def run(x, vec, arrays, before):
            return attend(place, doc, x, vec, weights.over(arrays), column, first, count, before)

        return dict(work=run, given=(x, vec, weights.arrays, before))

    def rows_work(name, body, blocks, wholes, weights, out_blocks, out_sums):
        def run(blocks, wholes, arrays):
            held = [w.over(own) for w, own in zip(weights, arrays)]
            return by_rows(name, body, place, blocks, wholes, held, out_blocks, out_sums)

        return dict(work=run, given=(blocks, wholes, [w.arrays for w in weights]))

    steps.slot("qa qb", strict=True)
    steps.slot("qa", strict=True)
    steps.slot("qa,qb,o,f,p", strict=True)
    steps.slot("qa qb o f", hold="qb f", strict=True)
    steps.slot("qa", hold="f", strict=True)
    steps.slot("qa qb o", strict=True)
    steps.slot("qa qb f p", hold="f p", strict=True)
    state = steps.slot("qb o", **attention(x, vec, "qa", 0, 0, 2, None))
    state, (h1, h1_t, vec) = list(state[:3]), state[3:]
    state = steps.slot(
        "qb o f p", hold="p", **attention(h1, vec, "qa", 768, 2, 1, state)
    )
    state = steps.slot("o f", hold="", **attention(h1, vec, "qb", 0, 3, 2, list(state)))
    state = steps.slot("f o p", **attention(h1, vec, "qb", 768, 5, 1, list(state)))
    mixed, soft, qkv = state
    steps.slot("f p", hold="p")
    w_a, w_b, w_out, w_fc = [steps.done[name] for name in ("qa", "qb", "o", "f")]
    hidden = w_fc.width
    y1, slope, h2_t, g_t = steps.slot(
        "",
        **rows_work(
            "widen",
            widen_body,
            [x, mixed],
            [vec],
            [w_out, w_fc],
            [
                ((length, width), f32),
                ((length, hidden), bf16),
                ((width, length), bf16),
                ((hidden, length), bf16),
            ],
            [],
        ),
    )
    p_send, p_keep = steps.slot(
        "p", work=lambda g_t, dout: proj_terms(place, g_t, dout), given=(g_t, dout)
    )
    end("dp", p_keep, p_send, "deal", True)
    steps.slot("p dp")
    w_proj = steps.done["p"]

    def run(dout, slope, y1, mixed, h2_t, vec, arrays):
        held = [w.over(own) for w, own in zip((w_out, w_fc, w_proj), arrays)]
        return back_middle(place, dout, slope, y1, mixed, h2_t, vec, *held)

    found = steps.slot(
        "dp",
        work=run,
        given=(dout, slope, y1, mixed, h2_t, vec, [w.arrays for w in (w_out, w_fc, w_proj)]),
    )
    dmixed, dy1, f_send, f_keep, d_gain2, d_shift2, d_outb, d_fcb, d_projb = found
    end("df", f_keep, f_send, "halves", True)

    def heads_back(first, count, before):
        def run(qkv, mixed, dmixed, soft, h1_t, before):
            return attend_back(place, qkv, mixed, dmixed, soft, h1_t, first, count, before)

        return dict(work=run, given=(qkv, mixed, dmixed, soft, h1_t, before))

    dqkv, a_send, a_keep = steps.slot("df dp", **heads_back(0, half, None))
    end("da", a_keep, a_send, "turn", False)
    dqkv, b_send, b_keep = steps.slot("da df dp", **heads_back(half, half, dqkv))
    end("db", b_keep, b_send, "turn", False)
    sums = [(1, width), (1, width), (1, 2 * width), (72, 128)]
    tokens_grad, d_gain1, d_shift1, d_qv, packed = steps.slot(
        "all",
        **rows_work(
            "back_first",
            back_first_body,
            [dqkv, x, dy1],
            [vec, d_outb, d_gain2, d_shift2, d_fcb, d_projb],
            [w_a, w_b],
            [((length, width), bf16)],
            sums,
        ),
    )
    small = (d_gain1, d_shift1, d_qv, d_outb, d_gain2, d_shift2, d_fcb, d_projb)
    if plain:
        steps.done["dv"] = collect_vectors_plain(place, small)
    else:
        steps.add("dv", collect_vectors_steps(place, packed.reshape(2, -1, 128)))
    (block_out,) = steps.slot(
        "all",
        **rows_work(
            "finish", finish_body, [y1, g_t], [vec], [w_proj], [((length, width), bf16)], []
        ),
    )
    rows = width // 2
    placed = {}
    makers = {
        "dp": (put_rows, [(hidden // 2, width)], "put_proj"),
        "df": (put_wide, [(rows, hidden), (rows, width)], "put_fc"),
    }
    while steps.asked:
        ready = [n for n in makers if n in steps.done and n not in placed and not plain]
        if ready:
            found = steps.done[ready[0]]
            run = lambda *v: put(place, [v], *makers[ready[0]])
            placed[ready[0]] = steps.slot("all", work=run, given=found)
        else:
            steps.slot("all")

    held = lambda v: jnp.where(place.holder, v.astype(f32), 0.0)
    if plain:
        s_proj = held(steps.done["dp"])
        found = steps.done["df"].reshape(-1, hidden // width + 1, width // 8, width)
        fc = [found[:, i].reshape(-1, width) for i in range(hidden // width)]
        s_fc = held(jnp.concatenate(fc, axis=1))
        s_out = held(found[:, -1].reshape(-1, width))
        both = [
            v[:, (3 * p + j) * 128 : (3 * p + j + 1) * 128]
            for j in range(3)
            for v in (steps.done["da"], steps.done["db"])
            for p in range(half)
        ]
        s_qkv = held(jnp.concatenate(both, axis=1))
    else:
        for name in makers:
            if name not in placed:
                placed[name] = put(place, [steps.done[name]], *makers[name])
        (s_proj,), (s_fc, s_out) = placed["dp"], placed["df"]
        parts = [steps.done["da"], steps.done["db"]]
        (s_qkv,) = put(place, parts, put_pairs, [(rows, 3 * width)], "put_qkv")
    s_proj, s_fc, s_out, s_qkv = s_proj[None], s_fc[None], s_out[None], s_qkv[None]
    small = unpack_vectors(steps.done["dv"], [v.shape[1] // narrow for v in small])
    small = [held(v) for v in small]
    s_gain1, s_shift1, s_qv, s_outb, s_gain2, s_shift2, s_fcb, s_projb = small
    return (
        block_out[None],
        tokens_grad[None],
        s_gain1,
        s_shift1,
        s_qkv,
        s_qv,
        s_out,
        s_outb,
        s_gain2,
        s_shift2,
        s_fc,
        s_fcb,
        s_proj,
        s_projb,
    )


def solution(mesh):
    rows = P(AXES, None, None)
    flat, deep = P("wide", "narrow"), P("wide", "narrow", None)
    in_specs = (
        rows,
        P(AXES, None),
        rows,
        P(),
        flat,
        flat,
        deep,
        flat,
        deep,
        flat,
        flat,
        flat,
        deep,
        flat,
        deep,
        flat,
    )
    out_specs = (
        rows,
        rows,
        flat,
        flat,
        deep,
        flat,
        deep,
        flat,
        flat,
        flat,
        deep,
        flat,
        deep,
        flat,
    )
    body = functools.partial(on_device, mesh.shape["wide"], mesh.shape["narrow"])
    return jax.shard_map(
        body, mesh=mesh, in_specs=in_specs, out_specs=out_specs, check_vma=False
    )
```

```python
import functools
import math

import jax
import jax.numpy as jnp
from jax import lax
from jax.experimental import pallas as pl
from jax.experimental.pallas import tpu as pltpu
from jax.sharding import PartitionSpec as P

H = 12
HD = 64
QB = 256
REACH = 512

epsilon = 1e-05
AXES = ("wide", "narrow")
VMEM = 56 * 1024 * 1024
TINY = pl.CostEstimate(flops=1000, bytes_accessed=1000, transcendentals=0)
f32 = jnp.float32
bf16 = jnp.bfloat16


def spans(length):
    out = []
    for b in range(length // QB):
        low = max(0, (b * QB - (REACH - 1)) // QB * QB)
        out.append((low, (b + 1) * QB))
    return out


def soft_rows(length):
    return sum(hi - lo for lo, hi in spans(length))


def attend_pair(doc, q, k, v, o_ref, p_ref):
    length = q.shape[0]
    lane = lax.broadcasted_iota(jnp.int32, (length, 128), 1)
    low = lane < HD
    hot = (lane & (HD - 1)) == doc
    q_side = jnp.where(hot, 1.0, 0.0)
    k_side = jnp.where(hot, 0.0, -1e9)
    q = q.astype(f32) * HD ** (-0.5)
    k = k.astype(f32)
    v_t = v.T
    sides = []
    for h in range(2):
        mine = low if h == 0 else jnp.logical_not(low)
        sides.append(
            (jnp.where(mine, q, q_side).astype(bf16), jnp.where(mine, k, k_side).astype(bf16))
        )
    rows = lax.broadcasted_iota(jnp.int32, (QB, QB), 0)
    tri = rows <= lax.broadcasted_iota(jnp.int32, (QB, QB), 1)
    at = 0
    for b, (lo, hi) in enumerate(spans(length)):
        n = hi - lo
        outs = []
        for h in range(2):
            qa, ka = sides[h]
            s = dot(ka[lo:hi], qa[b * QB : (b + 1) * QB], ((1,), (1,)))
            last = jnp.where(tri, s[n - QB :], -1e9)
            s = last if n == QB else jnp.concatenate([s[: n - QB], last], axis=0)
            e = jnp.exp(s - jnp.max(s, axis=0, keepdims=True))
            p = (e * (1.0 / jnp.sum(e, axis=0, keepdims=True))).astype(bf16)
            p_ref[h, at : at + n, :] = p
            outs.append(dot(v_t[h * HD : (h + 1) * HD, lo:hi], p))
        o_ref[b * QB : (b + 1) * QB, :] = jnp.concatenate(outs, axis=0).T.astype(bf16)
        at += n


def attend(place, doc, x, vec, weights, column, first, count, before):
    length, width = x.shape
    start = before is None
    packed = vec is None
    rows = soft_rows(length)
    n_p, n_v = len(weights.arrays), 0 if packed else 1
    n_a = 0 if start else 3

    def kernel(*refs):
        refs = list(refs)
        take = lambda n: [refs.pop(0) for _ in range(n)]
        place_ref, doc_ref, x_ref = take(3)
        vec_refs, pieces = take(n_v), take(n_p)
        take(n_a)
        mixed_ref, soft_ref, qkv_ref = take(3)
        if start:
            h1_ref, h1_t_ref, vec_out = take(3)
        w, sem = take(2)
        step = pl.program_id(0)

        @pl.when(step == 0)
        def _():
            weights.load(place_ref, pieces, w, sem)
            if start:
                if packed:
                    vec_out[...] = unpack_rows(w)
                else:
                    vec_out[...] = vec_refs[0][...]
                for at in range(0, length, 256):
                    here = slice(at, at + 256)
                    h1 = norm_rows(
                        x_ref[here, :].astype(f32), row_of(vec_out, GAIN1), row_of(vec_out, SHIFT1)
                    ).astype(bf16)
                    h1_ref[here, :] = h1
                    h1_t_ref[:, here] = h1.T

        h1 = (h1_ref if start else x_ref)[...]
        known = vec_out if start else vec_refs[0]
        cols = w[:, pl.ds(pl.multiple_of(column + step * 384, 128), 384)]
        bias = jnp.concatenate(
            [
                known[pl.ds(QV[0] + first + step, 1), :],
                jnp.zeros((1, 128), f32),
                known[pl.ds(QV[0] + 6 + first + step, 1), :],
            ],
            axis=1,
        )
        qkv = (dot(h1, cols) + bias).astype(bf16)
        qkv_ref[...] = qkv
        attend_pair(
            doc_ref[...], qkv[:, :128], qkv[:, 128:256], qkv[:, 256:], mixed_ref, soft_ref
        )

    full = lambda shape: pl.BlockSpec(shape, lambda i: (0,) * len(shape))
    anyplace = pl.BlockSpec(memory_space=pl.ANY)
    outs = [
        ((length, width), (length, 128), lambda i: (0, first + i), bf16),
        ((H, rows, QB), (2, rows, QB), lambda i: (first + i, 0, 0), bf16),
        ((length, 3 * width), (length, 384), lambda i: (0, first + i), bf16),
    ]
    if start:
        outs += [
            ((length, width), (length, width), lambda i: (0, 0), bf16),
            ((width, length), (width, length), lambda i: (0, 0), bf16),
            ((72, 128), (72, 128), lambda i: (0, 0), f32),
        ]
    given = [place.spot, doc, x] + ([] if packed else [vec]) + weights.arrays
    aliases = {}
    if not start:
        aliases = {len(given) + i: i for i in range(3)}
        given += before
    return pl.pallas_call(
        kernel,
        grid=(count,),
        in_specs=[pl.BlockSpec(memory_space=pltpu.SMEM), full((length, 1)), full(x.shape)]
        + [full((72, 128))] * n_v
        + [anyplace] * (n_p + n_a),
        out_specs=[pl.BlockSpec(block, index) for _, block, index, _ in outs],
        out_shape=[jax.ShapeDtypeStruct(shape, kind) for shape, _, _, kind in outs],
        scratch_shapes=[
            pltpu.VMEM((weights.rows, weights.width), bf16),
            pltpu.SemaphoreType.DMA((n_p,)),
        ],
        input_output_aliases=aliases,
        compiler_params=pltpu.CompilerParams(vmem_limit_bytes=VMEM),
        cost_estimate=TINY,
        name="attend",
    )(*given)


def lay_blocks(ref, place_ref, other, rows):
    out = []
    core = 1 - place_ref[0] if other else place_ref[0]
    for x in range(2):
        for y in range(2):
            at = pl.multiple_of((4 * x + 2 * core + y) * rows, 16)
            out.append(ref[pl.ds(at, rows), :])
    return jnp.concatenate(out, axis=0)


def attend_back_kernel(
    place_ref,
    q_ref,
    k_ref,
    v_ref,
    o_ref,
    do_ref,
    p_ref,
    h1_t_ref,
    *refs,
    length,
):
    out_ref, send_ref, keep_ref, dk_acc, dv_acc = refs[-5:]
    lane = lax.broadcasted_iota(jnp.int32, (length, 128), 1)
    low = lane < HD
    spot = lane & (HD - 1)
    q = q_ref[...].astype(f32) * HD ** (-0.5)
    do = do_ref[...].astype(f32)
    v = v_ref[...].astype(f32)
    product = do * o_ref[...].astype(f32)
    k_t = k_ref[...].T
    sides = []
    for h in range(2):
        mine = low if h == 0 else jnp.logical_not(low)
        center = jnp.sum(jnp.where(mine, product, 0.0), axis=1, keepdims=True)
        first = center.astype(bf16).astype(f32)
        second = (center - first).astype(bf16).astype(f32)
        third = center - first - second
        extra = jnp.where(
            spot == 0, -first, jnp.where(spot == 1, -second, jnp.where(spot == 2, -third, 0.0))
        )
        sides.append(
            (
                jnp.where(mine, do, extra).astype(bf16),
                jnp.where(mine, v, jnp.where(spot < 3, 1.0, 0.0)).astype(bf16),
                jnp.where(mine, do, 0.0).astype(bf16),
                jnp.where(mine, q, 0.0).astype(bf16),
            )
        )
    dk_acc[...] = jnp.zeros_like(dk_acc)
    dv_acc[...] = jnp.zeros_like(dv_acc)
    at = 0
    for b, (lo, hi) in enumerate(spans(length)):
        n = hi - lo
        here = slice(b * QB, (b + 1) * QB)
        dqs = []
        dk = dv = None
        for h in range(2):
            do_more, v_more, do_own, q_own = sides[h]
            p = p_ref[h, at : at + n, :]
            dp = dot(v_more[lo:hi], do_more[here], ((1,), (1,)))
            ds = (p.astype(f32) * dp).astype(bf16)
            dv_part = dot(p, do_own[here])
            dk_part = dot(ds, q_own[here])
            dv = dv_part if dv is None else dv + dv_part
            dk = dk_part if dk is None else dk + dk_part
            dqs.append(dot(k_t[h * HD : (h + 1) * HD, lo:hi], ds))
        dv_acc[lo:hi, :] += dv
        dk_acc[lo:hi, :] += dk
        out_ref[here, :128] = (jnp.concatenate(dqs, axis=0) * HD ** (-0.5)).T.astype(bf16)
        at += n
    out_ref[:, 128:256] = dk_acc[...].astype(bf16)
    out_ref[:, 256:] = dv_acc[...].astype(bf16)
    parts = out_ref[...]
    for other, ref in ((True, send_ref), (False, keep_ref)):
        rows = h1_t_ref.shape[0] // 8
        ref[...] = dot(lay_blocks(h1_t_ref, place_ref, other, rows), parts).astype(bf16)


def attend_back(place, qkv, mixed, grad_mixed, soft, h1_t, first, count, before):
    length, width = mixed.shape
    rows = soft_rows(length)
    col = lambda off: pl.BlockSpec((length, 128), lambda i: (0, 3 * (first + i) + off))
    pair = pl.BlockSpec((length, 128), lambda i: (0, first + i))
    terms = pl.BlockSpec((width // 2, 384), lambda i: (0, i))
    term = jax.ShapeDtypeStruct((width // 2, 384 * count), bf16)
    given = [place.spot, qkv, qkv, qkv, mixed, grad_mixed, soft, h1_t]
    aliases = {}
    if before is not None:
        aliases = {len(given): 0}
        given.append(before)
    return pl.pallas_call(
        functools.partial(attend_back_kernel, length=length),
        grid=(count,),
        in_specs=[
            pl.BlockSpec(memory_space=pltpu.SMEM),
            col(0),
            col(1),
            col(2),
            pair,
            pair,
            pl.BlockSpec((2, rows, QB), lambda i: (first + i, 0, 0)),
            pl.BlockSpec(h1_t.shape, lambda i: (0, 0)),
        ]
        + [pl.BlockSpec(memory_space=pl.ANY)] * len(aliases),
        out_specs=[pl.BlockSpec((length, 384), lambda i: (0, first + i)), terms, terms],
        out_shape=[jax.ShapeDtypeStruct(qkv.shape, bf16), term, term],
        scratch_shapes=[pltpu.VMEM((length, 128), f32)] * 2,
        input_output_aliases=aliases,
        compiler_params=pltpu.CompilerParams(vmem_limit_bytes=VMEM),
        cost_estimate=TINY,
        name="attend_back",
    )(*given)


def proj_terms(place, g_t, dout):
    hidden, length = g_t.shape
    width = dout.shape[1]
    rows = hidden // 4

    def kernel(place_ref, g_ref, dout_ref, send_ref, keep_ref):
        value = dot(g_ref[...], dout_ref[...]).astype(bf16)

        @pl.when(pl.program_id(0) < 2)
        def _():
            send_ref[...] = value

        @pl.when(pl.program_id(0) >= 2)
        def _():
            keep_ref[...] = value

    def block(i, place_ref):
        core = jnp.where(i < 2, 1 - place_ref[0], place_ref[0])
        return 2 * (i % 2) + core, 0

    out = jax.ShapeDtypeStruct((hidden // 2, width), bf16)
    return pl.pallas_call(
        kernel,
        grid_spec=pltpu.PrefetchScalarGridSpec(
            num_scalar_prefetch=1,
            grid=(4,),
            in_specs=[
                pl.BlockSpec((rows, length), block),
                pl.BlockSpec((length, width), lambda i, p: (0, 0)),
            ],
            out_specs=[
                pl.BlockSpec((rows, width), lambda i, p: (jnp.minimum(i, 1), 0)),
                pl.BlockSpec((rows, width), lambda i, p: (jnp.maximum(i - 2, 0), 0)),
            ],
        ),
        out_shape=[out, out],
        compiler_params=pltpu.CompilerParams(vmem_limit_bytes=VMEM),
        cost_estimate=TINY,
        name="proj_terms",
    )(place.spot, g_t, dout)


def back_middle(place, dout, slope, y1, mixed, h2_t, vec, w_out, w_fc, w_proj):
    length, width = dout.shape
    hidden = w_fc.width
    step_rows, part = 256, PART
    steps = length // step_rows
    f_steps, rows = hidden // width, width // 8
    weights = (w_out, w_fc, w_proj)
    counts = [len(w.arrays) for w in weights]

    def kernel(*refs):
        refs = list(refs)
        take = lambda n: [refs.pop(0) for _ in range(n)]
        place_ref, dout_ref, slope_ref, y1_ref, mixed_ref, h2_t, vec_ref = take(7)
        pieces = [take(n) for n in counts]
        dmixed_ref, dy1_ref, send_ref, keep_ref = take(4)
        gain_ref, shift_ref, outb_ref, fcb_ref, projb_ref = sums = take(5)
        wo, wf, wp = buffers = take(3)
        sems = take(3)
        du_all, mixed_t, db1_all = take(3)
        i = pl.program_id(0)

        @pl.when(i == 0)
        def _():
            for w, own, buffer, sem in zip(weights, pieces, buffers, sems):
                w.load(place_ref, own, buffer, sem)
            for ref in sums:
                ref[...] = jnp.zeros_like(ref)

        @pl.when(i < steps)
        def _():
            here = pl.ds(pl.multiple_of(i * step_rows, step_rows), step_rows)
            dout = dout_ref[...]
            mixed_t[:, here] = mixed_ref[...].T
            dh2 = jnp.zeros((step_rows, width), f32)
            for c in range(0, hidden, part):
                cols = slice(c, c + part)
                du = dot(dout, wp[cols, :], ((1,), (1,))) * slope_ref[:, cols].astype(f32)
                du = du.astype(bf16)
                du_all[here, cols] = du
                fcb_ref[:, cols] += jnp.sum(du.astype(f32), axis=0, keepdims=True)
                dh2 = dh2 + dot(du, wf[:, cols], ((1,), (1,)))
            back, gain, shift = norm_back(y1_ref[...], row_of(vec_ref, GAIN2), dh2)
            wide_dout = dout.astype(f32)
            dy1 = wide_dout + back
            db1 = dy1.astype(bf16)
            dy1_ref[...] = dy1
            db1_all[here, :] = db1
            dmixed_ref[...] = dot(db1, wo[...], ((1,), (1,))).astype(bf16)
            gain_ref[...] += gain
            shift_ref[...] += shift
            outb_ref[...] += jnp.sum(db1.astype(f32), axis=0, keepdims=True)
            projb_ref[...] += jnp.sum(wide_dout, axis=0, keepdims=True)

        j = i - steps

        @pl.when((j >= 0) & (j < f_steps))
        def _():
            cols = pl.ds(pl.multiple_of(j * width, 128), width)
            for other, ref in ((True, send_ref), (False, keep_ref)):
                value = dot(lay_blocks(h2_t, place_ref, other, rows), du_all[:, cols])
                ref[...] = value.astype(bf16).reshape(ref.shape)

        @pl.when(j == f_steps)
        def _():
            for other, ref in ((True, send_ref), (False, keep_ref)):
                value = dot(lay_blocks(mixed_t, place_ref, other, rows), db1_all[...])
                ref[...] = value.astype(bf16).reshape(ref.shape)

    full = lambda shape: pl.BlockSpec(shape, lambda i: (0,) * len(shape))
    slab = lambda n: pl.BlockSpec((step_rows, n), lambda i: (jnp.minimum(i, steps - 1), 0))
    terms = pl.BlockSpec(
        (4, rows, width), lambda i: (0, jnp.clip(i - steps, 0, f_steps), 0)
    )
    like = jax.ShapeDtypeStruct
    one = (1, width)
    sum_shapes = [one, one, one, (1, hidden), one]
    return pl.pallas_call(
        kernel,
        grid=(steps + f_steps + 1,),
        in_specs=[
            pl.BlockSpec(memory_space=pltpu.SMEM),
            slab(width),
            slab(hidden),
            slab(width),
            slab(width),
            full(h2_t.shape),
            full((72, 128)),
        ]
        + [pl.BlockSpec(memory_space=pl.ANY)] * sum(counts),
        out_specs=[slab(width), slab(width), terms, terms] + [full(v) for v in sum_shapes],
        out_shape=[
            like((length, width), bf16),
            like((length, width), f32),
            like((4, rows * (f_steps + 1), width), bf16),
            like((4, rows * (f_steps + 1), width), bf16),
        ]
        + [like(v, f32) for v in sum_shapes],
        scratch_shapes=[pltpu.VMEM((w.rows, w.width), bf16) for w in weights]
        + [pltpu.SemaphoreType.DMA((n,)) for n in counts]
        + [
            pltpu.VMEM((length, hidden), bf16),
            pltpu.VMEM((width, length), bf16),
            pltpu.VMEM((length, width), bf16),
        ],
        compiler_params=pltpu.CompilerParams(vmem_limit_bytes=VMEM),
        cost_estimate=TINY,
        name="back_middle",
    )(place.spot, dout, slope, y1, mixed, h2_t, vec, *[v for w in weights for v in w.arrays])


class Place:
    def __init__(self, owner, wide, narrow, plain):
        self.wide, self.narrow = wide, narrow
        self.deep = wide // 4
        mine = lax.axis_index("wide")
        self.core, self.y, self.z = mine & 1, (mine >> 1) & 1, mine >> 2
        self.o_core, self.o_y, self.o_z = owner & 1, (owner >> 1) & 1, owner >> 2
        self.x = lax.axis_index("narrow")
        self.holder = mine == owner
        spot = jnp.stack([self.core, self.x, self.y, self.holder]).astype(jnp.int32)
        self.spot = jnp.zeros_like(spot) if plain else spot

    def swap(self, value, flip):
        return lax.ppermute(value, "wide", [(i, i ^ flip) for i in range(self.wide)])

    def cross(self, value, flip):
        pairs = [(2 * i + j, 2 * (i ^ flip) + 1 - j) for i in range(self.wide) for j in range(2)]
        return lax.ppermute(value, AXES, pairs)

    def shift(self, value, pairs):
        places = [(4 * a + low, 4 * b + low) for a, b in pairs for low in range(4)]
        return lax.ppermute(value, "wide", places)

    def z_pairs(self):
        last = self.deep - 1
        return [((i, i + 1), (last - i, last - i - 1)) for i in range(self.deep // 2 - 1)]

    def deal(self, value, kind):
        if kind == "plane":
            groups = [
                [2 * (4 * z + 2 * y + core) + x for x in range(2) for y in range(2)]
                for z in range(self.deep)
                for core in range(2)
            ]
            return lax.all_to_all(
                value, AXES, 0, 0, axis_index_groups=groups, tiled=True
            )
        groups = [
            [4 * z + 2 * y + core for y in range(2) for z in range(self.deep)]
            for core in range(2)
        ]
        return lax.all_to_all(value, "wide", 0, 0, axis_index_groups=groups, tiled=True)

    def z_flips(self):
        step = self.deep // 2
        while step:
            yield step
            step //= 2


def pick(parts, index):
    return lax.dynamic_index_in_dim(parts, index, axis=0, keepdims=False)


def ordered(mine, other, index):
    first = index == 0
    return jnp.stack([jnp.where(first, mine, other), jnp.where(first, other, mine)])


def spread_plain(place, shard):
    now = jnp.where(place.core == place.o_core, shard, place.swap(shard, 1))
    now = jnp.where(place.y == place.o_y, now, place.swap(now, 2))
    for step in place.z_flips():
        other = place.swap(now, 4 * step)
        now = jnp.where((place.z & step) == (place.o_z & step), now, other)
    return lax.all_gather(now, "narrow", axis=0, tiled=True)


def spread_steps(place, shard):
    if isinstance(shard, tuple):
        keep, send = shard
    else:
        halves = shard.reshape(2, shard.shape[0] // 2, shard.shape[1])
        keep, send = pick(halves, place.core), pick(halves, 1 - place.core)
    rows, width = 2 * keep.shape[0], keep.shape[1]
    (other,) = yield [(send, 1)]
    now = jnp.where(place.core == place.o_core, keep, other)
    halves = now.reshape(2, rows // 4, width)
    (other,) = yield [(pick(halves, 1 - place.y), 2)]
    now = jnp.where(place.y == place.o_y, pick(halves, place.y), other)
    for step in place.z_flips():
        (other,) = yield [(now, 4 * step)]
        now = jnp.where((place.z & step) == (place.o_z & step), now, other)
    by_y, by_x = yield [(now, 2), (now, 0)]
    cut = rows // 8
    far_a, far_b = yield [(by_y[:cut], 0), (by_x[cut:], 2)]
    mine = [
        (now, (0, 0, 0), 0),
        (by_y, (0, 0, 1), 0),
        (by_x, (0, 1, 0), 0),
        (far_a, (0, 1, 1), 0),
        (far_b, (0, 1, 1), cut),
    ]
    theirs = yield [(piece, 1) for piece, _, _ in mine]
    return Pieces(
        mine + [(got, (1, x, y), row) for got, (_, (_, x, y), row) in zip(theirs, mine)]
    )


class Pieces:
    def __init__(self, found):
        self.arrays = [piece for piece, _, _ in found]
        self.spots = [(flips, row) for _, flips, row in found]
        self.block, self.width = self.arrays[0].shape
        self.rows = self.block if len(found) == 1 else 8 * self.block

    def over(self, arrays):
        return Pieces([(v, flips, row) for v, (flips, row) in zip(arrays, self.spots)])

    def load(self, place_ref, refs, buffer, sem):
        copies = []
        for ref, ((core, x, y), row) in zip(refs, self.spots):
            start = 0
            if len(refs) > 1:
                at = 4 * (place_ref[1] ^ x) + 2 * (place_ref[0] ^ core) + (place_ref[2] ^ y)
                start = pl.multiple_of(at * self.block + row, 16)
            target = buffer.at[pl.ds(start, ref.shape[0]), :]
            copies.append(pltpu.make_async_copy(ref, target, sem.at[len(copies)]))
        for copy in copies:
            copy.start()
        for copy in copies:
            copy.wait()


ROWS = 256
PART = 1024


def by_rows(name, body, place, blocks, wholes, weights, out_blocks, out_sums):
    length = blocks[0].shape[0]
    n_b, n_w, n_o, n_s = len(blocks), len(wholes), len(out_blocks), len(out_sums)
    counts = [len(w.arrays) for w in weights]

    def kernel(*refs):
        refs = list(refs)
        take = lambda n: [refs.pop(0) for _ in range(n)]
        (place_ref,) = take(1)
        block_refs, whole_refs = take(n_b), take(n_w)
        piece_refs = [take(n) for n in counts]
        out_refs, sum_refs = take(n_o), take(n_s)
        buffers, sems = take(len(weights)), take(len(weights))

        @pl.when(pl.program_id(0) == 0)
        def _():
            for w, pieces, buffer, sem in zip(weights, piece_refs, buffers, sems):
                w.load(place_ref, pieces, buffer, sem)
            for ref in sum_refs:
                ref[...] = jnp.zeros_like(ref)

        body(block_refs, whole_refs, buffers, out_refs, sum_refs)

    full = lambda shape: pl.BlockSpec(shape, lambda i: (0,) * len(shape))
    slab = lambda shape: (
        pl.BlockSpec((ROWS, shape[1]), lambda i: (i, 0))
        if shape[0] == length
        else pl.BlockSpec((shape[0], ROWS), lambda i: (0, i))
    )
    return pl.pallas_call(
        kernel,
        grid=(length // ROWS,),
        in_specs=[pl.BlockSpec(memory_space=pltpu.SMEM)]
        + [slab(v.shape) for v in blocks]
        + [full(v.shape) for v in wholes]
        + [pl.BlockSpec(memory_space=pl.ANY)] * sum(counts),
        out_specs=[slab(shape) for shape, _ in out_blocks] + [full(s) for s in out_sums],
        out_shape=[jax.ShapeDtypeStruct(shape, kind) for shape, kind in out_blocks]
        + [jax.ShapeDtypeStruct(shape, f32) for shape in out_sums],
        scratch_shapes=[pltpu.VMEM((w.rows, w.width), bf16) for w in weights]
        + [pltpu.SemaphoreType.DMA((n,)) for n in counts],
        compiler_params=pltpu.CompilerParams(vmem_limit_bytes=VMEM),
        cost_estimate=TINY,
        name=name,
    )(place.spot, *blocks, *wholes, *[v for w in weights for v in w.arrays])


def tie(groups):
    flat, tree = jax.tree.flatten(groups)
    return jax.tree.unflatten(tree, lax.optimization_barrier(flat))


class Steps:
    def __init__(self, place):
        self.place = place
        self.asked, self.flips, self.chains, self.done, self.going = {}, {}, {}, {}, {}

    def ask(self, name, pairs):
        self.asked[name] = [value for value, _ in pairs]
        self.flips[name] = [flip for _, flip in pairs]

    def add(self, name, chain):
        self.chains[name] = chain
        self.ask(name, next(chain))

    def exchange(self, value, flip):
        if isinstance(flip, tuple):
            return self.place.shift(value, flip)
        if isinstance(flip, str):
            return self.place.deal(value, flip)
        if flip <= 0:
            return self.place.cross(value, -flip)
        return self.place.swap(value, flip)

    def slot(self, names="", hold="", work=None, given=(), strict=False):
        names = list(self.asked) if names == "all" else names.replace(",", " ").split()
        hold = hold.split()
        assert not set(names) & set(self.going)
        asked = {name: self.asked[name] for name in names if name in self.asked}
        if strict:
            asked = tie(asked)
        for name, values in asked.items():
            self.going[name] = [
                self.exchange(value, flip) for value, flip in zip(values, self.flips[name])
            ]
        held = tie({"asked": asked, "given": given})
        result = work(*held["given"]) if work else ()
        ready = {name: got for name, got in self.going.items() if name not in hold}
        ready, result, self.asked = tie((ready, result, self.asked))
        for name, got in ready.items():
            del self.going[name], self.asked[name]
            try:
                self.ask(name, self.chains[name].send(got))
            except StopIteration as stop:
                self.done[name] = stop.value
        return result


def collect_plain(place, keep, send):
    width = keep.shape[-1]
    parts = [v.reshape(2, 1, 2, -1, width) for v in (keep, send)]
    terms = jnp.concatenate(parts, axis=1).reshape(-1, width)
    now = lax.psum_scatter(terms, "narrow", scatter_dimension=0, tiled=True)
    return lax.psum(now, "wide")


def add(*values):
    return functools.reduce(lambda a, b: a + b, [v.astype(f32) for v in values]).astype(bf16)


def collect_steps(place, keep, send, plane, line):
    width = keep.shape[-1]
    (other,) = yield [(send, 1)]
    if plane == "deal":
        (got,) = yield [(add(keep, other).reshape(-1, width), "plane")]
        now = add(*got.reshape(4, -1, width))
    else:
        terms = [v.reshape(2, 2, -1, width) for v in (keep, other)]
        at_x = lambda v, i: pick(v, place.x ^ i)
        at_y = lambda v, i: lax.dynamic_index_in_dim(v, place.y ^ i, axis=1, keepdims=False)
        if plane == "turn":
            (other,) = yield [(add(*[at_x(v, 1) for v in terms]), 0)]
            terms = [at_x(v, 0) for v in terms] + [other]
            part = lambda i: add(*[pick(v, place.y ^ i) for v in terms])
            (other,) = yield [(part(1), 2)]
            now = add(part(0), other)
        else:
            cut = terms[0].shape[2] // 2
            upper = [v[:, :, :cut] for v in terms]
            lower = [v[:, :, cut:] for v in terms]
            by_x, by_y = yield [
                (add(*[at_x(v, 1) for v in upper]), 0),
                (add(*[at_y(v, 1) for v in lower]), 2),
            ]
            upper = [at_x(v, 0) for v in upper] + [by_x]
            lower = [at_y(v, 0) for v in lower] + [by_y]
            top = lambda i: add(*[pick(v, place.y ^ i) for v in upper])
            low = lambda i: add(*[pick(v, place.x ^ i) for v in lower])
            by_y, by_x = yield [(top(1), 2), (low(1), 0)]
            now = jnp.concatenate([add(top(0), by_y), add(low(0), by_x)], axis=0)
    if line:
        inward = place.z_pairs()
        for pairs in inward:
            (other,) = yield [(now, pairs)]
            now = add(now, other)
        half = place.deep // 2
        (other,) = yield [(now, ((half - 1, half), (half, half - 1)))]
        now = add(now, other)
        for pairs in reversed(inward):
            (other,) = yield [(now, tuple((b, a) for a, b in pairs))]
            got = (place.z == pairs[0][0]) | (place.z == pairs[1][0])
            now = jnp.where(got, other, now)
    else:
        for step in reversed(list(place.z_flips())):
            (other,) = yield [(now, 4 * step)]
            now = add(now, other)
    (other,) = yield [(now, 2)]
    far, far_other = yield [(now, 1), (other, 1)]
    return [now, other, far, far_other]


def put_kernel(place_ref, *refs, counts, bodies):
    refs = list(refs)
    take = lambda n: [refs.pop(0) for _ in range(n)]
    pieces = [take(4) for _ in range(counts[0])]
    outs = take(counts[1])
    buffers, sem = take(counts[0]), refs[0]
    copies = []
    for group, buffer in zip(pieces, buffers):
        for i, ref in enumerate(group):
            rows = ref.shape[0]
            at = 2 * (place_ref[0] ^ (i // 2)) + (place_ref[2] ^ (i % 2))
            target = buffer.at[pl.ds(pl.multiple_of(at * rows, 16), rows), :]
            copies.append(pltpu.make_async_copy(ref, target, sem.at[len(copies)]))
    for copy in copies:
        copy.start()
    for copy in copies:
        copy.wait()
    holder = place_ref[3] == 1
    bodies(buffers, outs, lambda v: jnp.where(holder, v.astype(f32), 0.0))


def put(place, groups, bodies, shapes, name):
    flat = [v for group in groups for v in group]
    return pl.pallas_call(
        functools.partial(put_kernel, counts=(len(groups), len(shapes)), bodies=bodies),
        in_specs=[pl.BlockSpec(memory_space=pltpu.SMEM)]
        + [pl.BlockSpec(memory_space=pl.ANY)] * len(flat),
        out_specs=[pl.BlockSpec(memory_space=pltpu.VMEM)] * len(shapes),
        out_shape=[jax.ShapeDtypeStruct(v, f32) for v in shapes],
        scratch_shapes=[
            pltpu.VMEM((4 * group[0].shape[0], group[0].shape[1]), bf16) for group in groups
        ]
        + [pltpu.SemaphoreType.DMA((len(flat),))],
        compiler_params=pltpu.CompilerParams(vmem_limit_bytes=VMEM),
        cost_estimate=TINY,
        name=name,
    )(place.spot, *flat)


def put_rows(buffers, outs, mask):
    outs[0][...] = mask(buffers[0][...])


def put_wide(buffers, outs, mask):
    wide, narrow = outs
    rows = narrow.shape[0] // 4
    width = narrow.shape[1]
    blocks = wide.shape[1] // width
    for quarter in range(4):
        here = slice(quarter * rows, (quarter + 1) * rows)
        for i in range(blocks + 1):
            start = (quarter * (blocks + 1) + i) * rows
            value = mask(buffers[0][start : start + rows, :])
            if i < blocks:
                wide[here, i * width : (i + 1) * width] = value
            else:
                narrow[here, :] = value


def put_pairs(buffers, outs, mask):
    width = outs[0].shape[1] // 3
    for part, buffer in enumerate(buffers):
        pairs = buffer.shape[1] // 384
        for p in range(pairs):
            for j in range(3):
                at = j * width + (part * pairs + p) * 128
                source = (3 * p + j) * 128
                outs[0][:, at : at + 128] = mask(buffer[:, source : source + 128])


def unpack_vectors(now, sizes):
    now = now.reshape(1, -1)
    out, at = [], 0
    for size in sizes:
        out.append(now[:, at : at + size])
        at += size
    return out


def shares(vectors, narrow):
    out = []
    for i in range(narrow):
        for v in vectors:
            size = v.shape[1] // narrow
            out.append(v[:, i * size : (i + 1) * size])
    return jnp.concatenate(out, axis=1)


def collect_vectors_steps(place, now):
    (other,) = yield [(now, 1)]
    now = now + other
    (other,) = yield [(pick(now, 1 - place.x), 0)]
    now = pick(now, place.x) + other
    (other,) = yield [(now, 2)]
    now = now + other
    for step in place.z_flips():
        (other,) = yield [(now, 4 * step)]
        now = now + other
    return now


def collect_vectors_plain(place, vectors):
    now = shares(vectors, place.narrow).reshape(place.narrow, -1)
    now = lax.psum_scatter(now, "narrow", scatter_dimension=0, tiled=False)
    return lax.psum(now, "wide")


def norm_rows(values, gain, shift):
    center = values - jnp.mean(values, axis=-1, keepdims=True)
    spread_of = jnp.mean(center * center, axis=-1, keepdims=True)
    return center * lax.rsqrt(spread_of + epsilon) * gain + shift


def norm_back(values, gain, grad):
    center = values - jnp.mean(values, axis=-1, keepdims=True)
    inverse = lax.rsqrt(jnp.mean(center * center, axis=-1, keepdims=True) + epsilon)
    hat = center * inverse
    scaled = grad * gain
    inner = jnp.mean(scaled * hat, axis=-1, keepdims=True)
    back = inverse * (scaled - jnp.mean(scaled, axis=-1, keepdims=True) - hat * inner)
    return (
        back,
        jnp.sum(grad * hat, axis=0, keepdims=True),
        jnp.sum(grad, axis=0, keepdims=True),
    )


def gelu_both(u):
    c = math.sqrt(2.0 / math.pi)
    square = u * u
    half = 0.5 + 0.5 * jnp.tanh(u * (c + c * 0.044715 * square))
    g = u * half
    return g, half + g * (1.0 - half) * (2 * c + 6 * c * 0.044715 * square)


def dot(a, b, dims=((1,), (0,))):
    return lax.dot_general(a, b, (dims, ((), ())), preferred_element_type=f32)


GAIN1, SHIFT1, QV, OUTB = (0, 6), (6, 6), (12, 12), (24, 6)
GAIN2, SHIFT2, FCB, PROJB = (30, 6), (36, 6), (42, 24), (66, 6)


def row_of(vec, spot, first=0, count=None):
    start = spot[0] + first
    count = spot[1] if count is None else count
    return jnp.concatenate([vec[start + i : start + i + 1, :] for i in range(count)], axis=1)


def unpack_rows(w):
    shard = w.shape[0] // 2
    near = w[:64, w.shape[1] - 128 :].astype(f32)
    far = w[shard : shard + 64, w.shape[1] - 128 :].astype(f32)
    parts = []
    for start, count in (GAIN1, SHIFT1, QV, OUTB, GAIN2, SHIFT2, FCB, PROJB):
        rows = slice(start // 2, (start + count) // 2)
        parts += [near[rows], far[rows]]
    return jnp.concatenate(parts, axis=0)


def pack_kernel(core_ref, w_ref, *refs):
    vectors, outs, rows_ref = refs[:-5], refs[-5:-1], refs[-1]
    half, width = w_ref.shape[0] // 2, w_ref.shape[1] // 3
    rows_ref[...] = jnp.zeros_like(rows_ref)
    at = 0
    for ref in vectors:
        value = ref[...].astype(f32)
        for i in range(value.shape[1] // 128):
            rows_ref[at : at + 1, :] = value[:, i * 128 : (i + 1) * 128]
            at += 1
    pairs = width // 128
    for other in range(2):
        core = 1 - core_ref[0] if other else core_ref[0]
        w = w_ref[pl.ds(pl.multiple_of(core * half, 16), half), :]
        for part in range(2):
            ref = outs[2 * part + other]
            for p in range(pairs // 2):
                for j in range(3):
                    source = j * width + (part * (pairs // 2) + p) * 128
                    to = (3 * p + j) * 128
                    ref[:, to : to + 128] = w[:, source : source + 128]
            if part == 0:
                block = rows_ref[...].astype(bf16)
                ref[:, 3 * width // 2 :] = jnp.concatenate([block, block], axis=0)


def pack(place, w, vectors):
    rows, width = w.shape
    side = width // 2
    shape = lambda more: jax.ShapeDtypeStruct((rows // 2, side + more), bf16)
    vmem = pl.BlockSpec(memory_space=pltpu.VMEM)
    near, near_send, far, far_send = pl.pallas_call(
        pack_kernel,
        in_specs=[pl.BlockSpec(memory_space=pltpu.SMEM)] + [vmem] * (1 + len(vectors)),
        out_specs=[vmem] * 4,
        out_shape=[shape(128), shape(128), shape(0), shape(0)],
        scratch_shapes=[pltpu.VMEM((rows // 4, 128), f32)],
        compiler_params=pltpu.CompilerParams(vmem_limit_bytes=VMEM),
        cost_estimate=TINY,
        name="pack",
    )(place.spot, w, *vectors)
    return (near, near_send), (far, far_send)


def widen_body(blocks, wholes, weights, outs, sums):
    (x_ref, mixed_ref), (vec,), (w_out, w_fc) = blocks, wholes, weights
    y1_ref, slope_ref, h2_t_ref, g_t_ref = outs
    y1 = x_ref[...].astype(f32) + dot(mixed_ref[...], w_out[...]) + row_of(vec, OUTB)
    y1_ref[...] = y1
    h2 = norm_rows(y1, row_of(vec, GAIN2), row_of(vec, SHIFT2)).astype(bf16)
    h2_t_ref[...] = h2.T
    for at in range(0, w_fc.shape[1], PART):
        here = slice(at, at + PART)
        g, slope = gelu_both(dot(h2, w_fc[:, here]) + row_of(vec, FCB, at // 128, PART // 128))
        g_t_ref[here, :] = g.astype(bf16).T
        slope_ref[:, here] = slope.astype(bf16)


def finish_body(blocks, wholes, weights, outs, sums):
    (y1_ref, g_t_ref), (vec,), (w,) = blocks, wholes, weights
    result = y1_ref[...] + dot(g_t_ref[...], w[...], ((0,), (0,))) + row_of(vec, PROJB)
    outs[0][...] = result.astype(bf16)


def back_first_body(blocks, wholes, weights, outs, sums):
    (dqkv_ref, x_ref, dy1_ref), (vec, *more), (w_a, w_b) = blocks, wholes, weights
    side = w_b.shape[1]
    dqkv = dqkv_ref[...]
    dh1 = dot(dqkv[:, :side], w_a[:, :side], ((1,), (1,)))
    dh1 = dh1 + dot(dqkv[:, side:], w_b[...], ((1,), (1,)))
    back, gain, shift = norm_back(x_ref[...].astype(f32), row_of(vec, GAIN1), dh1)
    outs[0][...] = (dy1_ref[...] + back).astype(bf16)
    total = jnp.sum(dqkv.astype(f32), axis=0, keepdims=True)
    parts = [total[:, p * 384 + j : p * 384 + j + 128] for j in (0, 256) for p in range(H // 2)]
    for ref, value in zip(sums, (gain, shift, jnp.concatenate(parts, axis=1))):
        ref[...] += value

    @pl.when(pl.program_id(0) == pl.num_programs(0) - 1)
    def _():
        found = sums[:3] + more
        at = 0
        for half in range(2):
            for ref in found:
                count = ref.shape[1] // 256
                for i in range(count):
                    start = (half * count + i) * 128
                    sums[3][at : at + 1, :] = ref[:, start : start + 128]
                    at += 1


def on_device(
    wide,
    narrow,
    tokens,
    doc_ids,
    cotangent,
    owner,
    ln1_gain,
    ln1_bias,
    qkv_weight,
    qv_bias,
    out_weight,
    out_bias,
    ln2_gain,
    ln2_bias,
    fc_weight,
    fc_bias,
    proj_weight,
    proj_bias,
):
    _, length, width = tokens.shape
    plain = narrow != 2 or ln1_gain.shape[1] % 128 != 0
    place = Place(owner[0], wide, narrow, plain)
    x = tokens[0]
    dout = cotangent[0]
    doc = doc_ids[0][:, None]
    pairs = H // 2
    half = pairs // 2

    def begin(name, shard):
        if plain:
            steps.done[name] = Pieces([(spread_plain(place, shard), (0, 0, 0), 0)])
        else:
            steps.add(name, spread_steps(place, shard))

    def end(name, keep, send, plane, line):
        if plain:
            steps.done[name] = collect_plain(place, keep, send)
        else:
            steps.add(name, collect_steps(place, keep, send, plane, line))

    steps = Steps(place)
    vectors = (ln1_gain, ln1_bias, qv_bias, out_bias, ln2_gain, ln2_bias, fc_bias, proj_bias)
    sizes = [v.shape[1] for v in vectors]
    vec = None
    if plain:
        rows = spread_plain(place, jnp.concatenate(vectors, axis=1))
        parts, at = [], 0
        for size in sizes:
            parts.append(rows[:, at : at + size].reshape(-1))
            at += size
        vec = jnp.concatenate(parts).reshape(-1, 128).astype(f32)
        order = [
            qkv_weight[0][:, j * width + p * 128 : j * width + (p + 1) * 128]
            for p in range(pairs)
            for j in range(3)
        ]
        near = jnp.concatenate(order[: 3 * half], axis=1)
        far = jnp.concatenate(order[3 * half :], axis=1)
    else:
        near, far = pack(place, qkv_weight[0], vectors)
    begin("qa", near)
    begin("qb", far)
    begin("o", out_weight[0])
    begin("f", fc_weight[0])
    begin("p", proj_weight[0])

    def attention(x, vec, name, column, first, count, before):
        weights = steps.done[name]

        def run(x, vec, arrays, before):
            return attend(place, doc, x, vec, weights.over(arrays), column, first, count, before)

        return dict(work=run, given=(x, vec, weights.arrays, before))

    def rows_work(name, body, blocks, wholes, weights, out_blocks, out_sums):
        def run(blocks, wholes, arrays):
            held = [w.over(own) for w, own in zip(weights, arrays)]
            return by_rows(name, body, place, blocks, wholes, held, out_blocks, out_sums)

        return dict(work=run, given=(blocks, wholes, [w.arrays for w in weights]))

    steps.slot("qa qb", strict=True)
    steps.slot("qa", strict=True)
    steps.slot("qa,qb,o,f,p", strict=True)
    steps.slot("qa qb o f", hold="qb f", strict=True)
    steps.slot("qa", hold="f", strict=True)
    steps.slot("qa qb o", strict=True)
    steps.slot("qa qb f p", hold="f p", strict=True)
    state = steps.slot("qb o", **attention(x, vec, "qa", 0, 0, 2, None))
    state, (h1, h1_t, vec) = list(state[:3]), state[3:]
    state = steps.slot(
        "qb o f p", hold="p", **attention(h1, vec, "qa", 768, 2, 1, state)
    )
    state = steps.slot("o f", hold="", **attention(h1, vec, "qb", 0, 3, 2, list(state)))
    state = steps.slot("f o p", **attention(h1, vec, "qb", 768, 5, 1, list(state)))
    mixed, soft, qkv = state
    steps.slot("f p", hold="p")
    w_a, w_b, w_out, w_fc = [steps.done[name] for name in ("qa", "qb", "o", "f")]
    hidden = w_fc.width
    y1, slope, h2_t, g_t = steps.slot(
        "",
        **rows_work(
            "widen",
            widen_body,
            [x, mixed],
            [vec],
            [w_out, w_fc],
            [
                ((length, width), f32),
                ((length, hidden), bf16),
                ((width, length), bf16),
                ((hidden, length), bf16),
            ],
            [],
        ),
    )
    p_send, p_keep = steps.slot(
        "p", work=lambda g_t, dout: proj_terms(place, g_t, dout), given=(g_t, dout)
    )
    end("dp", p_keep, p_send, "deal", False)
    steps.slot("p dp")
    w_proj = steps.done["p"]

    def run(dout, slope, y1, mixed, h2_t, vec, arrays):
        held = [w.over(own) for w, own in zip((w_out, w_fc, w_proj), arrays)]
        return back_middle(place, dout, slope, y1, mixed, h2_t, vec, *held)

    found = steps.slot(
        "dp",
        work=run,
        given=(dout, slope, y1, mixed, h2_t, vec, [w.arrays for w in (w_out, w_fc, w_proj)]),
    )
    dmixed, dy1, f_send, f_keep, d_gain2, d_shift2, d_outb, d_fcb, d_projb = found
    end("df", f_keep, f_send, "deal", False)

    def heads_back(first, count, before):
        def run(qkv, mixed, dmixed, soft, h1_t, before):
            return attend_back(place, qkv, mixed, dmixed, soft, h1_t, first, count, before)

        return dict(work=run, given=(qkv, mixed, dmixed, soft, h1_t, before))

    dqkv, a_send, a_keep = steps.slot("df dp", **heads_back(0, half, None))
    end("da", a_keep, a_send, "turn", False)
    dqkv, b_send, b_keep = steps.slot("da df dp", **heads_back(half, half, dqkv))
    end("db", b_keep, b_send, "turn", False)
    sums = [(1, width), (1, width), (1, 2 * width), (72, 128)]
    tokens_grad, d_gain1, d_shift1, d_qv, packed = steps.slot(
        "all",
        **rows_work(
            "back_first",
            back_first_body,
            [dqkv, x, dy1],
            [vec, d_outb, d_gain2, d_shift2, d_fcb, d_projb],
            [w_a, w_b],
            [((length, width), bf16)],
            sums,
        ),
    )
    small = (d_gain1, d_shift1, d_qv, d_outb, d_gain2, d_shift2, d_fcb, d_projb)
    if plain:
        steps.done["dv"] = collect_vectors_plain(place, small)
    else:
        steps.add("dv", collect_vectors_steps(place, packed.reshape(2, -1, 128)))
    (block_out,) = steps.slot(
        "all",
        **rows_work(
            "finish", finish_body, [y1, g_t], [vec], [w_proj], [((length, width), bf16)], []
        ),
    )
    rows = width // 2
    placed = {}
    makers = {
        "dp": (put_rows, [(hidden // 2, width)], "put_proj"),
        "df": (put_wide, [(rows, hidden), (rows, width)], "put_fc"),
    }
    while steps.asked:
        ready = [n for n in makers if n in steps.done and n not in placed and not plain]
        if ready:
            found = steps.done[ready[0]]
            run = lambda *v: put(place, [v], *makers[ready[0]])
            placed[ready[0]] = steps.slot("all", work=run, given=found)
        else:
            steps.slot("all")

    held = lambda v: jnp.where(place.holder, v.astype(f32), 0.0)
    if plain:
        s_proj = held(steps.done["dp"])
        found = steps.done["df"].reshape(-1, hidden // width + 1, width // 8, width)
        fc = [found[:, i].reshape(-1, width) for i in range(hidden // width)]
        s_fc = held(jnp.concatenate(fc, axis=1))
        s_out = held(found[:, -1].reshape(-1, width))
        both = [
            v[:, (3 * p + j) * 128 : (3 * p + j + 1) * 128]
            for j in range(3)
            for v in (steps.done["da"], steps.done["db"])
            for p in range(half)
        ]
        s_qkv = held(jnp.concatenate(both, axis=1))
    else:
        for name in makers:
            if name not in placed:
                placed[name] = put(place, [steps.done[name]], *makers[name])
        (s_proj,), (s_fc, s_out) = placed["dp"], placed["df"]
        parts = [steps.done["da"], steps.done["db"]]
        (s_qkv,) = put(place, parts, put_pairs, [(rows, 3 * width)], "put_qkv")
    s_proj, s_fc, s_out, s_qkv = s_proj[None], s_fc[None], s_out[None], s_qkv[None]
    small = unpack_vectors(steps.done["dv"], [v.shape[1] // narrow for v in small])
    small = [held(v) for v in small]
    s_gain1, s_shift1, s_qv, s_outb, s_gain2, s_shift2, s_fcb, s_projb = small
    return (
        block_out[None],
        tokens_grad[None],
        s_gain1,
        s_shift1,
        s_qkv,
        s_qv,
        s_out,
        s_outb,
        s_gain2,
        s_shift2,
        s_fc,
        s_fcb,
        s_proj,
        s_projb,
    )


def solution(mesh):
    rows = P(AXES, None, None)
    flat, deep = P("wide", "narrow"), P("wide", "narrow", None)
    in_specs = (
        rows,
        P(AXES, None),
        rows,
        P(),
        flat,
        flat,
        deep,
        flat,
        deep,
        flat,
        flat,
        flat,
        deep,
        flat,
        deep,
        flat,
    )
    out_specs = (
        rows,
        rows,
        flat,
        flat,
        deep,
        flat,
        deep,
        flat,
        flat,
        flat,
        deep,
        flat,
        deep,
        flat,
    )
    body = functools.partial(on_device, mesh.shape["wide"], mesh.shape["narrow"])
    return jax.shard_map(
        body, mesh=mesh, in_specs=in_specs, out_specs=out_specs, check_vma=False
    )
```

```python
import functools
import math

import jax
import jax.numpy as jnp
from jax import lax
from jax.experimental import pallas as pl
from jax.experimental.pallas import tpu as pltpu
from jax.sharding import PartitionSpec as P

H = 12
HD = 64
QB = 256
REACH = 512

epsilon = 1e-05
AXES = ("wide", "narrow")
VMEM = 56 * 1024 * 1024
TINY = pl.CostEstimate(flops=1000, bytes_accessed=1000, transcendentals=0)
f32 = jnp.float32
bf16 = jnp.bfloat16


def spans(length):
    out = []
    for b in range(length // QB):
        low = max(0, (b * QB - (REACH - 1)) // QB * QB)
        out.append((low, (b + 1) * QB))
    return out


def soft_rows(length):
    return sum(hi - lo for lo, hi in spans(length))


def attend_pair(doc, q, k, v, o_ref, p_ref):
    length = q.shape[0]
    lane = lax.broadcasted_iota(jnp.int32, (length, 128), 1)
    low = lane < HD
    hot = (lane & (HD - 1)) == doc
    q_side = jnp.where(hot, 1.0, 0.0)
    k_side = jnp.where(hot, 0.0, -1e9)
    q = q.astype(f32) * HD ** (-0.5)
    k = k.astype(f32)
    v_t = v.T
    sides = []
    for h in range(2):
        mine = low if h == 0 else jnp.logical_not(low)
        sides.append(
            (jnp.where(mine, q, q_side).astype(bf16), jnp.where(mine, k, k_side).astype(bf16))
        )
    rows = lax.broadcasted_iota(jnp.int32, (QB, QB), 0)
    tri = rows <= lax.broadcasted_iota(jnp.int32, (QB, QB), 1)
    at = 0
    for b, (lo, hi) in enumerate(spans(length)):
        n = hi - lo
        outs = []
        for h in range(2):
            qa, ka = sides[h]
            s = dot(ka[lo:hi], qa[b * QB : (b + 1) * QB], ((1,), (1,)))
            last = jnp.where(tri, s[n - QB :], -1e9)
            s = last if n == QB else jnp.concatenate([s[: n - QB], last], axis=0)
            e = jnp.exp(s - jnp.max(s, axis=0, keepdims=True))
            p = (e * (1.0 / jnp.sum(e, axis=0, keepdims=True))).astype(bf16)
            p_ref[h, at : at + n, :] = p
            outs.append(dot(v_t[h * HD : (h + 1) * HD, lo:hi], p))
        o_ref[b * QB : (b + 1) * QB, :] = jnp.concatenate(outs, axis=0).T.astype(bf16)
        at += n


def attend(place, doc, x, vec, weights, column, first, count, before):
    length, width = x.shape
    start = before is None
    packed = vec is None
    rows = soft_rows(length)
    n_p, n_v = len(weights.arrays), 0 if packed else 1
    n_a = 0 if start else 3

    def kernel(*refs):
        refs = list(refs)
        take = lambda n: [refs.pop(0) for _ in range(n)]
        place_ref, doc_ref, x_ref = take(3)
        vec_refs, pieces = take(n_v), take(n_p)
        take(n_a)
        mixed_ref, soft_ref, qkv_ref = take(3)
        if start:
            h1_ref, h1_t_ref, vec_out = take(3)
        w, sem = take(2)
        step = pl.program_id(0)

        @pl.when(step == 0)
        def _():
            weights.load(place_ref, pieces, w, sem)
            if start:
                if packed:
                    vec_out[...] = unpack_rows(w)
                else:
                    vec_out[...] = vec_refs[0][...]
                for at in range(0, length, 256):
                    here = slice(at, at + 256)
                    h1 = norm_rows(
                        x_ref[here, :].astype(f32), row_of(vec_out, GAIN1), row_of(vec_out, SHIFT1)
                    ).astype(bf16)
                    h1_ref[here, :] = h1
                    h1_t_ref[:, here] = h1.T

        h1 = (h1_ref if start else x_ref)[...]
        known = vec_out if start else vec_refs[0]
        cols = w[:, pl.ds(pl.multiple_of(column + step * 384, 128), 384)]
        bias = jnp.concatenate(
            [
                known[pl.ds(QV[0] + first + step, 1), :],
                jnp.zeros((1, 128), f32),
                known[pl.ds(QV[0] + 6 + first + step, 1), :],
            ],
            axis=1,
        )
        qkv = (dot(h1, cols) + bias).astype(bf16)
        qkv_ref[...] = qkv
        attend_pair(
            doc_ref[...], qkv[:, :128], qkv[:, 128:256], qkv[:, 256:], mixed_ref, soft_ref
        )

    full = lambda shape: pl.BlockSpec(shape, lambda i: (0,) * len(shape))
    anyplace = pl.BlockSpec(memory_space=pl.ANY)
    outs = [
        ((length, width), (length, 128), lambda i: (0, first + i), bf16),
        ((H, rows, QB), (2, rows, QB), lambda i: (first + i, 0, 0), bf16),
        ((length, 3 * width), (length, 384), lambda i: (0, first + i), bf16),
    ]
    if start:
        outs += [
            ((length, width), (length, width), lambda i: (0, 0), bf16),
            ((width, length), (width, length), lambda i: (0, 0), bf16),
            ((72, 128), (72, 128), lambda i: (0, 0), f32),
        ]
    given = [place.spot, doc, x] + ([] if packed else [vec]) + weights.arrays
    aliases = {}
    if not start:
        aliases = {len(given) + i: i for i in range(3)}
        given += before
    return pl.pallas_call(
        kernel,
        grid=(count,),
        in_specs=[pl.BlockSpec(memory_space=pltpu.SMEM), full((length, 1)), full(x.shape)]
        + [full((72, 128))] * n_v
        + [anyplace] * (n_p + n_a),
        out_specs=[pl.BlockSpec(block, index) for _, block, index, _ in outs],
        out_shape=[jax.ShapeDtypeStruct(shape, kind) for shape, _, _, kind in outs],
        scratch_shapes=[
            pltpu.VMEM((weights.rows, weights.width), bf16),
            pltpu.SemaphoreType.DMA((n_p,)),
        ],
        input_output_aliases=aliases,
        compiler_params=pltpu.CompilerParams(vmem_limit_bytes=VMEM),
        cost_estimate=TINY,
        name="attend",
    )(*given)


def lay_blocks(ref, place_ref, other, rows):
    out = []
    core = 1 - place_ref[0] if other else place_ref[0]
    for x in range(2):
        for y in range(2):
            at = pl.multiple_of((4 * x + 2 * core + y) * rows, 16)
            out.append(ref[pl.ds(at, rows), :])
    return jnp.concatenate(out, axis=0)


def attend_back_kernel(
    place_ref,
    q_ref,
    k_ref,
    v_ref,
    o_ref,
    do_ref,
    p_ref,
    h1_t_ref,
    *refs,
    length,
):
    out_ref, send_ref, keep_ref, dk_acc, dv_acc = refs[-5:]
    lane = lax.broadcasted_iota(jnp.int32, (length, 128), 1)
    low = lane < HD
    spot = lane & (HD - 1)
    q = q_ref[...].astype(f32) * HD ** (-0.5)
    do = do_ref[...].astype(f32)
    v = v_ref[...].astype(f32)
    product = do * o_ref[...].astype(f32)
    k_t = k_ref[...].T
    sides = []
    for h in range(2):
        mine = low if h == 0 else jnp.logical_not(low)
        center = jnp.sum(jnp.where(mine, product, 0.0), axis=1, keepdims=True)
        first = center.astype(bf16).astype(f32)
        second = (center - first).astype(bf16).astype(f32)
        third = center - first - second
        extra = jnp.where(
            spot == 0, -first, jnp.where(spot == 1, -second, jnp.where(spot == 2, -third, 0.0))
        )
        sides.append(
            (
                jnp.where(mine, do, extra).astype(bf16),
                jnp.where(mine, v, jnp.where(spot < 3, 1.0, 0.0)).astype(bf16),
                jnp.where(mine, do, 0.0).astype(bf16),
                jnp.where(mine, q, 0.0).astype(bf16),
            )
        )
    dk_acc[...] = jnp.zeros_like(dk_acc)
    dv_acc[...] = jnp.zeros_like(dv_acc)
    at = 0
    for b, (lo, hi) in enumerate(spans(length)):
        n = hi - lo
        here = slice(b * QB, (b + 1) * QB)
        dqs = []
        dk = dv = None
        for h in range(2):
            do_more, v_more, do_own, q_own = sides[h]
            p = p_ref[h, at : at + n, :]
            dp = dot(v_more[lo:hi], do_more[here], ((1,), (1,)))
            ds = (p.astype(f32) * dp).astype(bf16)
            dv_part = dot(p, do_own[here])
            dk_part = dot(ds, q_own[here])
            dv = dv_part if dv is None else dv + dv_part
            dk = dk_part if dk is None else dk + dk_part
            dqs.append(dot(k_t[h * HD : (h + 1) * HD, lo:hi], ds))
        dv_acc[lo:hi, :] += dv
        dk_acc[lo:hi, :] += dk
        out_ref[here, :128] = (jnp.concatenate(dqs, axis=0) * HD ** (-0.5)).T.astype(bf16)
        at += n
    out_ref[:, 128:256] = dk_acc[...].astype(bf16)
    out_ref[:, 256:] = dv_acc[...].astype(bf16)
    parts = out_ref[...]
    for other, ref in ((True, send_ref), (False, keep_ref)):
        rows = h1_t_ref.shape[0] // 8
        ref[...] = dot(lay_blocks(h1_t_ref, place_ref, other, rows), parts).astype(bf16)


def attend_back(place, qkv, mixed, grad_mixed, soft, h1_t, first, count, before):
    length, width = mixed.shape
    rows = soft_rows(length)
    col = lambda off: pl.BlockSpec((length, 128), lambda i: (0, 3 * (first + i) + off))
    pair = pl.BlockSpec((length, 128), lambda i: (0, first + i))
    terms = pl.BlockSpec((width // 2, 384), lambda i: (0, i))
    term = jax.ShapeDtypeStruct((width // 2, 384 * count), bf16)
    given = [place.spot, qkv, qkv, qkv, mixed, grad_mixed, soft, h1_t]
    aliases = {}
    if before is not None:
        aliases = {len(given): 0}
        given.append(before)
    return pl.pallas_call(
        functools.partial(attend_back_kernel, length=length),
        grid=(count,),
        in_specs=[
            pl.BlockSpec(memory_space=pltpu.SMEM),
            col(0),
            col(1),
            col(2),
            pair,
            pair,
            pl.BlockSpec((2, rows, QB), lambda i: (first + i, 0, 0)),
            pl.BlockSpec(h1_t.shape, lambda i: (0, 0)),
        ]
        + [pl.BlockSpec(memory_space=pl.ANY)] * len(aliases),
        out_specs=[pl.BlockSpec((length, 384), lambda i: (0, first + i)), terms, terms],
        out_shape=[jax.ShapeDtypeStruct(qkv.shape, bf16), term, term],
        scratch_shapes=[pltpu.VMEM((length, 128), f32)] * 2,
        input_output_aliases=aliases,
        compiler_params=pltpu.CompilerParams(vmem_limit_bytes=VMEM),
        cost_estimate=TINY,
        name="attend_back",
    )(*given)


def proj_terms(place, g_t, dout):
    hidden, length = g_t.shape
    width = dout.shape[1]
    rows = hidden // 4

    def kernel(place_ref, g_ref, dout_ref, send_ref, keep_ref):
        value = dot(g_ref[...], dout_ref[...]).astype(bf16)

        @pl.when(pl.program_id(0) < 2)
        def _():
            send_ref[...] = value

        @pl.when(pl.program_id(0) >= 2)
        def _():
            keep_ref[...] = value

    def block(i, place_ref):
        core = jnp.where(i < 2, 1 - place_ref[0], place_ref[0])
        return 2 * (i % 2) + core, 0

    out = jax.ShapeDtypeStruct((hidden // 2, width), bf16)
    return pl.pallas_call(
        kernel,
        grid_spec=pltpu.PrefetchScalarGridSpec(
            num_scalar_prefetch=1,
            grid=(4,),
            in_specs=[
                pl.BlockSpec((rows, length), block),
                pl.BlockSpec((length, width), lambda i, p: (0, 0)),
            ],
            out_specs=[
                pl.BlockSpec((rows, width), lambda i, p: (jnp.minimum(i, 1), 0)),
                pl.BlockSpec((rows, width), lambda i, p: (jnp.maximum(i - 2, 0), 0)),
            ],
        ),
        out_shape=[out, out],
        compiler_params=pltpu.CompilerParams(vmem_limit_bytes=VMEM),
        cost_estimate=TINY,
        name="proj_terms",
    )(place.spot, g_t, dout)


def back_middle(place, dout, slope, y1, mixed, h2_t, vec, w_out, w_fc, w_proj):
    length, width = dout.shape
    hidden = w_fc.width
    step_rows, part = 256, PART
    steps = length // step_rows
    f_steps, rows = hidden // width, width // 8
    weights = (w_out, w_fc, w_proj)
    counts = [len(w.arrays) for w in weights]

    def kernel(*refs):
        refs = list(refs)
        take = lambda n: [refs.pop(0) for _ in range(n)]
        place_ref, dout_ref, slope_ref, y1_ref, mixed_ref, h2_t, vec_ref = take(7)
        pieces = [take(n) for n in counts]
        dmixed_ref, dy1_ref, send_ref, keep_ref = take(4)
        gain_ref, shift_ref, outb_ref, fcb_ref, projb_ref = sums = take(5)
        wo, wf, wp = buffers = take(3)
        sems = take(3)
        du_all, mixed_t, db1_all = take(3)
        i = pl.program_id(0)

        @pl.when(i == 0)
        def _():
            for w, own, buffer, sem in zip(weights, pieces, buffers, sems):
                w.load(place_ref, own, buffer, sem)
            for ref in sums:
                ref[...] = jnp.zeros_like(ref)

        @pl.when(i < steps)
        def _():
            here = pl.ds(pl.multiple_of(i * step_rows, step_rows), step_rows)
            dout = dout_ref[...]
            mixed_t[:, here] = mixed_ref[...].T
            dh2 = jnp.zeros((step_rows, width), f32)
            for c in range(0, hidden, part):
                cols = slice(c, c + part)
                du = dot(dout, wp[cols, :], ((1,), (1,))) * slope_ref[:, cols].astype(f32)
                du = du.astype(bf16)
                du_all[here, cols] = du
                fcb_ref[:, cols] += jnp.sum(du.astype(f32), axis=0, keepdims=True)
                dh2 = dh2 + dot(du, wf[:, cols], ((1,), (1,)))
            back, gain, shift = norm_back(y1_ref[...], row_of(vec_ref, GAIN2), dh2)
            wide_dout = dout.astype(f32)
            dy1 = wide_dout + back
            db1 = dy1.astype(bf16)
            dy1_ref[...] = dy1
            db1_all[here, :] = db1
            dmixed_ref[...] = dot(db1, wo[...], ((1,), (1,))).astype(bf16)
            gain_ref[...] += gain
            shift_ref[...] += shift
            outb_ref[...] += jnp.sum(db1.astype(f32), axis=0, keepdims=True)
            projb_ref[...] += jnp.sum(wide_dout, axis=0, keepdims=True)

        j = i - steps

        @pl.when((j >= 0) & (j < f_steps))
        def _():
            cols = pl.ds(pl.multiple_of(j * width, 128), width)
            for other, ref in ((True, send_ref), (False, keep_ref)):
                value = dot(lay_blocks(h2_t, place_ref, other, rows), du_all[:, cols])
                ref[...] = value.astype(bf16).reshape(ref.shape)

        @pl.when(j == f_steps)
        def _():
            for other, ref in ((True, send_ref), (False, keep_ref)):
                value = dot(lay_blocks(mixed_t, place_ref, other, rows), db1_all[...])
                ref[...] = value.astype(bf16).reshape(ref.shape)

    full = lambda shape: pl.BlockSpec(shape, lambda i: (0,) * len(shape))
    slab = lambda n: pl.BlockSpec((step_rows, n), lambda i: (jnp.minimum(i, steps - 1), 0))
    terms = pl.BlockSpec(
        (4, rows, width), lambda i: (0, jnp.clip(i - steps, 0, f_steps), 0)
    )
    like = jax.ShapeDtypeStruct
    one = (1, width)
    sum_shapes = [one, one, one, (1, hidden), one]
    return pl.pallas_call(
        kernel,
        grid=(steps + f_steps + 1,),
        in_specs=[
            pl.BlockSpec(memory_space=pltpu.SMEM),
            slab(width),
            slab(hidden),
            slab(width),
            slab(width),
            full(h2_t.shape),
            full((72, 128)),
        ]
        + [pl.BlockSpec(memory_space=pl.ANY)] * sum(counts),
        out_specs=[slab(width), slab(width), terms, terms] + [full(v) for v in sum_shapes],
        out_shape=[
            like((length, width), bf16),
            like((length, width), f32),
            like((4, rows * (f_steps + 1), width), bf16),
            like((4, rows * (f_steps + 1), width), bf16),
        ]
        + [like(v, f32) for v in sum_shapes],
        scratch_shapes=[pltpu.VMEM((w.rows, w.width), bf16) for w in weights]
        + [pltpu.SemaphoreType.DMA((n,)) for n in counts]
        + [
            pltpu.VMEM((length, hidden), bf16),
            pltpu.VMEM((width, length), bf16),
            pltpu.VMEM((length, width), bf16),
        ],
        compiler_params=pltpu.CompilerParams(vmem_limit_bytes=VMEM),
        cost_estimate=TINY,
        name="back_middle",
    )(place.spot, dout, slope, y1, mixed, h2_t, vec, *[v for w in weights for v in w.arrays])


class Place:
    def __init__(self, owner, wide, narrow, plain):
        self.wide, self.narrow = wide, narrow
        self.deep = wide // 4
        mine = lax.axis_index("wide")
        self.core, self.y, self.z = mine & 1, (mine >> 1) & 1, mine >> 2
        self.o_core, self.o_y, self.o_z = owner & 1, (owner >> 1) & 1, owner >> 2
        self.x = lax.axis_index("narrow")
        self.holder = mine == owner
        spot = jnp.stack([self.core, self.x, self.y, self.holder]).astype(jnp.int32)
        self.spot = jnp.zeros_like(spot) if plain else spot

    def swap(self, value, flip):
        return lax.ppermute(value, "wide", [(i, i ^ flip) for i in range(self.wide)])

    def cross(self, value, flip):
        pairs = [(2 * i + j, 2 * (i ^ flip) + 1 - j) for i in range(self.wide) for j in range(2)]
        return lax.ppermute(value, AXES, pairs)

    def shift(self, value, pairs):
        places = [(4 * a + low, 4 * b + low) for a, b in pairs for low in range(4)]
        return lax.ppermute(value, "wide", places)

    def z_pairs(self):
        last = self.deep - 1
        return [((i, i + 1), (last - i, last - i - 1)) for i in range(self.deep // 2 - 1)]

    def deal(self, value, kind):
        if kind == "plane":
            groups = [
                [2 * (4 * z + 2 * y + core) + x for x in range(2) for y in range(2)]
                for z in range(self.deep)
                for core in range(2)
            ]
            return lax.all_to_all(
                value, AXES, 0, 0, axis_index_groups=groups, tiled=True
            )
        groups = [
            [4 * z + 2 * y + core for y in range(2) for z in range(self.deep)]
            for core in range(2)
        ]
        return lax.all_to_all(value, "wide", 0, 0, axis_index_groups=groups, tiled=True)

    def z_flips(self):
        step = self.deep // 2
        while step:
            yield step
            step //= 2


def pick(parts, index):
    return lax.dynamic_index_in_dim(parts, index, axis=0, keepdims=False)


def ordered(mine, other, index):
    first = index == 0
    return jnp.stack([jnp.where(first, mine, other), jnp.where(first, other, mine)])


def spread_plain(place, shard):
    now = jnp.where(place.core == place.o_core, shard, place.swap(shard, 1))
    now = jnp.where(place.y == place.o_y, now, place.swap(now, 2))
    for step in place.z_flips():
        other = place.swap(now, 4 * step)
        now = jnp.where((place.z & step) == (place.o_z & step), now, other)
    return lax.all_gather(now, "narrow", axis=0, tiled=True)


def spread_steps(place, shard):
    if isinstance(shard, tuple):
        keep, send = shard
    else:
        halves = shard.reshape(2, shard.shape[0] // 2, shard.shape[1])
        keep, send = pick(halves, place.core), pick(halves, 1 - place.core)
    rows, width = 2 * keep.shape[0], keep.shape[1]
    (other,) = yield [(send, 1)]
    now = jnp.where(place.core == place.o_core, keep, other)
    halves = now.reshape(2, rows // 4, width)
    (other,) = yield [(pick(halves, 1 - place.y), 2)]
    now = jnp.where(place.y == place.o_y, pick(halves, place.y), other)
    for step in place.z_flips():
        (other,) = yield [(now, 4 * step)]
        now = jnp.where((place.z & step) == (place.o_z & step), now, other)
    by_y, by_x = yield [(now, 2), (now, 0)]
    cut = rows // 8
    far_a, far_b = yield [(by_y[:cut], 0), (by_x[cut:], 2)]
    mine = [
        (now, (0, 0, 0), 0),
        (by_y, (0, 0, 1), 0),
        (by_x, (0, 1, 0), 0),
        (far_a, (0, 1, 1), 0),
        (far_b, (0, 1, 1), cut),
    ]
    theirs = yield [(piece, 1) for piece, _, _ in mine]
    return Pieces(
        mine + [(got, (1, x, y), row) for got, (_, (_, x, y), row) in zip(theirs, mine)]
    )


class Pieces:
    def __init__(self, found):
        self.arrays = [piece for piece, _, _ in found]
        self.spots = [(flips, row) for _, flips, row in found]
        self.block, self.width = self.arrays[0].shape
        self.rows = self.block if len(found) == 1 else 8 * self.block

    def over(self, arrays):
        return Pieces([(v, flips, row) for v, (flips, row) in zip(arrays, self.spots)])

    def load(self, place_ref, refs, buffer, sem):
        copies = []
        for ref, ((core, x, y), row) in zip(refs, self.spots):
            start = 0
            if len(refs) > 1:
                at = 4 * (place_ref[1] ^ x) + 2 * (place_ref[0] ^ core) + (place_ref[2] ^ y)
                start = pl.multiple_of(at * self.block + row, 16)
            target = buffer.at[pl.ds(start, ref.shape[0]), :]
            copies.append(pltpu.make_async_copy(ref, target, sem.at[len(copies)]))
        for copy in copies:
            copy.start()
        for copy in copies:
            copy.wait()


ROWS = 256
PART = 1024


def by_rows(name, body, place, blocks, wholes, weights, out_blocks, out_sums):
    length = blocks[0].shape[0]
    n_b, n_w, n_o, n_s = len(blocks), len(wholes), len(out_blocks), len(out_sums)
    counts = [len(w.arrays) for w in weights]

    def kernel(*refs):
        refs = list(refs)
        take = lambda n: [refs.pop(0) for _ in range(n)]
        (place_ref,) = take(1)
        block_refs, whole_refs = take(n_b), take(n_w)
        piece_refs = [take(n) for n in counts]
        out_refs, sum_refs = take(n_o), take(n_s)
        buffers, sems = take(len(weights)), take(len(weights))

        @pl.when(pl.program_id(0) == 0)
        def _():
            for w, pieces, buffer, sem in zip(weights, piece_refs, buffers, sems):
                w.load(place_ref, pieces, buffer, sem)
            for ref in sum_refs:
                ref[...] = jnp.zeros_like(ref)

        body(block_refs, whole_refs, buffers, out_refs, sum_refs)

    full = lambda shape: pl.BlockSpec(shape, lambda i: (0,) * len(shape))
    slab = lambda shape: (
        pl.BlockSpec((ROWS, shape[1]), lambda i: (i, 0))
        if shape[0] == length
        else pl.BlockSpec((shape[0], ROWS), lambda i: (0, i))
    )
    return pl.pallas_call(
        kernel,
        grid=(length // ROWS,),
        in_specs=[pl.BlockSpec(memory_space=pltpu.SMEM)]
        + [slab(v.shape) for v in blocks]
        + [full(v.shape) for v in wholes]
        + [pl.BlockSpec(memory_space=pl.ANY)] * sum(counts),
        out_specs=[slab(shape) for shape, _ in out_blocks] + [full(s) for s in out_sums],
        out_shape=[jax.ShapeDtypeStruct(shape, kind) for shape, kind in out_blocks]
        + [jax.ShapeDtypeStruct(shape, f32) for shape in out_sums],
        scratch_shapes=[pltpu.VMEM((w.rows, w.width), bf16) for w in weights]
        + [pltpu.SemaphoreType.DMA((n,)) for n in counts],
        compiler_params=pltpu.CompilerParams(vmem_limit_bytes=VMEM),
        cost_estimate=TINY,
        name=name,
    )(place.spot, *blocks, *wholes, *[v for w in weights for v in w.arrays])


def tie(groups):
    flat, tree = jax.tree.flatten(groups)
    return jax.tree.unflatten(tree, lax.optimization_barrier(flat))


class Steps:
    def __init__(self, place):
        self.place = place
        self.asked, self.flips, self.chains, self.done, self.going = {}, {}, {}, {}, {}

    def ask(self, name, pairs):
        self.asked[name] = [value for value, _ in pairs]
        self.flips[name] = [flip for _, flip in pairs]

    def add(self, name, chain):
        self.chains[name] = chain
        self.ask(name, next(chain))

    def exchange(self, value, flip):
        if isinstance(flip, tuple):
            return self.place.shift(value, flip)
        if isinstance(flip, str):
            return self.place.deal(value, flip)
        if flip <= 0:
            return self.place.cross(value, -flip)
        return self.place.swap(value, flip)

    def slot(self, names="", hold="", work=None, given=(), strict=False):
        names = list(self.asked) if names == "all" else names.replace(",", " ").split()
        hold = hold.split()
        assert not set(names) & set(self.going)
        asked = {name: self.asked[name] for name in names if name in self.asked}
        if strict:
            asked = tie(asked)
        for name, values in asked.items():
            self.going[name] = [
                self.exchange(value, flip) for value, flip in zip(values, self.flips[name])
            ]
        held = tie({"asked": asked, "given": given})
        result = work(*held["given"]) if work else ()
        ready = {name: got for name, got in self.going.items() if name not in hold}
        ready, result, self.asked = tie((ready, result, self.asked))
        for name, got in ready.items():
            del self.going[name], self.asked[name]
            try:
                self.ask(name, self.chains[name].send(got))
            except StopIteration as stop:
                self.done[name] = stop.value
        return result


def collect_plain(place, keep, send):
    width = keep.shape[-1]
    parts = [v.reshape(2, 1, 2, -1, width) for v in (keep, send)]
    terms = jnp.concatenate(parts, axis=1).reshape(-1, width)
    now = lax.psum_scatter(terms, "narrow", scatter_dimension=0, tiled=True)
    return lax.psum(now, "wide")


def add(*values):
    return functools.reduce(lambda a, b: a + b, [v.astype(f32) for v in values]).astype(bf16)


def collect_steps(place, keep, send, plane, line):
    width = keep.shape[-1]
    (other,) = yield [(send, 1)]
    if plane == "deal":
        (got,) = yield [(add(keep, other).reshape(-1, width), "plane")]
        now = add(*got.reshape(4, -1, width))
    else:
        terms = [v.reshape(2, 2, -1, width) for v in (keep, other)]
        at_x = lambda v, i: pick(v, place.x ^ i)
        at_y = lambda v, i: lax.dynamic_index_in_dim(v, place.y ^ i, axis=1, keepdims=False)
        if plane == "turn":
            (other,) = yield [(add(*[at_x(v, 1) for v in terms]), 0)]
            terms = [at_x(v, 0) for v in terms] + [other]
            part = lambda i: add(*[pick(v, place.y ^ i) for v in terms])
            (other,) = yield [(part(1), 2)]
            now = add(part(0), other)
        else:
            cut = terms[0].shape[2] // 2
            upper = [v[:, :, :cut] for v in terms]
            lower = [v[:, :, cut:] for v in terms]
            by_x, by_y = yield [
                (add(*[at_x(v, 1) for v in upper]), 0),
                (add(*[at_y(v, 1) for v in lower]), 2),
            ]
            upper = [at_x(v, 0) for v in upper] + [by_x]
            lower = [at_y(v, 0) for v in lower] + [by_y]
            top = lambda i: add(*[pick(v, place.y ^ i) for v in upper])
            low = lambda i: add(*[pick(v, place.x ^ i) for v in lower])
            by_y, by_x = yield [(top(1), 2), (low(1), 0)]
            now = jnp.concatenate([add(top(0), by_y), add(low(0), by_x)], axis=0)
    if line:
        inward = place.z_pairs()
        for pairs in inward:
            (other,) = yield [(now, pairs)]
            now = add(now, other)
        half = place.deep // 2
        (other,) = yield [(now, ((half - 1, half), (half, half - 1)))]
        now = add(now, other)
        for pairs in reversed(inward):
            (other,) = yield [(now, tuple((b, a) for a, b in pairs))]
            got = (place.z == pairs[0][0]) | (place.z == pairs[1][0])
            now = jnp.where(got, other, now)
    else:
        for step in reversed(list(place.z_flips())):
            (other,) = yield [(now, 4 * step)]
            now = add(now, other)
    (other,) = yield [(now, 2)]
    far, far_other = yield [(now, 1), (other, 1)]
    return [now, other, far, far_other]


def put_kernel(place_ref, *refs, counts, bodies):
    refs = list(refs)
    take = lambda n: [refs.pop(0) for _ in range(n)]
    pieces = [take(4) for _ in range(counts[0])]
    outs = take(counts[1])
    buffers, sem = take(counts[0]), refs[0]
    copies = []
    for group, buffer in zip(pieces, buffers):
        for i, ref in enumerate(group):
            rows = ref.shape[0]
            at = 2 * (place_ref[0] ^ (i // 2)) + (place_ref[2] ^ (i % 2))
            target = buffer.at[pl.ds(pl.multiple_of(at * rows, 16), rows), :]
            copies.append(pltpu.make_async_copy(ref, target, sem.at[len(copies)]))
    for copy in copies:
        copy.start()
    for copy in copies:
        copy.wait()
    holder = place_ref[3] == 1
    bodies(buffers, outs, lambda v: jnp.where(holder, v.astype(f32), 0.0))


def put(place, groups, bodies, shapes, name):
    flat = [v for group in groups for v in group]
    return pl.pallas_call(
        functools.partial(put_kernel, counts=(len(groups), len(shapes)), bodies=bodies),
        in_specs=[pl.BlockSpec(memory_space=pltpu.SMEM)]
        + [pl.BlockSpec(memory_space=pl.ANY)] * len(flat),
        out_specs=[pl.BlockSpec(memory_space=pltpu.VMEM)] * len(shapes),
        out_shape=[jax.ShapeDtypeStruct(v, f32) for v in shapes],
        scratch_shapes=[
            pltpu.VMEM((4 * group[0].shape[0], group[0].shape[1]), bf16) for group in groups
        ]
        + [pltpu.SemaphoreType.DMA((len(flat),))],
        compiler_params=pltpu.CompilerParams(vmem_limit_bytes=VMEM),
        cost_estimate=TINY,
        name=name,
    )(place.spot, *flat)


def put_rows(buffers, outs, mask):
    outs[0][...] = mask(buffers[0][...])


def put_wide(buffers, outs, mask):
    wide, narrow = outs
    rows = narrow.shape[0] // 4
    width = narrow.shape[1]
    blocks = wide.shape[1] // width
    for quarter in range(4):
        here = slice(quarter * rows, (quarter + 1) * rows)
        for i in range(blocks + 1):
            start = (quarter * (blocks + 1) + i) * rows
            value = mask(buffers[0][start : start + rows, :])
            if i < blocks:
                wide[here, i * width : (i + 1) * width] = value
            else:
                narrow[here, :] = value


def put_pairs(buffers, outs, mask):
    width = outs[0].shape[1] // 3
    for part, buffer in enumerate(buffers):
        pairs = buffer.shape[1] // 384
        for p in range(pairs):
            for j in range(3):
                at = j * width + (part * pairs + p) * 128
                source = (3 * p + j) * 128
                outs[0][:, at : at + 128] = mask(buffer[:, source : source + 128])


def unpack_vectors(now, sizes):
    now = now.reshape(1, -1)
    out, at = [], 0
    for size in sizes:
        out.append(now[:, at : at + size])
        at += size
    return out


def shares(vectors, narrow):
    out = []
    for i in range(narrow):
        for v in vectors:
            size = v.shape[1] // narrow
            out.append(v[:, i * size : (i + 1) * size])
    return jnp.concatenate(out, axis=1)


def collect_vectors_steps(place, now):
    (other,) = yield [(now, 1)]
    now = now + other
    (other,) = yield [(pick(now, 1 - place.x), 0)]
    now = pick(now, place.x) + other
    (other,) = yield [(now, 2)]
    now = now + other
    for step in place.z_flips():
        (other,) = yield [(now, 4 * step)]
        now = now + other
    return now


def collect_vectors_plain(place, vectors):
    now = shares(vectors, place.narrow).reshape(place.narrow, -1)
    now = lax.psum_scatter(now, "narrow", scatter_dimension=0, tiled=False)
    return lax.psum(now, "wide")


def norm_rows(values, gain, shift):
    center = values - jnp.mean(values, axis=-1, keepdims=True)
    spread_of = jnp.mean(center * center, axis=-1, keepdims=True)
    return center * lax.rsqrt(spread_of + epsilon) * gain + shift


def norm_back(values, gain, grad):
    center = values - jnp.mean(values, axis=-1, keepdims=True)
    inverse = lax.rsqrt(jnp.mean(center * center, axis=-1, keepdims=True) + epsilon)
    hat = center * inverse
    scaled = grad * gain
    inner = jnp.mean(scaled * hat, axis=-1, keepdims=True)
    back = inverse * (scaled - jnp.mean(scaled, axis=-1, keepdims=True) - hat * inner)
    return (
        back,
        jnp.sum(grad * hat, axis=0, keepdims=True),
        jnp.sum(grad, axis=0, keepdims=True),
    )


def gelu_both(u):
    c = math.sqrt(2.0 / math.pi)
    square = u * u
    half = 0.5 + 0.5 * jnp.tanh(u * (c + c * 0.044715 * square))
    g = u * half
    return g, half + g * (1.0 - half) * (2 * c + 6 * c * 0.044715 * square)


def dot(a, b, dims=((1,), (0,))):
    return lax.dot_general(a, b, (dims, ((), ())), preferred_element_type=f32)


GAIN1, SHIFT1, QV, OUTB = (0, 6), (6, 6), (12, 12), (24, 6)
GAIN2, SHIFT2, FCB, PROJB = (30, 6), (36, 6), (42, 24), (66, 6)


def row_of(vec, spot, first=0, count=None):
    start = spot[0] + first
    count = spot[1] if count is None else count
    return jnp.concatenate([vec[start + i : start + i + 1, :] for i in range(count)], axis=1)


def unpack_rows(w):
    shard = w.shape[0] // 2
    near = w[:64, w.shape[1] - 128 :].astype(f32)
    far = w[shard : shard + 64, w.shape[1] - 128 :].astype(f32)
    parts = []
    for start, count in (GAIN1, SHIFT1, QV, OUTB, GAIN2, SHIFT2, FCB, PROJB):
        rows = slice(start // 2, (start + count) // 2)
        parts += [near[rows], far[rows]]
    return jnp.concatenate(parts, axis=0)


def pack_kernel(core_ref, w_ref, *refs):
    vectors, outs, rows_ref = refs[:-5], refs[-5:-1], refs[-1]
    half, width = w_ref.shape[0] // 2, w_ref.shape[1] // 3
    rows_ref[...] = jnp.zeros_like(rows_ref)
    at = 0
    for ref in vectors:
        value = ref[...].astype(f32)
        for i in range(value.shape[1] // 128):
            rows_ref[at : at + 1, :] = value[:, i * 128 : (i + 1) * 128]
            at += 1
    pairs = width // 128
    for other in range(2):
        core = 1 - core_ref[0] if other else core_ref[0]
        w = w_ref[pl.ds(pl.multiple_of(core * half, 16), half), :]
        for part in range(2):
            ref = outs[2 * part + other]
            for p in range(pairs // 2):
                for j in range(3):
                    source = j * width + (part * (pairs // 2) + p) * 128
                    to = (3 * p + j) * 128
                    ref[:, to : to + 128] = w[:, source : source + 128]
            if part == 0:
                block = rows_ref[...].astype(bf16)
                ref[:, 3 * width // 2 :] = jnp.concatenate([block, block], axis=0)


def pack(place, w, vectors):
    rows, width = w.shape
    side = width // 2
    shape = lambda more: jax.ShapeDtypeStruct((rows // 2, side + more), bf16)
    vmem = pl.BlockSpec(memory_space=pltpu.VMEM)
    near, near_send, far, far_send = pl.pallas_call(
        pack_kernel,
        in_specs=[pl.BlockSpec(memory_space=pltpu.SMEM)] + [vmem] * (1 + len(vectors)),
        out_specs=[vmem] * 4,
        out_shape=[shape(128), shape(128), shape(0), shape(0)],
        scratch_shapes=[pltpu.VMEM((rows // 4, 128), f32)],
        compiler_params=pltpu.CompilerParams(vmem_limit_bytes=VMEM),
        cost_estimate=TINY,
        name="pack",
    )(place.spot, w, *vectors)
    return (near, near_send), (far, far_send)


def widen_body(blocks, wholes, weights, outs, sums):
    (x_ref, mixed_ref), (vec,), (w_out, w_fc) = blocks, wholes, weights
    y1_ref, slope_ref, h2_t_ref, g_t_ref = outs
    y1 = x_ref[...].astype(f32) + dot(mixed_ref[...], w_out[...]) + row_of(vec, OUTB)
    y1_ref[...] = y1
    h2 = norm_rows(y1, row_of(vec, GAIN2), row_of(vec, SHIFT2)).astype(bf16)
    h2_t_ref[...] = h2.T
    for at in range(0, w_fc.shape[1], PART):
        here = slice(at, at + PART)
        g, slope = gelu_both(dot(h2, w_fc[:, here]) + row_of(vec, FCB, at // 128, PART // 128))
        g_t_ref[here, :] = g.astype(bf16).T
        slope_ref[:, here] = slope.astype(bf16)


def finish_body(blocks, wholes, weights, outs, sums):
    (y1_ref, g_t_ref), (vec,), (w,) = blocks, wholes, weights
    result = y1_ref[...] + dot(g_t_ref[...], w[...], ((0,), (0,))) + row_of(vec, PROJB)
    outs[0][...] = result.astype(bf16)


def back_first_body(blocks, wholes, weights, outs, sums):
    (dqkv_ref, x_ref, dy1_ref), (vec, *more), (w_a, w_b) = blocks, wholes, weights
    side = w_b.shape[1]
    dqkv = dqkv_ref[...]
    dh1 = dot(dqkv[:, :side], w_a[:, :side], ((1,), (1,)))
    dh1 = dh1 + dot(dqkv[:, side:], w_b[...], ((1,), (1,)))
    back, gain, shift = norm_back(x_ref[...].astype(f32), row_of(vec, GAIN1), dh1)
    outs[0][...] = (dy1_ref[...] + back).astype(bf16)
    total = jnp.sum(dqkv.astype(f32), axis=0, keepdims=True)
    parts = [total[:, p * 384 + j : p * 384 + j + 128] for j in (0, 256) for p in range(H // 2)]
    for ref, value in zip(sums, (gain, shift, jnp.concatenate(parts, axis=1))):
        ref[...] += value

    @pl.when(pl.program_id(0) == pl.num_programs(0) - 1)
    def _():
        found = sums[:3] + more
        at = 0
        for half in range(2):
            for ref in found:
                count = ref.shape[1] // 256
                for i in range(count):
                    start = (half * count + i) * 128
                    sums[3][at : at + 1, :] = ref[:, start : start + 128]
                    at += 1


def on_device(
    wide,
    narrow,
    tokens,
    doc_ids,
    cotangent,
    owner,
    ln1_gain,
    ln1_bias,
    qkv_weight,
    qv_bias,
    out_weight,
    out_bias,
    ln2_gain,
    ln2_bias,
    fc_weight,
    fc_bias,
    proj_weight,
    proj_bias,
):
    _, length, width = tokens.shape
    plain = narrow != 2 or ln1_gain.shape[1] % 128 != 0
    place = Place(owner[0], wide, narrow, plain)
    x = tokens[0]
    dout = cotangent[0]
    doc = doc_ids[0][:, None]
    pairs = H // 2
    half = pairs // 2

    def begin(name, shard):
        if plain:
            steps.done[name] = Pieces([(spread_plain(place, shard), (0, 0, 0), 0)])
        else:
            steps.add(name, spread_steps(place, shard))

    def end(name, keep, send, plane, line):
        if plain:
            steps.done[name] = collect_plain(place, keep, send)
        else:
            steps.add(name, collect_steps(place, keep, send, plane, line))

    steps = Steps(place)
    vectors = (ln1_gain, ln1_bias, qv_bias, out_bias, ln2_gain, ln2_bias, fc_bias, proj_bias)
    sizes = [v.shape[1] for v in vectors]
    vec = None
    if plain:
        rows = spread_plain(place, jnp.concatenate(vectors, axis=1))
        parts, at = [], 0
        for size in sizes:
            parts.append(rows[:, at : at + size].reshape(-1))
            at += size
        vec = jnp.concatenate(parts).reshape(-1, 128).astype(f32)
        order = [
            qkv_weight[0][:, j * width + p * 128 : j * width + (p + 1) * 128]
            for p in range(pairs)
            for j in range(3)
        ]
        near = jnp.concatenate(order[: 3 * half], axis=1)
        far = jnp.concatenate(order[3 * half :], axis=1)
    else:
        near, far = pack(place, qkv_weight[0], vectors)
    begin("qa", near)
    begin("qb", far)
    begin("o", out_weight[0])
    begin("f", fc_weight[0])
    begin("p", proj_weight[0])

    def attention(x, vec, name, column, first, count, before):
        weights = steps.done[name]

        def run(x, vec, arrays, before):
            return attend(place, doc, x, vec, weights.over(arrays), column, first, count, before)

        return dict(work=run, given=(x, vec, weights.arrays, before))

    def rows_work(name, body, blocks, wholes, weights, out_blocks, out_sums):
        def run(blocks, wholes, arrays):
            held = [w.over(own) for w, own in zip(weights, arrays)]
            return by_rows(name, body, place, blocks, wholes, held, out_blocks, out_sums)

        return dict(work=run, given=(blocks, wholes, [w.arrays for w in weights]))

    steps.slot("qa qb", strict=True)
    steps.slot("qa", strict=True)
    steps.slot("qa,qb,o,f,p", strict=True)
    steps.slot("qa qb o f", hold="qb f", strict=True)
    steps.slot("qa", hold="f", strict=True)
    steps.slot("qa qb o", strict=True)
    steps.slot("qa qb f p", hold="f p", strict=True)
    state = steps.slot("qb o", **attention(x, vec, "qa", 0, 0, 2, None))
    state, (h1, h1_t, vec) = list(state[:3]), state[3:]
    state = steps.slot(
        "qb o f p", hold="p", **attention(h1, vec, "qa", 768, 2, 1, state)
    )
    state = steps.slot("o f", hold="", **attention(h1, vec, "qb", 0, 3, 2, list(state)))
    state = steps.slot("f o p", **attention(h1, vec, "qb", 768, 5, 1, list(state)))
    mixed, soft, qkv = state
    steps.slot("f p", hold="p")
    w_a, w_b, w_out, w_fc = [steps.done[name] for name in ("qa", "qb", "o", "f")]
    hidden = w_fc.width
    y1, slope, h2_t, g_t = steps.slot(
        "",
        **rows_work(
            "widen",
            widen_body,
            [x, mixed],
            [vec],
            [w_out, w_fc],
            [
                ((length, width), f32),
                ((length, hidden), bf16),
                ((width, length), bf16),
                ((hidden, length), bf16),
            ],
            [],
        ),
    )
    p_send, p_keep = steps.slot(
        "p", work=lambda g_t, dout: proj_terms(place, g_t, dout), given=(g_t, dout)
    )
    end("dp", p_keep, p_send, "deal", False)
    steps.slot("p dp")
    w_proj = steps.done["p"]

    def run(dout, slope, y1, mixed, h2_t, vec, arrays):
        held = [w.over(own) for w, own in zip((w_out, w_fc, w_proj), arrays)]
        return back_middle(place, dout, slope, y1, mixed, h2_t, vec, *held)

    found = steps.slot(
        "dp",
        work=run,
        given=(dout, slope, y1, mixed, h2_t, vec, [w.arrays for w in (w_out, w_fc, w_proj)]),
    )
    dmixed, dy1, f_send, f_keep, d_gain2, d_shift2, d_outb, d_fcb, d_projb = found
    end("df", f_keep, f_send, "deal", True)

    def heads_back(first, count, before):
        def run(qkv, mixed, dmixed, soft, h1_t, before):
            return attend_back(place, qkv, mixed, dmixed, soft, h1_t, first, count, before)

        return dict(work=run, given=(qkv, mixed, dmixed, soft, h1_t, before))

    dqkv, a_send, a_keep = steps.slot("df dp", **heads_back(0, half, None))
    end("da", a_keep, a_send, "turn", False)
    heads = heads_back(half, half, dqkv)
    last = rows_work(
        "finish", finish_body, [y1, g_t], [vec], [w_proj], [((length, width), bf16)], []
    )
    (dqkv, b_send, b_keep), (block_out,) = steps.slot(
        "da df dp",
        work=lambda a, b: (heads["work"](*a), last["work"](*b)),
        given=(heads["given"], last["given"]),
    )
    end("db", b_keep, b_send, "turn", False)
    sums = [(1, width), (1, width), (1, 2 * width), (72, 128)]
    tokens_grad, d_gain1, d_shift1, d_qv, packed = steps.slot(
        "all",
        **rows_work(
            "back_first",
            back_first_body,
            [dqkv, x, dy1],
            [vec, d_outb, d_gain2, d_shift2, d_fcb, d_projb],
            [w_a, w_b],
            [((length, width), bf16)],
            sums,
        ),
    )
    small = (d_gain1, d_shift1, d_qv, d_outb, d_gain2, d_shift2, d_fcb, d_projb)
    if plain:
        steps.done["dv"] = collect_vectors_plain(place, small)
    else:
        steps.add("dv", collect_vectors_steps(place, packed.reshape(2, -1, 128)))
    rows = width // 2
    placed = {}
    makers = {
        "dp": (put_rows, [(hidden // 2, width)], "put_proj"),
        "df": (put_wide, [(rows, hidden), (rows, width)], "put_fc"),
    }
    while steps.asked:
        ready = [n for n in makers if n in steps.done and n not in placed and not plain]
        if ready:
            found = steps.done[ready[0]]
            run = lambda *v: put(place, [v], *makers[ready[0]])
            placed[ready[0]] = steps.slot("all", work=run, given=found)
        else:
            steps.slot("all")

    held = lambda v: jnp.where(place.holder, v.astype(f32), 0.0)
    if plain:
        s_proj = held(steps.done["dp"])
        found = steps.done["df"].reshape(-1, hidden // width + 1, width // 8, width)
        fc = [found[:, i].reshape(-1, width) for i in range(hidden // width)]
        s_fc = held(jnp.concatenate(fc, axis=1))
        s_out = held(found[:, -1].reshape(-1, width))
        both = [
            v[:, (3 * p + j) * 128 : (3 * p + j + 1) * 128]
            for j in range(3)
            for v in (steps.done["da"], steps.done["db"])
            for p in range(half)
        ]
        s_qkv = held(jnp.concatenate(both, axis=1))
    else:
        for name in makers:
            if name not in placed:
                placed[name] = put(place, [steps.done[name]], *makers[name])
        (s_proj,), (s_fc, s_out) = placed["dp"], placed["df"]
        parts = [steps.done["da"], steps.done["db"]]
        (s_qkv,) = put(place, parts, put_pairs, [(rows, 3 * width)], "put_qkv")
    s_proj, s_fc, s_out, s_qkv = s_proj[None], s_fc[None], s_out[None], s_qkv[None]
    small = unpack_vectors(steps.done["dv"], [v.shape[1] // narrow for v in small])
    small = [held(v) for v in small]
    s_gain1, s_shift1, s_qv, s_outb, s_gain2, s_shift2, s_fcb, s_projb = small
    return (
        block_out[None],
        tokens_grad[None],
        s_gain1,
        s_shift1,
        s_qkv,
        s_qv,
        s_out,
        s_outb,
        s_gain2,
        s_shift2,
        s_fc,
        s_fcb,
        s_proj,
        s_projb,
    )


def solution(mesh):
    rows = P(AXES, None, None)
    flat, deep = P("wide", "narrow"), P("wide", "narrow", None)
    in_specs = (
        rows,
        P(AXES, None),
        rows,
        P(),
        flat,
        flat,
        deep,
        flat,
        deep,
        flat,
        flat,
        flat,
        deep,
        flat,
        deep,
        flat,
    )
    out_specs = (
        rows,
        rows,
        flat,
        flat,
        deep,
        flat,
        deep,
        flat,
        flat,
        flat,
        deep,
        flat,
        deep,
        flat,
    )
    body = functools.partial(on_device, mesh.shape["wide"], mesh.shape["narrow"])
    return jax.shard_map(
        body, mesh=mesh, in_specs=in_specs, out_specs=out_specs, check_vma=False
    )
```
